256 devices in a mesh: gx: 16 (over x, y_lo, core), gy: 16 (over y_hi, z).
Axes of the slice: x: 4, y: 4 (y_hi: 2, y_lo: 2; y = y_hi * 2 + y_lo), z: 8, core: 2. Of those that a mesh axis runs over, the one named last changes fastest.
Arguments:
- particles: bfloat16 [64, 64, 16, 128], P('gx', 'gy'), may hold values from -6 to 6
- neighbours: int32 [64, 64, 16, 16], P('gx', 'gy'), may hold values from 0 to 143
- edge_valid: int32 [64, 64, 16, 16], P('gx', 'gy'), may hold values 0 or 1
- dropout_keep: int32 [2, 2, 64, 64, 16, 128], P(None, None, 'gx', 'gy'), may hold values 0 or 1
- weights: bfloat16 [2, 7, 128, 128], replicated, may hold values from -0.5 to 0.5
- biases: float32 [2, 3, 128], replicated, may hold values from -3 to 3
- cotangent: float32 [64, 64, 16, 128], P('gx', 'gy'), may hold values from -12 to 12
Outputs:
- particle_grad: float32 [64, 64, 16, 128], P('gx', 'gy')
- weight_grad: float32 [2, 7, 128, 128], replicated
- bias_grad: float32 [2, 3, 128], replicated
The draws below stay inside these ranges and needn't reach their ends.
All inputs are finite; a program needn't handle non-finite values. No bound on the sum of `edge_valid` or of `dropout_keep` on one device may be relied on, other than what follows from the above.
Results may differ from the reference program's by a relative error of at most 0.011.
Values may be sent and summed in bfloat16 or wider, within the bound.
A program may use at most 64 MiB of HBM per device.

```python
import jax
import jax.numpy as jnp
from jax import lax

H = 128
K = 16
LAYERS = 2
M = 16
NX = 64
NY = 64


def draw_cotangent(key, part):
    key = jax.random.fold_in(key, 11)
    along_x = jax.lax.broadcasted_iota(jnp.float32, (NX, NY, M, H), 0) / NX
    spread = jnp.clip(jax.random.normal(key, (NX, NY, M, H), jnp.float32), -4.0, 4.0)
    return spread * (1.0 + 2.0 * along_x)


def touch_ends(entries, stream_key, smallest, top_value):
    longest = entries.shape.index(max(entries.shape))
    spots = []
    for shift in (0, 1):
        where = [jax.random.randint(jax.random.fold_in(stream_key, axis), (), 0, length) for axis, length in enumerate(entries.shape)]
        where[longest] = (where[longest] + shift) % entries.shape[longest]
        spots.append(tuple(where))
    return entries.at[spots[0]].set(smallest).at[spots[1]].set(top_value)


def block_levels(stream_key, dims, split, smallest, high):
    gain, own = 1.0, jax.random.fold_in(stream_key, 6)
    for position, blocks in split:
        draws = jnp.exp(jax.random.uniform(jax.random.fold_in(own, position), (blocks,), jnp.float32, smallest / len(split), high / len(split)))
        gain = gain * jnp.repeat(draws, dims[position] // blocks).reshape([-1 if axis == position else 1 for axis in range(len(dims))])
    return gain


def scatter_about(rng, shape, scale, limit, cuts=(), kind=jnp.bfloat16):
    gain = block_levels(rng, shape, cuts, -0.22, 0.18) if cuts else 1.0
    result = jax.random.normal(rng, shape, jnp.float32) * scale * gain
    return jnp.minimum(jnp.maximum(result, -limit), limit).astype(kind)


def setup_inputs(seed: int = 0) -> dict:
    keys = jax.random.split(jax.random.key(seed), 8)
    return {
        "particles": scatter_about(keys[0], (NX, NY, M, H), 1.0, 6.0, ((0, 16), (1, 16))),
        "neighbours": touch_ends(jax.random.randint(keys[1], (NX, NY, M, K), 0, 9 * M), jax.random.fold_in(keys[1], 1), 0, (9 * M) - 1).astype(jnp.int32),
        "edge_valid": touch_ends((jax.random.randint(keys[2], (NX, NY, M, K), 0, 4) < 3).astype(jnp.int32), jax.random.fold_in(keys[2], 1), 0, 1),
        "dropout_keep": touch_ends((jax.random.randint(keys[3], (LAYERS, 2, NX, NY, M, H), 0, 10) < 9).astype(jnp.int32), jax.random.fold_in(keys[3], 1), 0, 1),
        "weights": scatter_about(keys[4], (LAYERS, 7, H, H), H ** -0.5, 0.5),
        "biases": scatter_about(keys[5], (LAYERS, 3, H), 0.5, 3.0, (), jnp.float32),
        "cotangent": draw_cotangent(jax.random.fold_in(keys[7], 71), 0),
    }


keep_scale = 10.0 / 9.0

def silu_grad(in_value):
    sigmoid_val = jax.nn.sigmoid(in_value)
    return sigmoid_val * (1.0 + in_value * (1.0 - sigmoid_val))

def back_dot(left_op, right_op):
    return lax.dot_general(left_op, right_op, (((0,), (0,)), ((), ())), preferred_element_type=jnp.float32)

def side_dot(left_op, right_op):
    return lax.dot_general(left_op, right_op, (((1,), (1,)), ((), ())), preferred_element_type=jnp.float32)

def edge_forward(near_proj, far_table, row_index, valid_rows, mid_w, mid_b):
    node_count, feat_width = near_proj.shape
    slot_k = row_index.shape[1]
    fetched = jnp.take(far_table, row_index.reshape(-1), axis=0).reshape(node_count, slot_k, feat_width)
    pre_one = near_proj[:, None, :] + fetched.astype(jnp.float32)
    edge_first = jax.nn.silu(pre_one).astype(jnp.bfloat16).reshape(-1, feat_width)
    pre_two = jnp.dot(edge_first, mid_w, preferred_element_type=jnp.float32) + mid_b
    edge_second = jax.nn.silu(pre_two).astype(jnp.bfloat16).reshape(node_count, slot_k, feat_width)
    return jnp.einsum('qk,qkh->qh', valid_rows.astype(jnp.float32), edge_second.astype(jnp.float32))

def edge_backward(near_proj, far_table, row_index, valid_rows, mid_w, mid_b, d_pooled):
    node_count, feat_width = near_proj.shape
    slot_k = row_index.shape[1]
    fetched = jnp.take(far_table, row_index.reshape(-1), axis=0).reshape(node_count, slot_k, feat_width)
    pre_one = near_proj[:, None, :] + fetched.astype(jnp.float32)
    edge_first = jax.nn.silu(pre_one).astype(jnp.bfloat16).reshape(-1, feat_width)
    pre_two = jnp.dot(edge_first, mid_w, preferred_element_type=jnp.float32) + mid_b
    lifted = valid_rows.astype(jnp.float32)[:, :, None] * d_pooled.astype(jnp.float32)[:, None, :]
    d_two = lifted.reshape(-1, feat_width) * silu_grad(pre_two)
    d_two_b = d_two.astype(jnp.bfloat16)
    grad_mid_w = back_dot(edge_first, d_two_b)
    d_first = side_dot(d_two_b, mid_w).reshape(node_count, slot_k, feat_width)
    d_one = d_first * silu_grad(pre_one)
    return (lax.optimization_barrier(jnp.sum(d_one, axis=1)), d_one, grad_mid_w, lax.optimization_barrier(jnp.sum(d_two, axis=0)), lax.optimization_barrier(jnp.sum(d_one, axis=(0, 1))))

def slab_rows(slab_codes, slab_no):
    offset_code = slab_codes // M
    within_col = slab_codes % M
    column_y = lax.broadcasted_iota(jnp.int32, slab_codes.shape, 0)
    target_x = (slab_no + offset_code // 3 - 1) % NX
    target_y = (column_y + offset_code % 3 - 1) % NY
    return ((target_x * NY + target_y) * M + within_col).reshape(NY * M, K).astype(jnp.int32)

def edges_over_slabs(near_proj, far_table, neighbours, edge_valid, mid_w, mid_b):

    def one_slab(inputs):
        near_slab, code_slab, valid_slab, slab_no = inputs
        return edge_forward(near_slab, far_table, slab_rows(code_slab, slab_no), valid_slab.reshape(NY * M, K), mid_w, mid_b)
    slab_ids = jnp.arange(NX, dtype=jnp.int32)
    pooled = lax.map(one_slab, (near_proj.reshape(NX, NY * M, H), neighbours, edge_valid, slab_ids))
    return pooled.reshape(NX * NY * M, H)

def edges_back_slabs(near_proj, far_table, neighbours, edge_valid, mid_w, mid_b, d_pooled):

    def advance(carry, inputs):
        far_grad, mid_grad, midb_grad, edgeb_grad = carry
        near_slab, code_slab, valid_slab, pool_slab, slab_no = inputs
        row_slab = slab_rows(code_slab, slab_no)
        d_near, d_one, grad_mid_w, grad_mid_b, grad_edge_b = edge_backward(near_slab, far_table, row_slab, valid_slab.reshape(NY * M, K), mid_w, mid_b, pool_slab)
        far_grad = far_grad.at[row_slab.reshape(-1)].add(d_one.reshape(-1, H))
        return ((far_grad, mid_grad + grad_mid_w, midb_grad + grad_mid_b, edgeb_grad + grad_edge_b), d_near)
    start = (jnp.zeros((NX * NY * M, H), jnp.float32), jnp.zeros((H, H), jnp.float32), jnp.zeros((H,), jnp.float32), jnp.zeros((H,), jnp.float32))
    slab_ids = jnp.arange(NX, dtype=jnp.int32)
    inputs = (near_proj.reshape(NX, NY * M, H), neighbours, edge_valid, d_pooled.reshape(NX, NY * M, H), slab_ids)
    totals, d_near = lax.scan(advance, start, inputs)
    return (d_near.reshape(NX * NY * M, H), totals)

def reference(particles, neighbours, edge_valid, dropout_keep, weights, biases, cotangent):
    node_count = NX * NY * M
    state = particles.reshape(node_count, H)
    saved = []
    for layer_no in range(LAYERS):
        layer_w = weights[layer_no]
        layer_b = biases[layer_no]
        keep_msg = dropout_keep[layer_no, 0].reshape(node_count, H).astype(jnp.float32) * keep_scale
        keep_node = dropout_keep[layer_no, 1].reshape(node_count, H).astype(jnp.float32) * keep_scale
        near_proj = jnp.dot(state, layer_w[0], preferred_element_type=jnp.float32) + layer_b[0]
        far_table = jnp.dot(state, layer_w[1], preferred_element_type=jnp.float32).astype(jnp.bfloat16)
        pooled = edges_over_slabs(near_proj, far_table, neighbours, edge_valid, layer_w[4], layer_b[1]).astype(jnp.bfloat16)
        message = (jnp.dot(pooled, layer_w[5], preferred_element_type=jnp.float32) * keep_msg / K).astype(jnp.bfloat16)
        node_pre = jnp.dot(state, layer_w[2], preferred_element_type=jnp.float32) + jnp.dot(message, layer_w[3], preferred_element_type=jnp.float32) + layer_b[2]
        node_hidden = (jax.nn.silu(node_pre) * keep_node).astype(jnp.bfloat16)
        saved.append((state, near_proj, far_table, pooled, message, node_pre, node_hidden, keep_msg, keep_node))
        state = (state.astype(jnp.float32) + jnp.dot(node_hidden, layer_w[6], preferred_element_type=jnp.float32)).astype(jnp.bfloat16)
    upstream = cotangent.reshape(node_count, H).astype(jnp.float32)
    weight_parts = [None] * LAYERS
    bias_parts = [None] * LAYERS
    for layer_no in reversed(range(LAYERS)):
        layer_w = weights[layer_no]
        layer_b = biases[layer_no]
        state_in, near_proj, far_table, pooled, message, node_pre, node_hidden, keep_msg, keep_node = saved[layer_no]
        up_b = upstream.astype(jnp.bfloat16)
        grad_out_w = back_dot(node_hidden, up_b)
        d_pre = side_dot(up_b, layer_w[6]) * keep_node * silu_grad(node_pre)
        d_pre_b = d_pre.astype(jnp.bfloat16)
        grad_node_b = lax.optimization_barrier(jnp.sum(d_pre, axis=0))
        grad_self_w = back_dot(state_in, d_pre_b)
        grad_msg_w = back_dot(message, d_pre_b)
        d_msg = (side_dot(d_pre_b, layer_w[3]) * keep_msg / K).astype(jnp.bfloat16)
        grad_pool_w = back_dot(pooled, d_msg)
        d_pooled = side_dot(d_msg, layer_w[5]).astype(jnp.bfloat16)
        d_near, totals = edges_back_slabs(near_proj, far_table, neighbours, edge_valid, layer_w[4], layer_b[1], d_pooled)
        d_far, grad_mid_w, grad_mid_b, grad_edge_b = totals
        d_near_b = d_near.astype(jnp.bfloat16)
        d_far_b = d_far.astype(jnp.bfloat16)
        grad_near_w = back_dot(state_in, d_near_b)
        grad_far_w = back_dot(state_in, d_far_b)
        upstream = upstream + side_dot(d_pre_b, layer_w[2]) + side_dot(d_near_b, layer_w[0]) + side_dot(d_far_b, layer_w[1])
        weight_parts[layer_no] = jnp.stack([grad_near_w, grad_far_w, grad_self_w, grad_msg_w, grad_mid_w, grad_pool_w, grad_out_w])
        bias_parts[layer_no] = jnp.stack([grad_edge_b, grad_mid_b, grad_node_b])
    norm_scale = 1.0 / node_count ** 0.5
    return (upstream.reshape(NX, NY, M, H), jnp.stack(weight_parts) * norm_scale, jnp.stack(bias_parts) * norm_scale)
```

```python
import functools

import jax
import jax.experimental.pallas as pl
import jax.experimental.pallas.tpu as pltpu
import jax.numpy as jnp
from jax import lax
from jax.sharding import PartitionSpec as P

MESH = pl.DeviceIdType.MESH
BF16, F32 = jnp.bfloat16, jnp.float32
keep_scale = 10.0 / 9.0

Y_HI = 2
NEAR, FAR, SELF, MSG, MID, POOL, OUT = range(7)
EARLY = [(0, SELF), (0, MSG), (0, POOL), (0, OUT)] + [(1, m) for m in range(7)]
LATE = [(0, NEAR), (0, FAR), (0, MID)]
EARLY_TILES, LATE_TILES = 96, 32
BIAS_TILE = 24
ROUTES = [(1, 0), (-1, 0), (0, 1), (0, -1), (1, 1), (1, -1), (-1, 1), (-1, -1)]


def dot(a, b):
    return jnp.dot(a, b, preferred_element_type=F32)


def side_dot(a, b):
    return lax.dot_general(a, b, (((1,), (1,)), ((), ())), preferred_element_type=F32)


def back_dot(a, b):
    return lax.dot_general(a, b, (((0,), (0,)), ((), ())), preferred_element_type=F32)


def silu_parts(v):
    sig = 0.5 * jnp.tanh(0.5 * v) + 0.5
    value = v * sig
    return value, sig + value * (1.0 - sig)


def kernel(
    gx,
    gy,
    part_ref,
    code_ref,
    valid_ref,
    drop_ref,
    w_ref,
    b_ref,
    cot_ref,
    pgrad_ref,
    wgrad_ref,
    bgrad_ref,
    state_tab,
    far_tab,
    pick,
    place,
    group,
    valid_b,
    code_rows,
    near,
    g_one,
    g_two,
    first_t,
    pooled,
    message,
    hidden,
    g_node,
    d_pool,
    d_near,
    far_acc,
    far_send,
    far_recv,
    mid_acc,
    stage_e,
    rs_e,
    ar_e,
    ag_e,
    stage_l,
    rs_l,
    ar_l,
    ag_l,
    halo_send_sem,
    halo_recv_sem,
    back_send_sem,
    back_recv_sem,
    red_send_sem,
    red_recv_sem,
):
    me_x = lax.axis_index("gx")
    me_y = lax.axis_index("gy")
    depth = gy // Y_HI
    ring = gx * Y_HI
    me_z = lax.rem(me_y, depth)
    me_r = me_x * Y_HI + me_y // depth
    nodes = 256
    cells = 16

    barrier = pltpu.get_barrier_semaphore()

    def greet_ring(d, _):
        t = lax.rem(me_r + d, ring)
        pl.semaphore_signal(
            barrier,
            inc=1,
            device_id=(t // Y_HI, lax.rem(t, Y_HI) * depth + me_z),
            device_id_type=MESH,
        )
        return 0

    def greet_z(d, _):
        t = lax.rem(me_z + d, depth)
        pl.semaphore_signal(
            barrier, inc=1, device_id=(me_x, me_y - me_z + t), device_id_type=MESH
        )
        return 0

    def neighbour(dx, dy):
        return (lax.rem(me_x + dx + gx, gx), lax.rem(me_y + dy + gy, gy))

    for dx, dy in ROUTES:
        pl.semaphore_signal(barrier, inc=1, device_id=neighbour(dx, dy), device_id_type=MESH)
    lax.fori_loop(1, ring, greet_ring, 0)
    lax.fori_loop(1, depth, greet_z, 0)

    state_tab[0, 1:5, 1:5] = part_ref[...]

    spread = jnp.where(
        lax.broadcasted_iota(jnp.int32, (16, 256), 1) // 16
        == lax.broadcasted_iota(jnp.int32, (16, 256), 0),
        1.0,
        0.0,
    ).astype(BF16)
    own = jnp.where(
        lax.rem(lax.broadcasted_iota(jnp.int32, (nodes, 256), 0), 16)
        == lax.rem(lax.broadcasted_iota(jnp.int32, (nodes, 256), 1), 16),
        1.0,
        0.0,
    )
    gather_cell = jnp.where(
        lax.broadcasted_iota(jnp.int32, (cells, nodes), 1) // 16
        == lax.broadcasted_iota(jnp.int32, (cells, nodes), 0),
        1.0,
        0.0,
    ).astype(BF16)
    codes = code_ref[...].reshape(nodes, 16).astype(F32).astype(BF16)
    valid = valid_ref[...].reshape(nodes, 16).astype(F32).astype(BF16)
    code_rows[...] = dot(gather_cell, (dot(codes, spread) * own).astype(BF16))
    group[...] = (dot(valid, spread) * own).astype(BF16).reshape(cells, 16, 256)

    pl.semaphore_wait(barrier, ring - 1 + depth - 1 + len(ROUTES))

    def part(step, edge, width):
        return pl.ds(1, 4) if step == 0 else pl.ds(edge[0] if step > 0 else edge[1], width)

    def halo_copies(layer):
        copies = []
        for n, (dx, dy) in enumerate(ROUTES):
            tab = state_tab.at[layer]
            copies.append(
                pltpu.make_async_remote_copy(
                    src_ref=tab.at[part(dx, (4, 1), 1), part(dy, (4, 1), 1)],
                    dst_ref=tab.at[part(dx, (0, 5), 1), part(dy, (0, 5), 1)],
                    send_sem=halo_send_sem.at[layer, n],
                    recv_sem=halo_recv_sem.at[layer, n],
                    device_id=neighbour(dx, dy),
                    device_id_type=MESH,
                )
            )
        return copies

    def back_copies(layer):
        copies = []
        for n, (dx, dy) in enumerate(ROUTES):
            x = pl.ds(1, 4) if dx == 0 else (5 if dx > 0 else 0)
            y = pl.ds(1, 4) if dy == 0 else (5 if dy > 0 else 0)
            target = far_recv.at[layer, n]
            copies.append(
                pltpu.make_async_remote_copy(
                    src_ref=far_send.at[layer, x, y],
                    dst_ref=target.at[0] if dx and dy else target,
                    send_sem=back_send_sem.at[layer, n],
                    recv_sem=back_recv_sem.at[layer, n],
                    device_id=neighbour(dx, dy),
                    device_id_type=MESH,
                )
            )
        return copies

    halos = [halo_copies(layer) for layer in range(2)]
    backs = [back_copies(layer) for layer in range(2)]
    for copy in halos[0]:
        copy.start()

    slot_rows = lax.broadcasted_iota(jnp.int32, (144, 256), 0).astype(F32)
    slot_lanes = lax.broadcasted_iota(jnp.int32, (16, 256), 1).astype(F32)

    def prepare(c, _):
        row = code_rows[pl.ds(c, 1), :]
        place[c] = jnp.where(slot_rows == row, 1.0, 0.0).astype(BF16)
        code = code_ref[c].astype(F32)
        flag = valid_ref[c].astype(F32)
        for k in range(16):
            column = jnp.broadcast_to(code[:, k : k + 1], (16, 256))
            pick[c, k * 16 : (k + 1) * 16, :] = jnp.where(column == slot_lanes, 1.0, 0.0).astype(
                BF16
            )
            valid_b[c, k * 16 : (k + 1) * 16, :] = jnp.broadcast_to(
                flag[:, k : k + 1], (16, 128)
            ).astype(BF16)
        return 0

    lax.fori_loop(0, cells, prepare, 0)

    def matrix(layer, m):
        return w_ref[layer, m]

    def inner_state(layer):
        return state_tab[layer, 1:5, 1:5].reshape(nodes, 128)

    def forward(layer):
        state = inner_state(layer)
        near[...] = dot(state, matrix(layer, NEAR)) + b_ref[layer, 0:1, :]
        for copy in halos[layer]:
            copy.wait_recv()
        far = dot(state_tab[layer].reshape(576, 128), matrix(layer, FAR)).astype(BF16)
        far_tab[...] = far.reshape(6, 6, 16, 128)
        mid_w = matrix(layer, MID)
        mid_b = b_ref[layer, 1:2, :]

        def row(x, _):
            for y in range(4):
                c = x * 4 + y
                block = far_tab[pl.ds(x, 3), y : y + 3].reshape(144, 128)
                block = jnp.concatenate([block, jnp.zeros((112, 128), BF16)], axis=0)
                fetched = dot(pick[c], block)
                base = near[pl.ds(pl.multiple_of(c * 16, 16), 16), :]
                pre_one = (fetched.reshape(16, 16, 128) + base[None]).reshape(256, 128)
                value, slope = silu_parts(pre_one)
                first = value.astype(BF16)
                g_one[layer, c] = slope.astype(BF16)
                first_t[layer, c] = first.T
                pre_two = dot(first, mid_w) + mid_b
                value, slope = silu_parts(pre_two)
                g_two[layer, c] = (slope * valid_b[c].astype(F32)).astype(BF16)
                total = dot(group[c], value.astype(BF16))
                pooled[layer, pl.ds(pl.multiple_of(c * 16, 16), 16), :] = total.astype(BF16)
            return 0

        lax.fori_loop(0, 4, row, 0)
        keep_msg = drop_ref[2 * layer].astype(F32) * (keep_scale / 16)
        keep_node = drop_ref[2 * layer + 1].astype(F32) * keep_scale
        msg = (dot(pooled[layer], matrix(layer, POOL)) * keep_msg).astype(BF16)
        message[layer] = msg
        node_pre = (
            dot(state, matrix(layer, SELF)) + dot(msg, matrix(layer, MSG)) + b_ref[layer, 2:3, :]
        )
        value, slope = silu_parts(node_pre)
        node_hidden = (value * keep_node).astype(BF16)
        hidden[layer] = node_hidden
        g_node[layer] = slope * keep_node
        return state, node_hidden

    state, node_hidden = forward(0)
    after = (state.astype(F32) + dot(node_hidden, matrix(0, OUT))).astype(BF16)
    state_tab[1, 1:5, 1:5] = after.reshape(4, 4, 16, 128)
    for copy in halos[1]:
        copy.start()
    forward(1)

    def node_back(layer, up_b):
        d_pre = side_dot(up_b, matrix(layer, OUT)) * g_node[layer]
        d_pre_b = d_pre.astype(BF16)
        keep_msg = drop_ref[2 * layer].astype(F32) * (keep_scale / 16)
        d_msg = (side_dot(d_pre_b, matrix(layer, MSG)) * keep_msg).astype(BF16)
        d_pool[...] = side_dot(d_msg, matrix(layer, POOL)).astype(BF16)
        return d_pre_b, d_msg, jnp.sum(d_pre, axis=0, keepdims=True)

    def edges_back(layer):
        mid_w = matrix(layer, MID)
        far_acc[...] = jnp.zeros((6, 6, 16, 128), F32)
        mid_acc[...] = jnp.zeros((128, 128), F32)

        def row(x, mid_b_sum):
            for y in range(4):
                c = x * 4 + y
                rows = pl.ds(pl.multiple_of(c * 16, 16), 16)
                upper = d_pool[rows, :].astype(F32)
                d_two = g_two[layer, c].astype(F32).reshape(16, 16, 128) * upper[None]
                mid_b_sum = mid_b_sum + jnp.sum(d_two, axis=0)
                d_two_b = d_two.reshape(256, 128).astype(BF16)
                mid_acc[...] += dot(first_t[layer, c], d_two_b)
                d_one = side_dot(d_two_b, mid_w) * g_one[layer, c].astype(F32)
                d_near[rows, :] = jnp.sum(d_one.reshape(16, 16, 128), axis=0)
                spill = dot(place[c], d_one.astype(BF16))
                far_acc[pl.ds(x, 3), y : y + 3] += spill.reshape(3, 3, 16, 128)
            return mid_b_sum

        mid_b_sum = lax.fori_loop(0, 4, row, jnp.zeros((16, 128), F32))
        far_send[layer] = far_acc[...].astype(BF16)
        for copy in backs[layer]:
            copy.start()
        return jnp.sum(mid_b_sum, axis=0, keepdims=True)

    def finish_far(layer):
        for n, (dx, dy) in enumerate(ROUTES):
            backs[layer][n].wait_recv()
            x = pl.ds(1, 4) if dx == 0 else pl.ds(1 if dx > 0 else 4, 1)
            y = pl.ds(1, 4) if dy == 0 else pl.ds(1 if dy > 0 else 4, 1)
            block = far_recv[layer, n].astype(F32)
            if dx and dy:
                far_acc[x, y] += block[0:1][None]
            elif dx:
                far_acc[x, y] += block[None]
            else:
                far_acc[x, y] += block[:, None]
        return far_acc[1:5, 1:5].reshape(nodes, 128).astype(BF16)

    def put(stage, index, value):
        rows = stage.shape[1]
        flat = index * 128
        value = value.astype(BF16)
        done = 0
        while done < 128:
            p, offset = divmod(flat + done, rows)
            count = min(rows - offset, 128 - done)
            stage[p, offset : offset + count, :] = value[done : done + count]
            done += count

    def put_weight(layer, m, value):
        if (layer, m) in EARLY:
            put(stage_e, EARLY.index((layer, m)), value)
        else:
            put(stage_l, LATE.index((layer, m)), value)

    def edge_grads(layer):
        put_weight(layer, MID, mid_acc[...])
        near_b = d_near[...].astype(BF16)
        put_weight(layer, NEAR, back_dot(inner_state(layer), near_b))
        put_weight(
            layer,
            FAR,
            back_dot(state_tab[layer].reshape(576, 128), far_send[layer].reshape(576, 128)),
        )
        return near_b, jnp.sum(d_near[...], axis=0, keepdims=True)

    def node_grads(layer, up_b, d_pre_b, d_msg):
        put_weight(layer, OUT, back_dot(hidden[layer], up_b))
        put_weight(layer, SELF, back_dot(inner_state(layer), d_pre_b))
        put_weight(layer, MSG, back_dot(message[layer], d_pre_b))
        put_weight(layer, POOL, back_dot(pooled[layer], d_msg))

    def ring_device(t):
        return (t // Y_HI, lax.rem(t, Y_HI) * depth + me_z)

    def ring_send(source, target, n, fixed):
        def body(d, _):
            t = lax.rem(me_r + d, ring)
            pltpu.make_async_remote_copy(
                src_ref=source.at[me_r if fixed else t],
                dst_ref=target.at[me_r],
                send_sem=red_send_sem.at[n],
                recv_sem=red_recv_sem.at[n],
                device_id=ring_device(t),
                device_id_type=MESH,
            ).start()
            return 0

        lax.fori_loop(1, ring, body, 0)

    def z_send(buffer, n):
        def body(d, _):
            t = lax.rem(me_z + d, depth)
            pltpu.make_async_remote_copy(
                src_ref=buffer.at[me_z],
                dst_ref=buffer.at[me_z],
                send_sem=red_send_sem.at[n],
                recv_sem=red_recv_sem.at[n],
                device_id=(me_x, me_y - me_z + t),
                device_id_type=MESH,
            ).start()
            return 0

        lax.fori_loop(1, depth, body, 0)

    def wait_all(sem, buffer, count):
        view = buffer.at[pl.ds(0, count)]
        pltpu.make_async_copy(view, view, sem).wait()

    def fold(buffer, count):
        total = buffer[0].astype(F32)
        for n in range(1, count):
            total = total + buffer[n].astype(F32)
        return total

    late_per = LATE_TILES // ring

    def split_again(total, late):
        plain = total.astype(BF16)
        if not late:
            return plain
        tile = BIAS_TILE % late_per * 16
        both = total[tile : tile + 8] + total[tile + 8 : tile + 16]
        high = both.astype(BF16).astype(F32)
        pieces = [total[:tile], high, both - high, total[tile + 16 :]]
        fixed = jnp.concatenate([p for p in pieces if p.shape[0]], axis=0).astype(BF16)
        return jnp.where(me_r == BIAS_TILE // late_per, fixed, plain)

    def reduce_start(stage, rs, n):
        rs[me_r] = stage[me_r]
        ring_send(stage, rs, n, False)

    def reduce_across(rs, ar, n, late):
        wait_all(red_recv_sem.at[n], rs, ring - 1)
        ar[me_z] = split_again(fold(rs, ring), late)
        z_send(ar, n + 1)

    def reduce_share(ar, ag, n, late):
        wait_all(red_recv_sem.at[n + 1], ar, depth - 1)
        ag[me_r] = split_again(fold(ar, depth), late)
        ring_send(ag, ag, n + 2, True)

    upstream = cot_ref[...]
    up_b = upstream.astype(BF16)
    d_pre_b, d_msg, node_b1 = node_back(1, up_b)
    mid_b1 = edges_back(1)
    near_b, edge_b1 = edge_grads(1)
    node_grads(1, up_b, d_pre_b, d_msg)
    upstream = (
        upstream + side_dot(d_pre_b, matrix(1, SELF)) + side_dot(near_b, matrix(1, NEAR))
    )
    upstream = upstream + side_dot(finish_far(1), matrix(1, FAR))

    up_b = upstream.astype(BF16)
    d_pre_b, d_msg, node_b0 = node_back(0, up_b)
    node_grads(0, up_b, d_pre_b, d_msg)
    used = len(EARLY) * 128
    rows = stage_e.shape[1]
    while used < EARLY_TILES * 16:
        p, offset = divmod(used, rows)
        stage_e[p, offset:rows, :] = jnp.zeros((rows - offset, 128), BF16)
        used += rows - offset
    reduce_start(stage_e, rs_e, 0)
    mid_b0 = edges_back(0)
    near_b, edge_b0 = edge_grads(0)
    sums = jnp.concatenate(
        [edge_b0, mid_b0, node_b0, edge_b1, mid_b1, node_b1, jnp.zeros((2, 128), F32)], axis=0
    )
    high = sums.astype(BF16).astype(F32)
    rows = stage_l.shape[1]
    p, offset = divmod(BIAS_TILE * 16, rows)
    stage_l[p, offset : offset + 16, :] = jnp.concatenate([high, sums - high], axis=0).astype(BF16)
    used = (BIAS_TILE + 1) * 16
    while used < LATE_TILES * 16:
        p, offset = divmod(used, rows)
        stage_l[p, offset:rows, :] = jnp.zeros((rows - offset, 128), BF16)
        used += rows - offset
    reduce_start(stage_l, rs_l, 3)
    reduce_across(rs_e, ar_e, 0, False)
    upstream = (
        upstream + side_dot(d_pre_b, matrix(0, SELF)) + side_dot(near_b, matrix(0, NEAR))
    )
    pgrad_ref[...] = upstream + side_dot(finish_far(0), matrix(0, FAR))
    reduce_across(rs_l, ar_l, 3, True)
    reduce_share(ar_e, ag_e, 0, False)
    reduce_share(ar_l, ag_l, 3, True)

    def take(gathered, index):
        rows = gathered.shape[1]
        pieces = []
        done = 0
        while done < 128:
            p, offset = divmod(index * 128 + done, rows)
            count = min(rows - offset, 128 - done)
            pieces.append(gathered[p, offset : offset + count, :])
            done += count
        return jnp.concatenate(pieces, axis=0)

    wait_all(red_recv_sem.at[2], ag_e, ring - 1)
    for n, (layer, m) in enumerate(EARLY):
        wgrad_ref[layer, m] = take(ag_e, n)
    wait_all(red_recv_sem.at[5], ag_l, ring - 1)
    for n, (layer, m) in enumerate(LATE):
        wgrad_ref[layer, m] = take(ag_l, n)
    p, offset = divmod(BIAS_TILE * 16, ag_l.shape[1])
    pair = ag_l[p, offset : offset + 16, :].astype(F32)
    bgrad_ref[...] = pair[0:8] + pair[8:16]

    for layer in range(2):
        for copy in halos[layer] + backs[layer]:
            copy.wait_send()
    for n, buffer, count in (
        (0, rs_e, ring - 1),
        (1, ar_e, depth - 1),
        (2, ag_e, ring - 1),
        (3, rs_l, ring - 1),
        (4, ar_l, depth - 1),
        (5, ag_l, ring - 1),
    ):
        wait_all(red_send_sem.at[n], buffer, count)


def solution(mesh):
    gx, gy = mesh.shape["gx"], mesh.shape["gy"]
    ring, depth = gx * Y_HI, gy // Y_HI
    early, late = EARLY_TILES // ring * 16, LATE_TILES // ring * 16
    total_nodes = gx * gy * 256
    norm_scale = 1.0 / total_nodes**0.5

    def shards(particles, neighbours, edge_valid, dropout_keep, weights, biases, cotangent):
        vmem = pltpu.VMEM
        scratch = [
            vmem((2, 6, 6, 16, 128), BF16),
            vmem((6, 6, 16, 128), BF16),
            vmem((16, 256, 256), BF16),
            vmem((16, 144, 256), BF16),
            vmem((16, 16, 256), BF16),
            vmem((16, 256, 128), BF16),
            vmem((16, 256), F32),
            vmem((256, 128), F32),
            vmem((2, 16, 256, 128), BF16),
            vmem((2, 16, 256, 128), BF16),
            vmem((2, 16, 128, 256), BF16),
            vmem((2, 256, 128), BF16),
            vmem((2, 256, 128), BF16),
            vmem((2, 256, 128), BF16),
            vmem((2, 256, 128), F32),
            vmem((256, 128), BF16),
            vmem((256, 128), F32),
            vmem((6, 6, 16, 128), F32),
            vmem((2, 6, 6, 16, 128), BF16),
            vmem((2, 8, 4, 16, 128), BF16),
            vmem((128, 128), F32),
            vmem((ring, early, 128), BF16),
            vmem((ring, early, 128), BF16),
            vmem((depth, early, 128), BF16),
            vmem((ring, early, 128), BF16),
            vmem((ring, late, 128), BF16),
            vmem((ring, late, 128), BF16),
            vmem((depth, late, 128), BF16),
            vmem((ring, late, 128), BF16),
            pltpu.SemaphoreType.DMA((2, 8)),
            pltpu.SemaphoreType.DMA((2, 8)),
            pltpu.SemaphoreType.DMA((2, 8)),
            pltpu.SemaphoreType.DMA((2, 8)),
            pltpu.SemaphoreType.DMA((6,)),
            pltpu.SemaphoreType.DMA((6,)),
        ]
        whole = pl.BlockSpec(memory_space=pltpu.VMEM)
        pgrad, wgrad, bgrad = pl.pallas_call(
            functools.partial(kernel, gx, gy),
            out_shape=(
                jax.ShapeDtypeStruct((256, 128), F32),
                jax.ShapeDtypeStruct((2, 7, 128, 128), BF16),
                jax.ShapeDtypeStruct((8, 128), F32),
            ),
            in_specs=[whole] * 7,
            out_specs=(whole, whole, whole),
            scratch_shapes=scratch,
            compiler_params=pltpu.CompilerParams(
                collective_id=0, has_side_effects=True, vmem_limit_bytes=40 * 2**20
            ),
            name="evolver",
        )(
            particles,
            neighbours.reshape(16, 16, 16),
            edge_valid.reshape(16, 16, 16),
            dropout_keep.reshape(4, 256, 128),
            weights,
            biases,
            cotangent.reshape(256, 128),
        )
        return (
            pgrad.reshape(particles.shape),
            wgrad.astype(F32) * norm_scale,
            bgrad[:6].reshape(biases.shape) * norm_scale,
        )

    cells = P("gx", "gy", None, None)
    return jax.shard_map(
        shards,
        mesh=mesh,
        in_specs=(cells, cells, cells, P(None, None, "gx", "gy", None, None), P(), P(), cells),
        out_specs=(cells, P(), P()),
        check_vma=False,
    )
```

```python
import functools

import jax
import jax.experimental.pallas as pl
import jax.experimental.pallas.tpu as pltpu
import jax.numpy as jnp
from jax import lax
from jax.sharding import PartitionSpec as P

MESH = pl.DeviceIdType.MESH
BF16, F32 = jnp.bfloat16, jnp.float32
keep_scale = 10.0 / 9.0

Y_HI = 2
NEAR, FAR, SELF, MSG, MID, POOL, OUT = range(7)
EARLY = [(0, SELF), (0, MSG), (0, POOL), (0, OUT)] + [(1, m) for m in range(7)]
LATE = [(0, NEAR), (0, FAR), (0, MID)]
EARLY_TILES, LATE_TILES = 96, 32
BIAS_TILE = 24
ROUTES = [(1, 0), (-1, 0), (0, 1), (0, -1), (1, 1), (1, -1), (-1, 1), (-1, -1)]


def dot(a, b):
    return jnp.dot(a, b, preferred_element_type=F32)


def side_dot(a, b):
    return lax.dot_general(a, b, (((1,), (1,)), ((), ())), preferred_element_type=F32)


def back_dot(a, b):
    return lax.dot_general(a, b, (((0,), (0,)), ((), ())), preferred_element_type=F32)


def silu_parts(v):
    sig = 0.5 * jnp.tanh(0.5 * v) + 0.5
    value = v * sig
    return value, sig + value * (1.0 - sig)


def kernel(
    gx,
    gy,
    part_ref,
    code_ref,
    valid_ref,
    drop_ref,
    w_ref,
    b_ref,
    cot_ref,
    pgrad_ref,
    wgrad_ref,
    bgrad_ref,
    state_tab,
    far_tab,
    pick,
    place,
    group,
    valid_b,
    code_rows,
    near,
    g_one,
    g_two,
    first_t,
    pooled,
    message,
    hidden,
    g_node,
    d_pool,
    d_near,
    far_acc,
    far_send,
    far_recv,
    mid_acc,
    mid_pair,
    stage_e,
    rs_e,
    ar_e,
    ag_e,
    stage_l,
    rs_l,
    ar_l,
    ag_l,
    halo_send_sem,
    halo_recv_sem,
    back_send_sem,
    back_recv_sem,
    red_send_sem,
    red_recv_sem,
):
    me_x = lax.axis_index("gx")
    me_y = lax.axis_index("gy")
    depth = gy // Y_HI
    ring = gx * Y_HI
    me_z = lax.rem(me_y, depth)
    me_r = me_x * Y_HI + me_y // depth
    nodes = 256
    cells = 16

    barrier = pltpu.get_barrier_semaphore()

    def greet_ring(d, _):
        t = lax.rem(me_r + d, ring)
        pl.semaphore_signal(
            barrier,
            inc=1,
            device_id=(t // Y_HI, lax.rem(t, Y_HI) * depth + me_z),
            device_id_type=MESH,
        )
        return 0

    def greet_z(d, _):
        t = lax.rem(me_z + d, depth)
        pl.semaphore_signal(
            barrier, inc=1, device_id=(me_x, me_y - me_z + t), device_id_type=MESH
        )
        return 0

    def neighbour(dx, dy):
        return (lax.rem(me_x + dx + gx, gx), lax.rem(me_y + dy + gy, gy))

    for dx, dy in ROUTES:
        pl.semaphore_signal(barrier, inc=1, device_id=neighbour(dx, dy), device_id_type=MESH)
    lax.fori_loop(1, ring, greet_ring, 0)
    lax.fori_loop(1, depth, greet_z, 0)

    state_tab[0, 1:5, 1:5] = part_ref[...]

    spread = jnp.where(
        lax.broadcasted_iota(jnp.int32, (16, 256), 1) // 16
        == lax.broadcasted_iota(jnp.int32, (16, 256), 0),
        1.0,
        0.0,
    ).astype(BF16)
    own = jnp.where(
        lax.rem(lax.broadcasted_iota(jnp.int32, (nodes, 256), 0), 16)
        == lax.rem(lax.broadcasted_iota(jnp.int32, (nodes, 256), 1), 16),
        1.0,
        0.0,
    )
    gather_cell = jnp.where(
        lax.broadcasted_iota(jnp.int32, (cells, nodes), 1) // 16
        == lax.broadcasted_iota(jnp.int32, (cells, nodes), 0),
        1.0,
        0.0,
    ).astype(BF16)
    codes = code_ref[...].reshape(nodes, 16).astype(F32).astype(BF16)
    valid = valid_ref[...].reshape(nodes, 16).astype(F32).astype(BF16)
    code_rows[...] = dot(gather_cell, (dot(codes, spread) * own).astype(BF16))
    group[...] = (dot(valid, spread) * own).astype(BF16).reshape(cells, 16, 256)

    pl.semaphore_wait(barrier, ring - 1 + depth - 1 + len(ROUTES))

    def part(step, edge, width):
        return pl.ds(1, 4) if step == 0 else pl.ds(edge[0] if step > 0 else edge[1], width)

    def halo_copies(layer):
        copies = []
        for n, (dx, dy) in enumerate(ROUTES):
            tab = state_tab.at[layer]
            copies.append(
                pltpu.make_async_remote_copy(
                    src_ref=tab.at[part(dx, (4, 1), 1), part(dy, (4, 1), 1)],
                    dst_ref=tab.at[part(dx, (0, 5), 1), part(dy, (0, 5), 1)],
                    send_sem=halo_send_sem.at[layer, n],
                    recv_sem=halo_recv_sem.at[layer, n],
                    device_id=neighbour(dx, dy),
                    device_id_type=MESH,
                )
            )
        return copies

    def back_copies(layer):
        copies = []
        for n, (dx, dy) in enumerate(ROUTES):
            x = pl.ds(1, 4) if dx == 0 else (5 if dx > 0 else 0)
            y = pl.ds(1, 4) if dy == 0 else (5 if dy > 0 else 0)
            target = far_recv.at[layer, n]
            copies.append(
                pltpu.make_async_remote_copy(
                    src_ref=far_send.at[layer, x, y],
                    dst_ref=target.at[0] if dx and dy else target,
                    send_sem=back_send_sem.at[layer, n],
                    recv_sem=back_recv_sem.at[layer, n],
                    device_id=neighbour(dx, dy),
                    device_id_type=MESH,
                )
            )
        return copies

    halos = [halo_copies(layer) for layer in range(2)]
    backs = [back_copies(layer) for layer in range(2)]
    for copy in halos[0]:
        copy.start()

    slot_rows = lax.broadcasted_iota(jnp.int32, (144, 256), 0).astype(F32)
    slot_lanes = lax.broadcasted_iota(jnp.int32, (16, 256), 1).astype(F32)

    def prepare(c, _):
        row = code_rows[pl.ds(c, 1), :]
        place[c] = jnp.where(slot_rows == row, 1.0, 0.0).astype(BF16)
        code = code_ref[c].astype(F32)
        flag = valid_ref[c].astype(F32)
        for k in range(16):
            column = jnp.broadcast_to(code[:, k : k + 1], (16, 256))
            pick[c, k * 16 : (k + 1) * 16, :] = jnp.where(column == slot_lanes, 1.0, 0.0).astype(
                BF16
            )
            valid_b[c, k * 16 : (k + 1) * 16, :] = jnp.broadcast_to(
                flag[:, k : k + 1], (16, 128)
            ).astype(BF16)
        return 0

    lax.fori_loop(0, cells, prepare, 0)

    empty = jnp.zeros((128, 128), BF16)
    for layer in range(2):
        mid_w = w_ref[layer, MID]
        mid_pair[layer] = jnp.concatenate(
            [
                jnp.concatenate([mid_w, empty], axis=1),
                jnp.concatenate([empty, mid_w], axis=1),
            ],
            axis=0,
        )

    def matrix(layer, m):
        return w_ref[layer, m]

    def inner_state(layer):
        return state_tab[layer, 1:5, 1:5].reshape(nodes, 128)

    def forward(layer):
        state = inner_state(layer)
        near[...] = dot(state, matrix(layer, NEAR)) + b_ref[layer, 0:1, :]
        for copy in halos[layer]:
            copy.wait_recv()
        far = dot(state_tab[layer].reshape(576, 128), matrix(layer, FAR)).astype(BF16)
        far_tab[...] = far.reshape(6, 6, 16, 128)
        mid_b = b_ref[layer, 1:2, :]

        def row(x, _):
            cells_here = [x * 4 + y for y in range(4)]
            fetched = []
            for y, c in enumerate(cells_here):
                block = far_tab[pl.ds(x, 3), y : y + 3].reshape(144, 128)
                block = jnp.concatenate([block, jnp.zeros((112, 128), BF16)], axis=0)
                fetched.append(dot(pick[c], block))
            firsts = []
            for y, c in enumerate(cells_here):
                base = near[pl.ds(pl.multiple_of(c * 16, 16), 16), :]
                pre_one = (fetched[y].reshape(16, 16, 128) + base[None]).reshape(256, 128)
                value, slope = silu_parts(pre_one)
                first = value.astype(BF16)
                g_one[layer, c] = slope.astype(BF16)
                first_t[layer, c] = first.T
                firsts.append(jnp.concatenate([first[:128], first[128:]], axis=1))
            seconds = [dot(first, mid_pair[layer]) for first in firsts]
            for y, c in enumerate(cells_here):
                pre_two = jnp.concatenate([seconds[y][:, :128], seconds[y][:, 128:]], axis=0) + mid_b
                value, slope = silu_parts(pre_two)
                flags = valid_b[c].astype(F32)
                g_two[layer, c] = (slope * flags).astype(BF16)
                total = jnp.sum((value * flags).reshape(16, 16, 128), axis=0)
                pooled[layer, pl.ds(pl.multiple_of(c * 16, 16), 16), :] = total.astype(BF16)
            return 0

        lax.fori_loop(0, 4, row, 0)
        keep_msg = drop_ref[2 * layer].astype(F32) * (keep_scale / 16)
        keep_node = drop_ref[2 * layer + 1].astype(F32) * keep_scale
        msg = (dot(pooled[layer], matrix(layer, POOL)) * keep_msg).astype(BF16)
        message[layer] = msg
        node_pre = (
            dot(state, matrix(layer, SELF)) + dot(msg, matrix(layer, MSG)) + b_ref[layer, 2:3, :]
        )
        value, slope = silu_parts(node_pre)
        node_hidden = (value * keep_node).astype(BF16)
        hidden[layer] = node_hidden
        g_node[layer] = slope * keep_node
        return state, node_hidden

    state, node_hidden = forward(0)
    after = (state.astype(F32) + dot(node_hidden, matrix(0, OUT))).astype(BF16)
    state_tab[1, 1:5, 1:5] = after.reshape(4, 4, 16, 128)
    for copy in halos[1]:
        copy.start()
    forward(1)

    def node_back(layer, up_b):
        d_pre = side_dot(up_b, matrix(layer, OUT)) * g_node[layer]
        d_pre_b = d_pre.astype(BF16)
        keep_msg = drop_ref[2 * layer].astype(F32) * (keep_scale / 16)
        d_msg = (side_dot(d_pre_b, matrix(layer, MSG)) * keep_msg).astype(BF16)
        d_pool[...] = side_dot(d_msg, matrix(layer, POOL)).astype(BF16)
        return d_pre_b, d_msg, jnp.sum(d_pre, axis=0, keepdims=True)

    def edges_back(layer):
        far_acc[...] = jnp.zeros((6, 6, 16, 128), F32)
        mid_acc[...] = jnp.zeros((128, 128), F32)

        def row(x, mid_b_sum):
            cells_here = [x * 4 + y for y in range(4)]
            twos = []
            for c in cells_here:
                rows = pl.ds(pl.multiple_of(c * 16, 16), 16)
                upper = d_pool[rows, :].astype(F32)
                d_two = g_two[layer, c].astype(F32).reshape(16, 16, 128) * upper[None]
                mid_b_sum = mid_b_sum + jnp.sum(d_two, axis=0)
                twos.append(d_two.reshape(256, 128).astype(BF16))
            outs = [
                side_dot(jnp.concatenate([t[:128], t[128:]], axis=1), mid_pair[layer]) for t in twos
            ]
            ones = []
            for y, c in enumerate(cells_here):
                rows = pl.ds(pl.multiple_of(c * 16, 16), 16)
                d_first = jnp.concatenate([outs[y][:, :128], outs[y][:, 128:]], axis=0)
                d_one = d_first * g_one[layer, c].astype(F32)
                d_near[rows, :] = jnp.sum(d_one.reshape(16, 16, 128), axis=0)
                ones.append(d_one.astype(BF16))
            both = [
                dot(
                    jnp.concatenate([first_t[layer, c], place[c]], axis=0),
                    jnp.concatenate([twos[y], ones[y]], axis=1),
                )
                for y, c in enumerate(cells_here)
            ]
            mid_acc[...] += sum(b[:128, :128] for b in both)
            for y in range(4):
                far_acc[pl.ds(x, 3), y : y + 3] += both[y][128:, 128:].reshape(3, 3, 16, 128)
            return mid_b_sum

        mid_b_sum = lax.fori_loop(0, 4, row, jnp.zeros((16, 128), F32))
        far_send[layer] = far_acc[...].astype(BF16)
        for copy in backs[layer]:
            copy.start()
        return jnp.sum(mid_b_sum, axis=0, keepdims=True)

    def finish_far(layer):
        for n, (dx, dy) in enumerate(ROUTES):
            backs[layer][n].wait_recv()
            x = pl.ds(1, 4) if dx == 0 else pl.ds(1 if dx > 0 else 4, 1)
            y = pl.ds(1, 4) if dy == 0 else pl.ds(1 if dy > 0 else 4, 1)
            block = far_recv[layer, n].astype(F32)
            if dx and dy:
                far_acc[x, y] += block[0:1][None]
            elif dx:
                far_acc[x, y] += block[None]
            else:
                far_acc[x, y] += block[:, None]
        return far_acc[1:5, 1:5].reshape(nodes, 128).astype(BF16)

    def put(stage, index, value):
        rows = stage.shape[1]
        flat = index * 128
        value = value.astype(BF16)
        done = 0
        while done < 128:
            p, offset = divmod(flat + done, rows)
            count = min(rows - offset, 128 - done)
            stage[p, offset : offset + count, :] = value[done : done + count]
            done += count

    def put_weight(layer, m, value):
        if (layer, m) in EARLY:
            put(stage_e, EARLY.index((layer, m)), value)
        else:
            put(stage_l, LATE.index((layer, m)), value)

    def edge_grads(layer):
        put_weight(layer, MID, mid_acc[...])
        near_b = d_near[...].astype(BF16)
        put_weight(layer, NEAR, back_dot(inner_state(layer), near_b))
        put_weight(
            layer,
            FAR,
            back_dot(state_tab[layer].reshape(576, 128), far_send[layer].reshape(576, 128)),
        )
        return near_b, jnp.sum(d_near[...], axis=0, keepdims=True)

    def node_grads(layer, up_b, d_pre_b, d_msg):
        put_weight(layer, OUT, back_dot(hidden[layer], up_b))
        put_weight(layer, SELF, back_dot(inner_state(layer), d_pre_b))
        put_weight(layer, MSG, back_dot(message[layer], d_pre_b))
        put_weight(layer, POOL, back_dot(pooled[layer], d_msg))

    def ring_device(t):
        return (t // Y_HI, lax.rem(t, Y_HI) * depth + me_z)

    def ring_send(source, target, n, fixed):
        def body(d, _):
            t = lax.rem(me_r + d, ring)
            pltpu.make_async_remote_copy(
                src_ref=source.at[me_r if fixed else t],
                dst_ref=target.at[me_r],
                send_sem=red_send_sem.at[n],
                recv_sem=red_recv_sem.at[n],
                device_id=ring_device(t),
                device_id_type=MESH,
            ).start()
            return 0

        lax.fori_loop(1, ring, body, 0)

    def z_send(buffer, n):
        def body(d, _):
            t = lax.rem(me_z + d, depth)
            pltpu.make_async_remote_copy(
                src_ref=buffer.at[me_z],
                dst_ref=buffer.at[me_z],
                send_sem=red_send_sem.at[n],
                recv_sem=red_recv_sem.at[n],
                device_id=(me_x, me_y - me_z + t),
                device_id_type=MESH,
            ).start()
            return 0

        lax.fori_loop(1, depth, body, 0)

    def wait_all(sem, buffer, count):
        view = buffer.at[pl.ds(0, count)]
        pltpu.make_async_copy(view, view, sem).wait()

    def fold(buffer, count):
        total = buffer[0].astype(F32)
        for n in range(1, count):
            total = total + buffer[n].astype(F32)
        return total

    late_per = LATE_TILES // ring

    def split_again(total, late):
        plain = total.astype(BF16)
        if not late:
            return plain
        tile = BIAS_TILE % late_per * 16
        both = total[tile : tile + 8] + total[tile + 8 : tile + 16]
        high = both.astype(BF16).astype(F32)
        pieces = [total[:tile], high, both - high, total[tile + 16 :]]
        fixed = jnp.concatenate([p for p in pieces if p.shape[0]], axis=0).astype(BF16)
        return jnp.where(me_r == BIAS_TILE // late_per, fixed, plain)

    def reduce_start(stage, rs, n):
        rs[me_r] = stage[me_r]
        ring_send(stage, rs, n, False)

    def reduce_across(rs, ar, n, late):
        wait_all(red_recv_sem.at[n], rs, ring - 1)
        ar[me_z] = split_again(fold(rs, ring), late)
        z_send(ar, n + 1)

    def reduce_share(ar, ag, n, late):
        wait_all(red_recv_sem.at[n + 1], ar, depth - 1)
        ag[me_r] = split_again(fold(ar, depth), late)
        ring_send(ag, ag, n + 2, True)

    upstream = cot_ref[...]
    up_b = upstream.astype(BF16)
    d_pre_b, d_msg, node_b1 = node_back(1, up_b)
    mid_b1 = edges_back(1)
    near_b, edge_b1 = edge_grads(1)
    node_grads(1, up_b, d_pre_b, d_msg)
    upstream = (
        upstream + side_dot(d_pre_b, matrix(1, SELF)) + side_dot(near_b, matrix(1, NEAR))
    )
    upstream = upstream + side_dot(finish_far(1), matrix(1, FAR))

    up_b = upstream.astype(BF16)
    d_pre_b, d_msg, node_b0 = node_back(0, up_b)
    node_grads(0, up_b, d_pre_b, d_msg)
    used = len(EARLY) * 128
    rows = stage_e.shape[1]
    while used < EARLY_TILES * 16:
        p, offset = divmod(used, rows)
        stage_e[p, offset:rows, :] = jnp.zeros((rows - offset, 128), BF16)
        used += rows - offset
    reduce_start(stage_e, rs_e, 0)
    mid_b0 = edges_back(0)
    near_b, edge_b0 = edge_grads(0)
    sums = jnp.concatenate(
        [edge_b0, mid_b0, node_b0, edge_b1, mid_b1, node_b1, jnp.zeros((2, 128), F32)], axis=0
    )
    high = sums.astype(BF16).astype(F32)
    rows = stage_l.shape[1]
    p, offset = divmod(BIAS_TILE * 16, rows)
    stage_l[p, offset : offset + 16, :] = jnp.concatenate([high, sums - high], axis=0).astype(BF16)
    used = (BIAS_TILE + 1) * 16
    while used < LATE_TILES * 16:
        p, offset = divmod(used, rows)
        stage_l[p, offset:rows, :] = jnp.zeros((rows - offset, 128), BF16)
        used += rows - offset
    reduce_start(stage_l, rs_l, 3)
    reduce_across(rs_e, ar_e, 0, False)
    upstream = (
        upstream + side_dot(d_pre_b, matrix(0, SELF)) + side_dot(near_b, matrix(0, NEAR))
    )
    pgrad_ref[...] = upstream + side_dot(finish_far(0), matrix(0, FAR))
    reduce_across(rs_l, ar_l, 3, True)
    reduce_share(ar_e, ag_e, 0, False)
    reduce_share(ar_l, ag_l, 3, True)

    def take(gathered, index):
        rows = gathered.shape[1]
        pieces = []
        done = 0
        while done < 128:
            p, offset = divmod(index * 128 + done, rows)
            count = min(rows - offset, 128 - done)
            pieces.append(gathered[p, offset : offset + count, :])
            done += count
        return jnp.concatenate(pieces, axis=0)

    wait_all(red_recv_sem.at[2], ag_e, ring - 1)
    for n, (layer, m) in enumerate(EARLY):
        wgrad_ref[layer, m] = take(ag_e, n)
    wait_all(red_recv_sem.at[5], ag_l, ring - 1)
    for n, (layer, m) in enumerate(LATE):
        wgrad_ref[layer, m] = take(ag_l, n)
    p, offset = divmod(BIAS_TILE * 16, ag_l.shape[1])
    pair = ag_l[p, offset : offset + 16, :].astype(F32)
    bgrad_ref[...] = pair[0:8] + pair[8:16]

    for layer in range(2):
        for copy in halos[layer] + backs[layer]:
            copy.wait_send()
    for n, buffer, count in (
        (0, rs_e, ring - 1),
        (1, ar_e, depth - 1),
        (2, ag_e, ring - 1),
        (3, rs_l, ring - 1),
        (4, ar_l, depth - 1),
        (5, ag_l, ring - 1),
    ):
        wait_all(red_send_sem.at[n], buffer, count)


def solution(mesh):
    gx, gy = mesh.shape["gx"], mesh.shape["gy"]
    ring, depth = gx * Y_HI, gy // Y_HI
    early, late = EARLY_TILES // ring * 16, LATE_TILES // ring * 16
    total_nodes = gx * gy * 256
    norm_scale = 1.0 / total_nodes**0.5

    def shards(particles, neighbours, edge_valid, dropout_keep, weights, biases, cotangent):
        vmem = pltpu.VMEM
        scratch = [
            vmem((2, 6, 6, 16, 128), BF16),
            vmem((6, 6, 16, 128), BF16),
            vmem((16, 256, 256), BF16),
            vmem((16, 144, 256), BF16),
            vmem((16, 16, 256), BF16),
            vmem((16, 256, 128), BF16),
            vmem((16, 256), F32),
            vmem((256, 128), F32),
            vmem((2, 16, 256, 128), BF16),
            vmem((2, 16, 256, 128), BF16),
            vmem((2, 16, 128, 256), BF16),
            vmem((2, 256, 128), BF16),
            vmem((2, 256, 128), BF16),
            vmem((2, 256, 128), BF16),
            vmem((2, 256, 128), F32),
            vmem((256, 128), BF16),
            vmem((256, 128), F32),
            vmem((6, 6, 16, 128), F32),
            vmem((2, 6, 6, 16, 128), BF16),
            vmem((2, 8, 4, 16, 128), BF16),
            vmem((128, 128), F32),
            vmem((2, 256, 256), BF16),
            vmem((ring, early, 128), BF16),
            vmem((ring, early, 128), BF16),
            vmem((depth, early, 128), BF16),
            vmem((ring, early, 128), BF16),
            vmem((ring, late, 128), BF16),
            vmem((ring, late, 128), BF16),
            vmem((depth, late, 128), BF16),
            vmem((ring, late, 128), BF16),
            pltpu.SemaphoreType.DMA((2, 8)),
            pltpu.SemaphoreType.DMA((2, 8)),
            pltpu.SemaphoreType.DMA((2, 8)),
            pltpu.SemaphoreType.DMA((2, 8)),
            pltpu.SemaphoreType.DMA((6,)),
            pltpu.SemaphoreType.DMA((6,)),
        ]
        whole = pl.BlockSpec(memory_space=pltpu.VMEM)
        pgrad, wgrad, bgrad = pl.pallas_call(
            functools.partial(kernel, gx, gy),
            out_shape=(
                jax.ShapeDtypeStruct((256, 128), F32),
                jax.ShapeDtypeStruct((2, 7, 128, 128), BF16),
                jax.ShapeDtypeStruct((8, 128), F32),
            ),
            in_specs=[whole] * 7,
            out_specs=(whole, whole, whole),
            scratch_shapes=scratch,
            compiler_params=pltpu.CompilerParams(
                collective_id=0, has_side_effects=True, vmem_limit_bytes=40 * 2**20
            ),
            name="evolver",
        )(
            particles,
            neighbours.reshape(16, 16, 16),
            edge_valid.reshape(16, 16, 16),
            dropout_keep.reshape(4, 256, 128),
            weights,
            biases,
            cotangent.reshape(256, 128),
        )
        return (
            pgrad.reshape(particles.shape),
            wgrad.astype(F32) * norm_scale,
            bgrad[:6].reshape(biases.shape) * norm_scale,
        )

    cells = P("gx", "gy", None, None)
    return jax.shard_map(
        shards,
        mesh=mesh,
        in_specs=(cells, cells, cells, P(None, None, "gx", "gy", None, None), P(), P(), cells),
        out_specs=(cells, P(), P()),
        check_vma=False,
    )
```

```python
import functools

import jax
import jax.experimental.pallas as pl
import jax.experimental.pallas.tpu as pltpu
import jax.numpy as jnp
from jax import lax
from jax.sharding import PartitionSpec as P

MESH = pl.DeviceIdType.MESH
BF16, F32 = jnp.bfloat16, jnp.float32
keep_scale = 10.0 / 9.0
VMEM_BYTES = 60 * 2**20

Y_HI = 2
NEAR, FAR, SELF, MSG, MID, POOL, OUT = range(7)
TOP = [(1, m) for m in range(7)]
NODE = [(0, OUT), (0, SELF), (0, MSG), (0, POOL)]
EDGE = [(0, NEAR), (0, FAR), (0, MID)]
GROUPS = [TOP, NODE, EDGE]
TILES = [64, 32, 32]
BIAS_TILE = 24
ROUTES = [(1, 0), (-1, 0), (0, 1), (0, -1), (1, 1), (1, -1), (-1, 1), (-1, -1)]
BORDER = [[0, 1, 2, 3], [12, 13, 14, 15], [4, 8, 7, 11]]
INSIDE = [[5, 6, 9, 10]]


def dot(a, b):
    return jnp.dot(a, b, preferred_element_type=F32)


def side_dot(a, b):
    return lax.dot_general(a, b, (((1,), (1,)), ((), ())), preferred_element_type=F32)


def back_dot(a, b):
    return lax.dot_general(a, b, (((0,), (0,)), ((), ())), preferred_element_type=F32)


def silu_parts(v):
    sig = 0.5 * jnp.tanh(0.5 * v) + 0.5
    value = v * sig
    return value, sig + value * (1.0 - sig)


def ones_where(mask):
    return jnp.where(mask, 1.0, 0.0)


def flat(fours):
    return [c for four in fours for c in four]


def rows_of(ref, cells):
    return jnp.concatenate([ref[c * 16 : (c + 1) * 16, :] for c in cells], axis=0)


def set_rows(ref, cells, value):
    for n, c in enumerate(cells):
        ref[c * 16 : (c + 1) * 16, :] = value[n * 16 : (n + 1) * 16]


def halves_side_by_side(a):
    return jnp.concatenate([a[:128], a[128:]], axis=1)


def halves_stacked(a):
    return jnp.concatenate([a[:, :128], a[:, 128:]], axis=0)


def kernel(
    gx,
    gy,
    norm_scale,
    part_hbm,
    code_hbm,
    valid_hbm,
    drop_hbm,
    w_hbm,
    b_hbm,
    cot_hbm,
    pgrad_hbm,
    wgrad_hbm,
    bgrad_hbm,
    pgrad_ref,
    wgrad_ref,
    bgrad_ref,
    code_ref,
    valid_ref,
    drop_ref,
    w_ref,
    b_ref,
    cot_ref,
    state_tab,
    far_tab,
    pick,
    place,
    valid_b,
    code_rows,
    near,
    g_one,
    g_two,
    first_t,
    pooled,
    message,
    hidden,
    g_node,
    up_b_ref,
    upstream,
    d_pre_ref,
    d_msg_ref,
    d_pool,
    d_near,
    far_acc,
    far_send,
    far_recv,
    mid_acc,
    mid_pair,
    *rest,
):
    groups = [rest[n * 6 : n * 6 + 6] for n in range(3)]
    (
        in_sem,
        out_sem,
        halo_send_sem,
        halo_recv_sem,
        back_send_sem,
        back_recv_sem,
        red_send_sem,
        red_recv_sem,
    ) = rest[18:]
    me_x = lax.axis_index("gx")
    me_y = lax.axis_index("gy")
    depth = gy // Y_HI
    plane = gx * Y_HI // 2
    me_z = lax.rem(me_y, depth)
    core = lax.rem(me_x, 2)
    me_p = (me_x // 4) * 4 + (me_y // depth) * 2 + lax.rem(me_x // 2, 2)

    def plane_device(p):
        return (
            (p // 4) * 4 + lax.rem(p, 2) * 2 + core,
            lax.rem(p // 2, 2) * depth + me_z,
        )

    def z_device(z):
        return (me_x, me_y - me_z + z)

    partner = (me_x + 1 - 2 * core, me_y)

    def neighbour(dx, dy):
        return (lax.rem(me_x + dx + gx, gx), lax.rem(me_y + dy + gy, gy))

    barrier = pltpu.get_barrier_semaphore()

    def greet(device):
        pl.semaphore_signal(barrier, inc=1, device_id=device, device_id_type=MESH)

    for dx, dy in ROUTES:
        greet(neighbour(dx, dy))

    def greet_plane(d, _):
        greet(plane_device(lax.rem(me_p + d, plane)))
        return 0

    def greet_z(d, _):
        greet(z_device(lax.rem(me_z + d, depth)))
        return 0

    lax.fori_loop(1, plane, greet_plane, 0)
    lax.fori_loop(1, depth, greet_z, 0)

    loads = [
        pltpu.make_async_copy(source, target, in_sem.at[n])
        for n, (source, target) in enumerate(
            [
                (part_hbm, state_tab.at[0, pl.ds(1, 4), pl.ds(1, 4)]),
                (code_hbm, code_ref),
                (valid_hbm, valid_ref),
                (w_hbm, w_ref),
                (b_hbm, b_ref),
                (drop_hbm, drop_ref),
                (cot_hbm, cot_ref),
            ]
        )
    ]
    for load in loads:
        load.start()

    def part(step, edge):
        return pl.ds(1, 4) if step == 0 else pl.ds(edge[0] if step > 0 else edge[1], 1)

    def halo_copies(layer):
        copies = []
        for n, (dx, dy) in enumerate(ROUTES):
            tab = state_tab.at[layer]
            copies.append(
                pltpu.make_async_remote_copy(
                    src_ref=tab.at[part(dx, (4, 1)), part(dy, (4, 1))],
                    dst_ref=tab.at[part(dx, (0, 5)), part(dy, (0, 5))],
                    send_sem=halo_send_sem.at[layer, n],
                    recv_sem=halo_recv_sem.at[layer, n],
                    device_id=neighbour(dx, dy),
                    device_id_type=MESH,
                )
            )
        return copies

    def back_copies(layer):
        copies = []
        for n, (dx, dy) in enumerate(ROUTES):
            x = pl.ds(1, 4) if dx == 0 else (5 if dx > 0 else 0)
            y = pl.ds(1, 4) if dy == 0 else (5 if dy > 0 else 0)
            target = far_recv.at[layer, n]
            copies.append(
                pltpu.make_async_remote_copy(
                    src_ref=far_send.at[layer, x, y],
                    dst_ref=target.at[0] if dx and dy else target,
                    send_sem=back_send_sem.at[layer, n],
                    recv_sem=back_recv_sem.at[layer, n],
                    device_id=neighbour(dx, dy),
                    device_id_type=MESH,
                )
            )
        return copies

    halos = [halo_copies(layer) for layer in range(2)]
    backs = [back_copies(layer) for layer in range(2)]

    spread = ones_where(
        lax.broadcasted_iota(jnp.int32, (16, 256), 1) // 16
        == lax.broadcasted_iota(jnp.int32, (16, 256), 0)
    ).astype(BF16)
    own = ones_where(
        lax.rem(lax.broadcasted_iota(jnp.int32, (256, 256), 0), 16)
        == lax.rem(lax.broadcasted_iota(jnp.int32, (256, 256), 1), 16)
    )
    gather_cell = ones_where(
        lax.broadcasted_iota(jnp.int32, (16, 256), 1) // 16
        == lax.broadcasted_iota(jnp.int32, (16, 256), 0)
    ).astype(BF16)
    loads[0].wait()
    loads[1].wait()
    loads[2].wait()
    codes = code_ref[...].reshape(256, 16).astype(F32).astype(BF16)
    code_rows[...] = dot(gather_cell, (dot(codes, spread) * own).astype(BF16))

    pl.semaphore_wait(barrier, plane - 1 + depth - 1 + len(ROUTES))
    for copy in halos[0]:
        copy.start()

    slot_rows = lax.broadcasted_iota(jnp.int32, (144, 256), 0).astype(F32)
    slot_lanes = lax.broadcasted_iota(jnp.int32, (16, 256), 1).astype(F32)

    def prepare(c, _):
        row = code_rows[pl.ds(c, 1), :]
        place[c] = ones_where(slot_rows == row).astype(BF16)
        code = code_ref[c].astype(F32)
        flag = valid_ref[c].astype(F32)
        for k in range(16):
            rows = slice(k * 16, (k + 1) * 16)
            column = jnp.broadcast_to(code[:, k : k + 1], (16, 256))
            pick[c, rows, :] = ones_where(column == slot_lanes).astype(BF16)
            valid_b[c, rows, :] = jnp.broadcast_to(flag[:, k : k + 1], (16, 128)).astype(BF16)
        return 0

    lax.fori_loop(0, 16, prepare, 0)
    for load in loads[3:]:
        load.wait()
    empty = jnp.zeros((128, 128), BF16)
    for layer in range(2):
        mid_w = w_ref[layer, MID]
        mid_pair[layer] = jnp.concatenate(
            [
                jnp.concatenate([mid_w, empty], axis=1),
                jnp.concatenate([empty, mid_w], axis=1),
            ],
            axis=0,
        )

    def matrix(layer, m):
        return w_ref[layer, m]

    def bias(layer, m):
        return b_ref[m, layer : layer + 1, :]

    def state_of(layer, cells):
        return jnp.concatenate(
            [state_tab[layer, c // 4 + 1, c % 4 + 1] for c in cells], axis=0
        )

    def inner_state(layer):
        return state_tab[layer, 1:5, 1:5].reshape(256, 128)

    def padded_state(layer):
        return state_tab[layer].reshape(576, 128)

    def kept(layer, which, cells, scale):
        return rows_of(drop_ref.at[2 * layer + which], cells).astype(F32) * scale

    def own_projections(layer):
        state = inner_state(layer)
        near[...] = dot(state, matrix(layer, NEAR)) + bias(layer, 0)
        far = dot(state, matrix(layer, FAR)).astype(BF16)
        far_tab[1:5, 1:5] = far.reshape(4, 4, 16, 128)

    def halo_projections(layer):
        for copy in halos[layer]:
            copy.wait_recv()
        pieces = [
            state_tab[layer, 0].reshape(96, 128),
            state_tab[layer, 5].reshape(96, 128),
            state_tab[layer, 1:5, 0].reshape(64, 128),
            state_tab[layer, 1:5, 5].reshape(64, 128),
        ]
        far = dot(jnp.concatenate(pieces, axis=0), matrix(layer, FAR)).astype(BF16)
        far_tab[0] = far[0:96].reshape(6, 16, 128)
        far_tab[5] = far[96:192].reshape(6, 16, 128)
        far_tab[1:5, 0] = far[192:256].reshape(4, 16, 128)
        far_tab[1:5, 5] = far[256:320].reshape(4, 16, 128)

    def edges_forward(layer, cells):
        fetched = []
        for c in cells:
            x, y = c // 4, c % 4
            block = far_tab[x : x + 3, y : y + 3].reshape(144, 128)
            block = jnp.concatenate([block, jnp.zeros((112, 128), BF16)], axis=0)
            fetched.append(dot(pick[c], block))
        firsts = []
        for n, c in enumerate(cells):
            base = near[c * 16 : (c + 1) * 16, :]
            pre_one = (fetched[n].reshape(16, 16, 128) + base[None]).reshape(256, 128)
            value, slope = silu_parts(pre_one)
            first = value.astype(BF16)
            g_one[layer, c] = slope.astype(BF16)
            first_t[layer, c] = first.T
            firsts.append(halves_side_by_side(first))
        seconds = [dot(first, mid_pair[layer]) for first in firsts]
        for n, c in enumerate(cells):
            value, slope = silu_parts(halves_stacked(seconds[n]) + bias(layer, 1))
            flags = valid_b[c].astype(F32)
            g_two[layer, c] = (slope * flags).astype(BF16)
            total = jnp.sum((value * flags).reshape(16, 16, 128), axis=0)
            pooled[layer, c * 16 : (c + 1) * 16, :] = total.astype(BF16)

    def nodes_forward(layer, cells):
        state = state_of(layer, cells)
        keep_msg = kept(layer, 0, cells, keep_scale / 16)
        keep_node = kept(layer, 1, cells, keep_scale)
        total = rows_of(pooled.at[layer], cells)
        msg = (dot(total, matrix(layer, POOL)) * keep_msg).astype(BF16)
        set_rows(message.at[layer], cells, msg)
        node_pre = dot(state, matrix(layer, SELF)) + dot(msg, matrix(layer, MSG)) + bias(layer, 2)
        value, slope = silu_parts(node_pre)
        node_hidden = (value * keep_node).astype(BF16)
        set_rows(hidden.at[layer], cells, node_hidden)
        set_rows(g_node.at[layer], cells, slope * keep_node)
        if layer == 0:
            after = (state.astype(F32) + dot(node_hidden, matrix(0, OUT))).astype(BF16)
            for n, c in enumerate(cells):
                state_tab[1, c // 4 + 1, c % 4 + 1] = after[n * 16 : (n + 1) * 16]

    own_projections(0)
    halo_projections(0)
    for four in BORDER:
        edges_forward(0, four)
    nodes_forward(0, flat(BORDER))
    for copy in halos[1]:
        copy.start()
    for four in INSIDE:
        edges_forward(0, four)
    nodes_forward(0, flat(INSIDE))
    own_projections(1)
    for four in INSIDE:
        edges_forward(1, four)
    nodes_forward(1, flat(INSIDE))
    halo_projections(1)
    for four in BORDER:
        edges_forward(1, four)
    nodes_forward(1, flat(BORDER))

    def node_back(layer, cells):
        up_b = rows_of(upstream, cells).astype(BF16)
        set_rows(up_b_ref, cells, up_b)
        d_pre = side_dot(up_b, matrix(layer, OUT)) * rows_of(g_node.at[layer], cells)
        d_pre_b = d_pre.astype(BF16)
        set_rows(d_pre_ref, cells, d_pre_b)
        keep_msg = kept(layer, 0, cells, keep_scale / 16)
        d_msg = (side_dot(d_pre_b, matrix(layer, MSG)) * keep_msg).astype(BF16)
        set_rows(d_msg_ref, cells, d_msg)
        set_rows(d_pool, cells, side_dot(d_msg, matrix(layer, POOL)).astype(BF16))
        return jnp.sum(d_pre, axis=0, keepdims=True)

    def edges_back(layer, cells, mid_b_sum):
        twos = []
        for c in cells:
            upper = d_pool[c * 16 : (c + 1) * 16, :].astype(F32)
            d_two = g_two[layer, c].astype(F32).reshape(16, 16, 128) * upper[None]
            mid_b_sum = mid_b_sum + jnp.sum(d_two, axis=0)
            twos.append(d_two.reshape(256, 128).astype(BF16))
        outs = [side_dot(halves_side_by_side(two), mid_pair[layer]) for two in twos]
        ones = []
        for n, c in enumerate(cells):
            d_one = halves_stacked(outs[n]) * g_one[layer, c].astype(F32)
            d_near[c * 16 : (c + 1) * 16, :] = jnp.sum(d_one.reshape(16, 16, 128), axis=0)
            ones.append(d_one.astype(BF16))
        both = [
            dot(
                jnp.concatenate([first_t[layer, c], place[c]], axis=0),
                jnp.concatenate([twos[n], ones[n]], axis=1),
            )
            for n, c in enumerate(cells)
        ]
        mid_acc[...] += sum(b[:128, :128] for b in both)
        for n, c in enumerate(cells):
            x, y = c // 4, c % 4
            far_acc[x : x + 3, y : y + 3] += both[n][128:, 128:].reshape(3, 3, 16, 128)
        return mid_b_sum

    def clear_sums():
        far_acc[...] = jnp.zeros((6, 6, 16, 128), F32)
        mid_acc[...] = jnp.zeros((128, 128), F32)

    def send_far(layer):
        far_send[layer, 0] = far_acc[0].astype(BF16)
        far_send[layer, 5] = far_acc[5].astype(BF16)
        far_send[layer, 1:5, 0] = far_acc[1:5, 0].astype(BF16)
        far_send[layer, 1:5, 5] = far_acc[1:5, 5].astype(BF16)
        for copy in backs[layer]:
            copy.start()

    def add_arrivals(layer):
        for n, (dx, dy) in enumerate(ROUTES):
            backs[layer][n].wait_recv()
            x = pl.ds(1, 4) if dx == 0 else pl.ds(1 if dx > 0 else 4, 1)
            y = pl.ds(1, 4) if dy == 0 else pl.ds(1 if dy > 0 else 4, 1)
            block = far_recv[layer, n].astype(F32)
            if dx and dy:
                far_acc[x, y] += block[0:1][None]
            elif dx:
                far_acc[x, y] += block[None]
            else:
                far_acc[x, y] += block[:, None]

    def far_rows(cells):
        return jnp.concatenate(
            [far_acc[c // 4 + 1, c % 4 + 1] for c in cells], axis=0
        ).astype(BF16)

    def new_upstream(layer, cells):
        return (
            rows_of(upstream, cells)
            + side_dot(rows_of(d_pre_ref, cells), matrix(layer, SELF))
            + side_dot(rows_of(d_near, cells).astype(BF16), matrix(layer, NEAR))
            + side_dot(far_rows(cells), matrix(layer, FAR))
        )

    def spans(n, index):
        rows = groups[n][0].shape[2]
        found = []
        done = 0
        while done < 128:
            chunk, offset = divmod(index * 128 + done, rows)
            count = min(rows - offset, 128 - done)
            found.append((done, count, chunk // plane, chunk % plane, offset))
            done += count
        return found

    def put(layer, m, value):
        value = value.astype(BF16)
        for n in range(3):
            if (layer, m) in GROUPS[n]:
                stage = groups[n][0]
                for done, count, half, p, offset in spans(n, GROUPS[n].index((layer, m))):
                    stage[half, p, offset : offset + count, :] = value[done : done + count]

    def take(n):
        gathered = groups[n][5]
        for index, (layer, m) in enumerate(GROUPS[n]):
            for done, count, half, p, offset in spans(n, index):
                piece = gathered[half, p, offset : offset + count, :]
                wgrad_ref[layer, m, done : done + count, :] = piece.astype(F32) * norm_scale

    def clear_rest(n, used):
        stage = groups[n][0]
        rows = stage.shape[2]
        while used < TILES[n] * 16:
            chunk, offset = divmod(used, rows)
            stage[chunk // plane, chunk % plane, offset:rows, :] = jnp.zeros(
                (rows - offset, 128), BF16
            )
            used += rows - offset

    def edge_grads(layer):
        put(layer, MID, mid_acc[...])
        near_b = d_near[...].astype(BF16)
        put(layer, NEAR, back_dot(inner_state(layer), near_b))
        far_b = far_acc[...].astype(BF16).reshape(576, 128)
        put(layer, FAR, back_dot(padded_state(layer), far_b))
        return jnp.sum(d_near[...], axis=0, keepdims=True)

    def node_grads(layer):
        put(layer, OUT, back_dot(hidden[layer], up_b_ref[...]))
        put(layer, SELF, back_dot(inner_state(layer), d_pre_ref[...]))
        put(layer, MSG, back_dot(message[layer], d_pre_ref[...]))
        put(layer, POOL, back_dot(pooled[layer], d_msg_ref[...]))

    bias_rows = TILES[2] // (2 * plane) * 16
    bias_chunk, bias_offset = divmod(BIAS_TILE * 16, bias_rows)
    bias_half, bias_p = divmod(bias_chunk, plane)
    bias_here = slice(bias_offset, bias_offset + 16)

    def split_again(tile):
        both = tile[0:8] + tile[8:16]
        high = both.astype(BF16).astype(F32)
        return jnp.concatenate([high, both - high], axis=0).astype(BF16)

    def remote(source, target, sem, device):
        return pltpu.make_async_remote_copy(
            src_ref=source,
            dst_ref=target,
            send_sem=red_send_sem.at[sem],
            recv_sem=red_recv_sem.at[sem],
            device_id=device,
            device_id_type=MESH,
        )

    def wait_all(sems, sem, buffer, count):
        view = buffer.at[pl.ds(0, count)]
        pltpu.make_async_copy(view, view, sems.at[sem]).wait()

    def fold(buffer, count):
        total = buffer[0].astype(F32)
        for n in range(1, count):
            total = total + buffer[n].astype(F32)
        return total

    def core_copy(n):
        return remote(groups[n][0].at[1 - core], groups[n][1], 5 * n, partner)

    def share_copy(n):
        return remote(groups[n][5].at[core], groups[n][5].at[core], 5 * n + 4, partner)

    def over_core(n):
        core_copy(n).start()

    def over_plane(n):
        stage, arrived, added, slots, across, gathered = groups[n]
        core_copy(n).wait_recv()
        total = stage[core].astype(F32) + arrived[...].astype(F32)
        added[...] = total.astype(BF16)
        if n == 2:
            tile = total[bias_p, bias_here]
            added[bias_p, bias_here] = jnp.where(
                core == bias_half, split_again(tile), tile.astype(BF16)
            )

        def body(d, _):
            p = lax.rem(me_p + d, plane)
            remote(added.at[p], slots.at[me_p], 5 * n + 1, plane_device(p)).start()
            return 0

        lax.fori_loop(1, plane, body, 0)
        slots[me_p] = added[me_p]

    def rounded(n, total):
        plain = total.astype(BF16)
        if n < 2:
            return plain
        mine = jnp.logical_and(core == bias_half, me_p == bias_p)
        pieces = [
            plain[:bias_offset],
            jnp.where(mine, split_again(total[bias_here]), plain[bias_here]),
            plain[bias_offset + 16 :],
        ]
        return jnp.concatenate([p for p in pieces if p.shape[0]], axis=0)

    def over_z(n):
        stage, arrived, added, slots, across, gathered = groups[n]
        wait_all(red_recv_sem, 5 * n + 1, slots, plane - 1)
        across[me_z] = rounded(n, fold(slots, plane))

        def body(d, _):
            z = lax.rem(me_z + d, depth)
            remote(across.at[me_z], across.at[me_z], 5 * n + 2, z_device(z)).start()
            return 0

        lax.fori_loop(1, depth, body, 0)

    def back_over_plane(n):
        stage, arrived, added, slots, across, gathered = groups[n]
        wait_all(red_recv_sem, 5 * n + 2, across, depth - 1)
        gathered[core, me_p] = rounded(n, fold(across, depth))

        def body(d, _):
            p = lax.rem(me_p + d, plane)
            here = gathered.at[core, me_p]
            remote(here, here, 5 * n + 3, plane_device(p)).start()
            return 0

        lax.fori_loop(1, plane, body, 0)

    def back_over_core(n):
        gathered = groups[n][5]
        wait_all(red_recv_sem, 5 * n + 3, gathered.at[core], plane - 1)
        share_copy(n).start()

    def arrived_whole(n):
        pltpu.make_async_copy(
            groups[n][5].at[1 - core], groups[n][5].at[1 - core], red_recv_sem.at[5 * n + 4]
        ).wait()

    runs = [(1, 0, 7), (0, SELF, 2), (0, POOL, 2), (0, NEAR, 2), (0, MID, 1)]
    outs = [
        pltpu.make_async_copy(
            wgrad_ref.at[layer, pl.ds(m, count)],
            wgrad_hbm.at[layer, pl.ds(m, count)],
            out_sem.at[n],
        )
        for n, (layer, m, count) in enumerate(runs)
    ]
    outs.append(pltpu.make_async_copy(pgrad_ref, pgrad_hbm, out_sem.at[5]))
    outs.append(pltpu.make_async_copy(bgrad_ref, bgrad_hbm, out_sem.at[6]))

    no_sum = jnp.zeros((16, 128), F32)

    upstream[...] = cot_ref[...]
    node_b1 = node_back(1, list(range(16)))
    clear_sums()
    mid_b1 = no_sum
    for four in BORDER:
        mid_b1 = edges_back(1, four, mid_b1)
    send_far(1)
    for four in INSIDE:
        mid_b1 = edges_back(1, four, mid_b1)
    edge_b1 = edge_grads(1)
    node_grads(1)
    clear_rest(0, len(TOP) * 128)
    over_core(0)

    set_rows(upstream, flat(INSIDE), new_upstream(1, flat(INSIDE)))
    node_b0 = node_back(0, flat(INSIDE))
    over_plane(0)
    add_arrivals(1)
    set_rows(upstream, flat(BORDER), new_upstream(1, flat(BORDER)))
    clear_sums()
    node_b0 = node_b0 + node_back(0, flat(BORDER))
    node_grads(0)
    over_core(1)
    mid_b0 = no_sum
    for four in BORDER:
        mid_b0 = edges_back(0, four, mid_b0)
    send_far(0)
    over_plane(1)
    over_z(0)
    for four in INSIDE:
        mid_b0 = edges_back(0, four, mid_b0)
    edge_b0 = edge_grads(0)
    column = [jnp.sum(v, axis=0, keepdims=True) for v in (mid_b0, mid_b1)]
    sums = jnp.concatenate(
        [edge_b0, edge_b1, column[0], column[1], node_b0, node_b1, jnp.zeros((2, 128), F32)],
        axis=0,
    )
    high = sums.astype(BF16).astype(F32)
    groups[2][0][bias_half, bias_p, bias_here, :] = jnp.concatenate(
        [high, sums - high], axis=0
    ).astype(BF16)
    clear_rest(2, (BIAS_TILE + 1) * 16)
    over_core(2)
    back_over_plane(0)
    over_plane(2)
    over_z(1)
    add_arrivals(0)
    pgrad_ref[...] = new_upstream(0, list(range(16)))
    outs[5].start()
    over_z(2)
    back_over_plane(1)
    back_over_core(0)
    back_over_plane(2)
    arrived_whole(0)
    take(0)
    outs[0].start()
    back_over_core(1)
    arrived_whole(1)
    take(1)
    outs[1].start()
    outs[2].start()
    back_over_core(2)
    arrived_whole(2)
    take(2)
    outs[3].start()
    outs[4].start()
    pair = groups[2][5][bias_half, bias_p, bias_here, :].astype(F32)
    bias_total = (pair[0:8] + pair[8:16]) * norm_scale
    for m in range(3):
        bgrad_ref[m] = bias_total[2 * m : 2 * m + 2]
    outs[6].start()

    for layer in range(2):
        for copy in halos[layer] + backs[layer]:
            copy.wait_send()
    for n in range(3):
        stage, arrived, added, slots, across, gathered = groups[n]
        core_copy(n).wait_send()
        wait_all(red_send_sem, 5 * n + 1, slots, plane - 1)
        wait_all(red_send_sem, 5 * n + 2, across, depth - 1)
        wait_all(red_send_sem, 5 * n + 3, gathered.at[core], plane - 1)
        share_copy(n).wait_send()
    for out in outs:
        out.wait()


def write_out(pgrad, wgrad, bgrad, pgrad_out, wgrad_out, bgrad_out, pbuf, wbuf, bbuf, in_sems, out_sems):
    routes = [(pgrad, pbuf, pgrad_out), (bgrad, bbuf, bgrad_out)]
    for layer in range(2):
        for m, count in ((0, 2), (2, 2), (4, 3)):
            part = (layer, pl.ds(m, count))
            routes.append((wgrad.at[part], wbuf.at[part], wgrad_out.at[part]))
    reads = [pltpu.make_async_copy(a, b, in_sems.at[n]) for n, (a, b, _) in enumerate(routes)]
    writes = [pltpu.make_async_copy(b, c, out_sems.at[n]) for n, (_, b, c) in enumerate(routes)]
    for read in reads:
        read.start()
    for read, write in zip(reads, writes):
        read.wait()
        write.start()
    for write in writes:
        write.wait()


def solution(mesh):
    gx, gy = mesh.shape["gx"], mesh.shape["gy"]
    plane, depth = gx * Y_HI // 2, gy // Y_HI
    norm_scale = 1.0 / (gx * gy * 256) ** 0.5
    vmem = pltpu.VMEM

    def group_buffers(tiles):
        rows = tiles // (2 * plane) * 16
        return [
            vmem((2, plane, rows, 128), BF16),
            vmem((plane, rows, 128), BF16),
            vmem((plane, rows, 128), BF16),
            vmem((plane, rows, 128), BF16),
            vmem((depth, rows, 128), BF16),
            vmem((2, plane, rows, 128), BF16),
        ]

    def shards(particles, neighbours, edge_valid, dropout_keep, weights, biases, cotangent):
        scratch = [
            vmem((256, 128), F32),
            vmem((2, 7, 128, 128), F32),
            vmem((3, 2, 128), F32),
            vmem((16, 16, 16), jnp.int32),
            vmem((16, 16, 16), jnp.int32),
            vmem((4, 256, 128), jnp.int32),
            vmem((2, 7, 128, 128), BF16),
            vmem((3, 2, 128), F32),
            vmem((256, 128), F32),
            vmem((2, 6, 6, 16, 128), BF16),
            vmem((6, 6, 16, 128), BF16),
            vmem((16, 256, 256), BF16),
            vmem((16, 144, 256), BF16),
            vmem((16, 256, 128), BF16),
            vmem((16, 256), F32),
            vmem((256, 128), F32),
            vmem((2, 16, 256, 128), BF16),
            vmem((2, 16, 256, 128), BF16),
            vmem((2, 16, 128, 256), BF16),
            vmem((2, 256, 128), BF16),
            vmem((2, 256, 128), BF16),
            vmem((2, 256, 128), BF16),
            vmem((2, 256, 128), F32),
            vmem((256, 128), BF16),
            vmem((256, 128), F32),
            vmem((256, 128), BF16),
            vmem((256, 128), BF16),
            vmem((256, 128), BF16),
            vmem((256, 128), F32),
            vmem((6, 6, 16, 128), F32),
            vmem((2, 6, 6, 16, 128), BF16),
            vmem((2, 8, 4, 16, 128), BF16),
            vmem((128, 128), F32),
            vmem((2, 256, 256), BF16),
        ]
        for tiles in TILES:
            scratch += group_buffers(tiles)
        scratch += [
            pltpu.SemaphoreType.DMA((7,)),
            pltpu.SemaphoreType.DMA((7,)),
            pltpu.SemaphoreType.DMA((2, 8)),
            pltpu.SemaphoreType.DMA((2, 8)),
            pltpu.SemaphoreType.DMA((2, 8)),
            pltpu.SemaphoreType.DMA((2, 8)),
            pltpu.SemaphoreType.DMA((15,)),
            pltpu.SemaphoreType.DMA((15,)),
        ]
        far_off = pl.BlockSpec(memory_space=pl.ANY)
        shapes = (
            jax.ShapeDtypeStruct((256, 128), F32),
            jax.ShapeDtypeStruct((2, 7, 128, 128), F32),
            jax.ShapeDtypeStruct((3, 2, 128), F32),
        )
        results = pl.pallas_call(
            functools.partial(kernel, gx, gy, norm_scale),
            out_shape=shapes,
            in_specs=[far_off] * 7,
            out_specs=(far_off, far_off, far_off),
            scratch_shapes=scratch,
            compiler_params=pltpu.CompilerParams(
                collective_id=0, has_side_effects=True, vmem_limit_bytes=VMEM_BYTES
            ),
            name="evolver",
        )(
            particles,
            neighbours.reshape(16, 16, 16),
            edge_valid.reshape(16, 16, 16),
            dropout_keep.reshape(4, 256, 128),
            weights,
            biases.transpose(1, 0, 2),
            cotangent.reshape(256, 128),
        )
        pgrad, wgrad, bgrad = pl.pallas_call(
            write_out,
            out_shape=shapes,
            in_specs=[far_off] * 3,
            out_specs=(far_off, far_off, far_off),
            scratch_shapes=[vmem(s.shape, s.dtype) for s in shapes]
            + [pltpu.SemaphoreType.DMA((8,)), pltpu.SemaphoreType.DMA((8,))],
            compiler_params=pltpu.CompilerParams(vmem_limit_bytes=VMEM_BYTES),
            name="write_out",
        )(*results)
        return (pgrad.reshape(particles.shape), wgrad, bgrad.transpose(1, 0, 2))

    cells = P("gx", "gy", None, None)
    return jax.shard_map(
        shards,
        mesh=mesh,
        in_specs=(cells, cells, cells, P(None, None, "gx", "gy", None, None), P(), P(), cells),
        out_specs=(cells, P(), P()),
        check_vma=False,
    )
```

```python
import functools

import jax
import jax.experimental.pallas as pl
import jax.experimental.pallas.tpu as pltpu
import jax.numpy as jnp
from jax import lax
from jax.sharding import PartitionSpec as P

MESH = pl.DeviceIdType.MESH
BF16, F32 = jnp.bfloat16, jnp.float32
keep_scale = 10.0 / 9.0
VMEM_BYTES = 60 * 2**20

Y_HI = 2
NEAR, FAR, SELF, MSG, MID, POOL, OUT = range(7)
TOP = [(1, m) for m in range(7)]
NODE = [(0, OUT), (0, SELF), (0, MSG), (0, POOL)]
EDGE = [(0, NEAR), (0, FAR), (0, MID)]
GROUPS = [TOP, NODE, EDGE]
TILES = [64, 32, 32]
BIAS_TILE = 24
ROUTES = [(1, 0), (-1, 0), (0, 1), (0, -1), (1, 1), (1, -1), (-1, 1), (-1, -1)]
BY_X, BY_Y, BY_CORNER = [0, 1], [2, 3], [4, 5, 6, 7]
SIDE_X, SIDE_Y, CORNERS, INSIDE = [1, 2, 13, 14], [4, 8, 7, 11], [0, 3, 12, 15], [5, 6, 9, 10]
BORDER = SIDE_X + SIDE_Y + CORNERS


def dot(a, b):
    return jnp.dot(a, b, preferred_element_type=F32)


def side_dot(a, b):
    return lax.dot_general(a, b, (((1,), (1,)), ((), ())), preferred_element_type=F32)


def back_dot(a, b):
    return lax.dot_general(a, b, (((0,), (0,)), ((), ())), preferred_element_type=F32)


def silu_parts(v):
    sig = 0.5 * jnp.tanh(0.5 * v) + 0.5
    value = v * sig
    return value, sig + value * (1.0 - sig)


def ones_where(mask):
    return jnp.where(mask, 1.0, 0.0)


def rows_of(ref, cells):
    return jnp.concatenate([ref[c * 16 : (c + 1) * 16, :] for c in cells], axis=0)


def set_rows(ref, cells, value):
    for n, c in enumerate(cells):
        ref[c * 16 : (c + 1) * 16, :] = value[n * 16 : (n + 1) * 16]


def halves_side_by_side(a):
    return jnp.concatenate([a[:128], a[128:]], axis=1)


def halves_stacked(a):
    return jnp.concatenate([a[:, :128], a[:, 128:]], axis=0)


def kernel(
    gx,
    gy,
    norm_scale,
    part_hbm,
    code_hbm,
    valid_hbm,
    drop_hbm,
    w_hbm,
    b_hbm,
    cot_hbm,
    pgrad_hbm,
    wgrad_hbm,
    bgrad_hbm,
    pgrad_ref,
    wgrad_ref,
    bgrad_ref,
    code_ref,
    valid_ref,
    drop_ref,
    w_ref,
    b_ref,
    cot_ref,
    state_tab,
    far_tab,
    pick,
    place,
    valid_b,
    code_rows,
    near,
    g_one,
    g_two,
    first_t,
    pooled,
    message,
    hidden,
    g_node,
    up_b_ref,
    upstream,
    d_pre_ref,
    d_msg_ref,
    d_pool,
    d_near,
    far_acc,
    far_send,
    far_recv,
    mid_acc,
    mid_pair,
    *rest,
):
    groups = [rest[0:6], rest[6:12], rest[12:17]]
    (
        in_sem,
        out_sem,
        halo_send_sem,
        halo_recv_sem,
        back_send_sem,
        back_recv_sem,
        red_send_sem,
        red_recv_sem,
    ) = rest[17:]
    me_x = lax.axis_index("gx")
    me_y = lax.axis_index("gy")
    depth = gy // Y_HI
    plane = gx * Y_HI // 2
    me_z = lax.rem(me_y, depth)
    core = lax.rem(me_x, 2)
    me_p = (me_x // 4) * 4 + (me_y // depth) * 2 + lax.rem(me_x // 2, 2)

    def plane_device(p):
        return (
            (p // 4) * 4 + lax.rem(p, 2) * 2 + core,
            lax.rem(p // 2, 2) * depth + me_z,
        )

    def z_device(z):
        return (me_x, me_y - me_z + z)

    partner = (me_x + 1 - 2 * core, me_y)

    def neighbour(dx, dy):
        return (lax.rem(me_x + dx + gx, gx), lax.rem(me_y + dy + gy, gy))

    barrier = pltpu.get_barrier_semaphore()

    def greet(device):
        pl.semaphore_signal(barrier, inc=1, device_id=device, device_id_type=MESH)

    for dx, dy in ROUTES:
        greet(neighbour(dx, dy))

    def greet_plane(d, _):
        greet(plane_device(lax.rem(me_p + d, plane)))
        return 0

    def greet_z(d, _):
        greet(z_device(lax.rem(me_z + d, depth)))
        return 0

    lax.fori_loop(1, plane, greet_plane, 0)
    lax.fori_loop(1, depth, greet_z, 0)

    loads = [
        pltpu.make_async_copy(source, target, in_sem.at[n])
        for n, (source, target) in enumerate(
            [
                (part_hbm, state_tab.at[0, pl.ds(1, 4), pl.ds(1, 4)]),
                (code_hbm, code_ref),
                (valid_hbm, valid_ref),
                (w_hbm, w_ref),
                (b_hbm, b_ref),
                (drop_hbm, drop_ref),
                (cot_hbm, cot_ref),
            ]
        )
    ]
    for load in loads:
        load.start()

    def part(step, edge):
        return pl.ds(1, 4) if step == 0 else pl.ds(edge[0] if step > 0 else edge[1], 1)

    def halo_copies(layer):
        copies = []
        for n, (dx, dy) in enumerate(ROUTES):
            tab = state_tab.at[layer]
            copies.append(
                pltpu.make_async_remote_copy(
                    src_ref=tab.at[part(dx, (4, 1)), part(dy, (4, 1))],
                    dst_ref=tab.at[part(dx, (0, 5)), part(dy, (0, 5))],
                    send_sem=halo_send_sem.at[layer, n],
                    recv_sem=halo_recv_sem.at[layer, n],
                    device_id=neighbour(dx, dy),
                    device_id_type=MESH,
                )
            )
        return copies

    def back_copies(layer):
        copies = []
        for n, (dx, dy) in enumerate(ROUTES):
            x = pl.ds(1, 4) if dx == 0 else (5 if dx > 0 else 0)
            y = pl.ds(1, 4) if dy == 0 else (5 if dy > 0 else 0)
            target = far_recv.at[layer, n]
            copies.append(
                pltpu.make_async_remote_copy(
                    src_ref=far_send.at[layer, x, y],
                    dst_ref=target.at[0] if dx and dy else target,
                    send_sem=back_send_sem.at[layer, n],
                    recv_sem=back_recv_sem.at[layer, n],
                    device_id=neighbour(dx, dy),
                    device_id_type=MESH,
                )
            )
        return copies

    halos = [halo_copies(layer) for layer in range(2)]
    backs = [back_copies(layer) for layer in range(2)]

    loads[0].wait()
    pl.semaphore_wait(barrier, plane - 1 + depth - 1 + len(ROUTES))
    for copy in reversed(halos[0]):
        copy.start()

    spread = ones_where(
        lax.broadcasted_iota(jnp.int32, (16, 256), 1) // 16
        == lax.broadcasted_iota(jnp.int32, (16, 256), 0)
    ).astype(BF16)
    own = ones_where(
        lax.rem(lax.broadcasted_iota(jnp.int32, (256, 256), 0), 16)
        == lax.rem(lax.broadcasted_iota(jnp.int32, (256, 256), 1), 16)
    )
    gather_cell = ones_where(
        lax.broadcasted_iota(jnp.int32, (16, 256), 1) // 16
        == lax.broadcasted_iota(jnp.int32, (16, 256), 0)
    ).astype(BF16)
    loads[1].wait()
    loads[2].wait()
    codes = code_ref[...].reshape(256, 16).astype(F32).astype(BF16)
    code_rows[...] = dot(gather_cell, (dot(codes, spread) * own).astype(BF16))

    slot_rows = lax.broadcasted_iota(jnp.int32, (144, 256), 0).astype(F32)
    slot_lanes = lax.broadcasted_iota(jnp.int32, (16, 256), 1).astype(F32)

    def prepare(c, _):
        row = code_rows[pl.ds(c, 1), :]
        place[c] = ones_where(slot_rows == row).astype(BF16)
        code = code_ref[c].astype(F32)
        flag = valid_ref[c].astype(F32)
        for k in range(16):
            rows = slice(k * 16, (k + 1) * 16)
            column = jnp.broadcast_to(code[:, k : k + 1], (16, 256))
            pick[c, rows, :] = ones_where(column == slot_lanes).astype(BF16)
            valid_b[c, rows, :] = jnp.broadcast_to(flag[:, k : k + 1], (16, 128)).astype(BF16)
        return 0

    lax.fori_loop(0, 16, prepare, 0)
    for load in loads[3:]:
        load.wait()
    empty = jnp.zeros((128, 128), BF16)
    for layer in range(2):
        mid_w = w_ref[layer, MID]
        mid_pair[layer] = jnp.concatenate(
            [
                jnp.concatenate([mid_w, empty], axis=1),
                jnp.concatenate([empty, mid_w], axis=1),
            ],
            axis=0,
        )

    def matrix(layer, m):
        return w_ref[layer, m]

    def bias(layer, m):
        return b_ref[m, layer : layer + 1, :]

    def state_of(layer, cells):
        return jnp.concatenate(
            [state_tab[layer, c // 4 + 1, c % 4 + 1] for c in cells], axis=0
        )

    def inner_state(layer):
        return state_tab[layer, 1:5, 1:5].reshape(256, 128)

    def padded_state(layer):
        return state_tab[layer].reshape(576, 128)

    def kept(layer, which, cells, scale):
        return rows_of(drop_ref.at[2 * layer + which], cells).astype(F32) * scale

    def own_projections(layer):
        state = inner_state(layer)
        near[...] = dot(state, matrix(layer, NEAR)) + bias(layer, 0)
        far = dot(state, matrix(layer, FAR)).astype(BF16)
        far_tab[1:5, 1:5] = far.reshape(4, 4, 16, 128)

    def halo_projections(layer, routes):
        for n in routes:
            halos[layer][n].wait_recv()
        places = []
        for n in routes:
            dx, dy = ROUTES[n]
            places.append((part(dx, (0, 5)), part(dy, (0, 5)), 16 if dx and dy else 64))
        pieces = [state_tab[layer, x, y].reshape(rows, 128) for x, y, rows in places]
        far = dot(jnp.concatenate(pieces, axis=0), matrix(layer, FAR)).astype(BF16)
        done = 0
        for n, (x, y, rows) in zip(routes, places):
            dx, dy = ROUTES[n]
            shape = (1 if dx else 4, 1 if dy else 4, 16, 128)
            far_tab[x, y] = far[done : done + rows].reshape(shape)
            done += rows

    def edges_forward(layer, cells):
        fetched = []
        for c in cells:
            x, y = c // 4, c % 4
            block = far_tab[x : x + 3, y : y + 3].reshape(144, 128)
            block = jnp.concatenate([block, jnp.zeros((112, 128), BF16)], axis=0)
            fetched.append(dot(pick[c], block))
        firsts = []
        for n, c in enumerate(cells):
            base = near[c * 16 : (c + 1) * 16, :]
            pre_one = (fetched[n].reshape(16, 16, 128) + base[None]).reshape(256, 128)
            value, slope = silu_parts(pre_one)
            first = value.astype(BF16)
            g_one[layer, c] = slope.astype(BF16)
            first_t[layer, c] = first.T
            firsts.append(halves_side_by_side(first))
        seconds = [dot(first, mid_pair[layer]) for first in firsts]
        for n, c in enumerate(cells):
            value, slope = silu_parts(halves_stacked(seconds[n]) + bias(layer, 1))
            flags = valid_b[c].astype(F32)
            g_two[layer, c] = (slope * flags).astype(BF16)
            total = jnp.sum((value * flags).reshape(16, 16, 128), axis=0)
            pooled[layer, c * 16 : (c + 1) * 16, :] = total.astype(BF16)

    def nodes_forward(layer, cells):
        state = state_of(layer, cells)
        keep_msg = kept(layer, 0, cells, keep_scale / 16)
        keep_node = kept(layer, 1, cells, keep_scale)
        total = rows_of(pooled.at[layer], cells)
        msg = (dot(total, matrix(layer, POOL)) * keep_msg).astype(BF16)
        set_rows(message.at[layer], cells, msg)
        node_pre = dot(state, matrix(layer, SELF)) + dot(msg, matrix(layer, MSG)) + bias(layer, 2)
        value, slope = silu_parts(node_pre)
        node_hidden = (value * keep_node).astype(BF16)
        set_rows(hidden.at[layer], cells, node_hidden)
        set_rows(g_node.at[layer], cells, slope * keep_node)
        if layer == 0:
            after = (state.astype(F32) + dot(node_hidden, matrix(0, OUT))).astype(BF16)
            for n, c in enumerate(cells):
                state_tab[1, c // 4 + 1, c % 4 + 1] = after[n * 16 : (n + 1) * 16]

    def border_forward(layer):
        for routes, cells in (
            (BY_X, SIDE_X),
            (BY_Y, SIDE_Y),
            (BY_CORNER, CORNERS),
        ):
            halo_projections(layer, routes)
            edges_forward(layer, cells)
        nodes_forward(layer, BORDER)

    own_projections(0)
    border_forward(0)
    for copy in reversed(halos[1]):
        copy.start()
    edges_forward(0, INSIDE)
    nodes_forward(0, INSIDE)
    own_projections(1)
    edges_forward(1, INSIDE)
    nodes_forward(1, INSIDE)
    border_forward(1)

    def node_back(layer, cells):
        up_b = rows_of(upstream, cells).astype(BF16)
        set_rows(up_b_ref.at[layer], cells, up_b)
        d_pre = side_dot(up_b, matrix(layer, OUT)) * rows_of(g_node.at[layer], cells)
        d_pre_b = d_pre.astype(BF16)
        set_rows(d_pre_ref.at[layer], cells, d_pre_b)
        keep_msg = kept(layer, 0, cells, keep_scale / 16)
        d_msg = (side_dot(d_pre_b, matrix(layer, MSG)) * keep_msg).astype(BF16)
        set_rows(d_msg_ref.at[layer], cells, d_msg)
        set_rows(d_pool, cells, side_dot(d_msg, matrix(layer, POOL)).astype(BF16))
        return jnp.sum(d_pre, axis=0, keepdims=True)

    def edges_back(layer, cells, mid_b_sum):
        twos = []
        for c in cells:
            upper = d_pool[c * 16 : (c + 1) * 16, :].astype(F32)
            d_two = g_two[layer, c].astype(F32).reshape(16, 16, 128) * upper[None]
            mid_b_sum = mid_b_sum + jnp.sum(d_two, axis=0)
            twos.append(d_two.reshape(256, 128).astype(BF16))
        outs = [side_dot(halves_side_by_side(two), mid_pair[layer]) for two in twos]
        ones = []
        for n, c in enumerate(cells):
            d_one = halves_stacked(outs[n]) * g_one[layer, c].astype(F32)
            d_near[layer, c * 16 : (c + 1) * 16, :] = jnp.sum(d_one.reshape(16, 16, 128), axis=0)
            ones.append(d_one.astype(BF16))
        both = [
            dot(
                jnp.concatenate([first_t[layer, c], place[c]], axis=0),
                jnp.concatenate([twos[n], ones[n]], axis=1),
            )
            for n, c in enumerate(cells)
        ]
        mid_acc[layer] += sum(b[:128, :128] for b in both)
        for n, c in enumerate(cells):
            x, y = c // 4, c % 4
            far_acc[layer, x : x + 3, y : y + 3] += both[n][128:, 128:].reshape(3, 3, 16, 128)
        return mid_b_sum

    def send_far(layer, routes):
        for n in routes:
            dx, dy = ROUTES[n]
            x = pl.ds(1, 4) if dx == 0 else pl.ds(5 if dx > 0 else 0, 1)
            y = pl.ds(1, 4) if dy == 0 else pl.ds(5 if dy > 0 else 0, 1)
            far_send[layer, x, y] = far_acc[layer, x, y].astype(BF16)
            backs[layer][n].start()

    def add_arrivals(layer, routes):
        for n in routes:
            dx, dy = ROUTES[n]
            backs[layer][n].wait_recv()
            x = pl.ds(1, 4) if dx == 0 else pl.ds(1 if dx > 0 else 4, 1)
            y = pl.ds(1, 4) if dy == 0 else pl.ds(1 if dy > 0 else 4, 1)
            block = far_recv[layer, n].astype(F32)
            if dx and dy:
                far_acc[layer, x, y] += block[0:1][None]
            elif dx:
                far_acc[layer, x, y] += block[None]
            else:
                far_acc[layer, x, y] += block[:, None]

    def far_rows(layer, cells):
        return jnp.concatenate(
            [far_acc[layer, c // 4 + 1, c % 4 + 1] for c in cells], axis=0
        ).astype(BF16)

    def new_upstream(layer, cells):
        return (
            rows_of(upstream, cells)
            + side_dot(rows_of(d_pre_ref.at[layer], cells), matrix(layer, SELF))
            + side_dot(rows_of(d_near.at[layer], cells).astype(BF16), matrix(layer, NEAR))
            + side_dot(far_rows(layer, cells), matrix(layer, FAR))
        )

    def spans(n, index):
        rows = groups[n][0].shape[2]
        found = []
        done = 0
        while done < 128:
            chunk, offset = divmod(index * 128 + done, rows)
            count = min(rows - offset, 128 - done)
            found.append((done, count, chunk // plane, chunk % plane, offset))
            done += count
        return found

    def put(layer, m, value):
        value = value.astype(BF16)
        for n in range(3):
            if (layer, m) in GROUPS[n]:
                stage = groups[n][0]
                for done, count, half, p, offset in spans(n, GROUPS[n].index((layer, m))):
                    stage[half, p, offset : offset + count, :] = value[done : done + count]

    def take(n):
        gathered = groups[n][-1]
        for index, (layer, m) in enumerate(GROUPS[n]):
            for done, count, half, p, offset in spans(n, index):
                piece = gathered[half, p, offset : offset + count, :]
                wgrad_ref[layer, m, done : done + count, :] = piece.astype(F32) * norm_scale

    def clear_rest(n, used):
        stage = groups[n][0]
        rows = stage.shape[2]
        while used < TILES[n] * 16:
            chunk, offset = divmod(used, rows)
            stage[chunk // plane, chunk % plane, offset:rows, :] = jnp.zeros(
                (rows - offset, 128), BF16
            )
            used += rows - offset

    def edge_grads(layer):
        put(layer, MID, mid_acc[layer])
        near_b = d_near[layer].astype(BF16)
        put(layer, NEAR, back_dot(inner_state(layer), near_b))
        far_b = far_acc[layer].astype(BF16).reshape(576, 128)
        put(layer, FAR, back_dot(padded_state(layer), far_b))
        return jnp.sum(d_near[layer], axis=0, keepdims=True)

    def node_grads(layer):
        put(layer, OUT, back_dot(hidden[layer], up_b_ref[layer]))
        put(layer, SELF, back_dot(inner_state(layer), d_pre_ref[layer]))
        put(layer, MSG, back_dot(message[layer], d_pre_ref[layer]))
        put(layer, POOL, back_dot(pooled[layer], d_msg_ref[layer]))

    bias_rows = TILES[2] // plane * 16
    bias_p, bias_offset = divmod(BIAS_TILE * 16, bias_rows)
    bias_here = slice(bias_offset, bias_offset + 16)

    def split_again(tile):
        both = tile[0:8] + tile[8:16]
        high = both.astype(BF16).astype(F32)
        return jnp.concatenate([high, both - high], axis=0).astype(BF16)

    def remote(source, target, sem, device):
        return pltpu.make_async_remote_copy(
            src_ref=source,
            dst_ref=target,
            send_sem=red_send_sem.at[sem],
            recv_sem=red_recv_sem.at[sem],
            device_id=device,
            device_id_type=MESH,
        )

    def wait_all(sems, sem, buffer, count):
        view = buffer.at[pl.ds(0, count)]
        pltpu.make_async_copy(view, view, sems.at[sem]).wait()

    def fold(buffer, count):
        total = buffer[0].astype(F32)
        for n in range(1, count):
            total = total + buffer[n].astype(F32)
        return total

    def core_copy(n):
        return remote(groups[n][0].at[1 - core], groups[n][1], 5 * n, partner)

    def share_copy(n):
        return remote(groups[n][5].at[core], groups[n][5].at[core], 5 * n + 4, partner)

    def over_core(n):
        core_copy(n).start()

    def over_plane(n):
        stage, arrived, added, slots, across, gathered = groups[n]
        core_copy(n).wait_recv()
        total = stage[core].astype(F32) + arrived[...].astype(F32)
        added[...] = total.astype(BF16)

        def body(d, _):
            p = lax.rem(me_p + d, plane)
            remote(added.at[p], slots.at[me_p], 5 * n + 1, plane_device(p)).start()
            return 0

        lax.fori_loop(1, plane, body, 0)
        slots[me_p] = added[me_p]

    def rounded(total):
        plain = total.astype(BF16)
        pieces = [
            plain[:bias_offset],
            jnp.where(me_p == bias_p, split_again(total[bias_here]), plain[bias_here]),
            plain[bias_offset + 16 :],
        ]
        return jnp.concatenate([p for p in pieces if p.shape[0]], axis=0)

    def over_z(n):
        stage, arrived, added, slots, across, gathered = groups[n]
        wait_all(red_recv_sem, 5 * n + 1, slots, plane - 1)
        across[me_z] = fold(slots, plane).astype(BF16)

        def body(d, _):
            z = lax.rem(me_z + d, depth)
            remote(across.at[me_z], across.at[me_z], 5 * n + 2, z_device(z)).start()
            return 0

        lax.fori_loop(1, depth, body, 0)

    def back_over_plane(n):
        stage, arrived, added, slots, across, gathered = groups[n]
        wait_all(red_recv_sem, 5 * n + 2, across, depth - 1)
        gathered[core, me_p] = fold(across, depth).astype(BF16)

        def body(d, _):
            p = lax.rem(me_p + d, plane)
            here = gathered.at[core, me_p]
            remote(here, here, 5 * n + 3, plane_device(p)).start()
            return 0

        lax.fori_loop(1, plane, body, 0)

    def back_over_core(n):
        gathered = groups[n][5]
        wait_all(red_recv_sem, 5 * n + 3, gathered.at[core], plane - 1)
        share_copy(n).start()

    def arrived_whole(n):
        pltpu.make_async_copy(
            groups[n][5].at[1 - core], groups[n][5].at[1 - core], red_recv_sem.at[5 * n + 4]
        ).wait()

    edge_stage, edge_slots, edge_pair, edge_across, edge_gathered = groups[2]

    def edge_core_copy():
        return remote(edge_pair.at[core], edge_pair.at[core], 11, partner)

    def edge_plane():
        edge_slots[me_p] = edge_stage[0, me_p]

        def body(d, _):
            p = lax.rem(me_p + d, plane)
            remote(edge_stage.at[0, p], edge_slots.at[me_p], 10, plane_device(p)).start()
            return 0

        lax.fori_loop(1, plane, body, 0)

    def edge_core():
        wait_all(red_recv_sem, 10, edge_slots, plane - 1)
        edge_pair[core] = rounded(fold(edge_slots, plane))
        edge_core_copy().start()

    def edge_z():
        pltpu.make_async_copy(
            edge_pair.at[1 - core], edge_pair.at[1 - core], red_recv_sem.at[11]
        ).wait()
        edge_across[me_z] = rounded(fold(edge_pair, 2))

        def body(d, _):
            here = edge_across.at[me_z]
            remote(here, here, 12, z_device(lax.rem(me_z + d, depth))).start()
            return 0

        lax.fori_loop(1, depth, body, 0)

    def edge_gather():
        wait_all(red_recv_sem, 12, edge_across, depth - 1)
        edge_gathered[0, me_p] = rounded(fold(edge_across, depth))

        def body(d, _):
            here = edge_gathered.at[0, me_p]
            remote(here, here, 13, plane_device(lax.rem(me_p + d, plane))).start()
            return 0

        lax.fori_loop(1, plane, body, 0)

    runs = [(1, 0, 7), (0, SELF, 2), (0, POOL, 2), (0, NEAR, 2), (0, MID, 1)]
    outs = [
        pltpu.make_async_copy(
            wgrad_ref.at[layer, pl.ds(m, count)],
            wgrad_hbm.at[layer, pl.ds(m, count)],
            out_sem.at[n],
        )
        for n, (layer, m, count) in enumerate(runs)
    ]
    outs.append(pltpu.make_async_copy(pgrad_ref, pgrad_hbm, out_sem.at[5]))
    outs.append(pltpu.make_async_copy(bgrad_ref, bgrad_hbm, out_sem.at[6]))

    no_sum = jnp.zeros((16, 128), F32)

    upstream[...] = cot_ref[...]
    for layer in range(2):
        far_acc[layer] = jnp.zeros((6, 6, 16, 128), F32)
        mid_acc[layer] = jnp.zeros((128, 128), F32)
    node_b1 = node_back(1, BORDER + INSIDE)
    mid_b1 = edges_back(1, CORNERS, no_sum)
    send_far(1, BY_CORNER)
    mid_b1 = edges_back(1, SIDE_Y, mid_b1)
    send_far(1, BY_Y)
    mid_b1 = edges_back(1, SIDE_X, mid_b1)
    send_far(1, BY_X)
    mid_b1 = edges_back(1, INSIDE, mid_b1)
    edge_b1 = edge_grads(1)
    node_grads(1)
    clear_rest(0, len(TOP) * 128)
    over_core(0)

    def start_layer(cells):
        set_rows(upstream, cells, new_upstream(1, cells))
        return node_back(0, cells)

    node_b0 = start_layer(INSIDE)
    mid_b0 = edges_back(0, INSIDE, no_sum)
    over_plane(0)
    add_arrivals(1, BY_X)
    node_b0 = node_b0 + start_layer(SIDE_X)
    mid_b0 = edges_back(0, SIDE_X, mid_b0)
    add_arrivals(1, BY_Y + BY_CORNER)
    node_b0 = node_b0 + start_layer(SIDE_Y + CORNERS)
    node_grads(0)
    over_core(1)
    mid_b0 = edges_back(0, CORNERS, mid_b0)
    mid_b0 = edges_back(0, SIDE_Y, mid_b0)
    edge_b0 = edge_grads(0)
    column = [jnp.sum(v, axis=0, keepdims=True) for v in (mid_b0, mid_b1)]
    sums = jnp.concatenate(
        [edge_b0, edge_b1, column[0], column[1], node_b0, node_b1, jnp.zeros((2, 128), F32)],
        axis=0,
    )
    high = sums.astype(BF16).astype(F32)
    edge_stage[0, bias_p, bias_here, :] = jnp.concatenate([high, sums - high], axis=0).astype(BF16)
    clear_rest(2, (BIAS_TILE + 1) * 16)
    edge_plane()
    send_far(0, BY_CORNER + BY_Y + BY_X)
    over_plane(1)
    over_z(0)
    edge_core()
    back_over_plane(0)
    edge_z()
    add_arrivals(0, BY_X + BY_Y + BY_CORNER)
    pgrad_ref[...] = new_upstream(0, list(range(16)))
    outs[5].start()
    over_z(1)
    edge_gather()
    back_over_core(0)
    back_over_plane(1)
    arrived_whole(0)
    take(0)
    outs[0].start()
    back_over_core(1)
    arrived_whole(1)
    take(1)
    outs[1].start()
    outs[2].start()
    wait_all(red_recv_sem, 13, edge_gathered.at[0], plane - 1)
    take(2)
    outs[3].start()
    outs[4].start()
    pair = edge_gathered[0, bias_p, bias_here, :].astype(F32)
    bias_total = (pair[0:8] + pair[8:16]) * norm_scale
    for m in range(3):
        bgrad_ref[m] = bias_total[2 * m : 2 * m + 2]
    outs[6].start()

    for layer in range(2):
        for copy in halos[layer] + backs[layer]:
            copy.wait_send()
    for n in range(2):
        stage, arrived, added, slots, across, gathered = groups[n]
        core_copy(n).wait_send()
        wait_all(red_send_sem, 5 * n + 1, slots, plane - 1)
        wait_all(red_send_sem, 5 * n + 2, across, depth - 1)
        wait_all(red_send_sem, 5 * n + 3, gathered.at[core], plane - 1)
        share_copy(n).wait_send()
    wait_all(red_send_sem, 10, edge_slots, plane - 1)
    edge_core_copy().wait_send()
    wait_all(red_send_sem, 12, edge_across, depth - 1)
    wait_all(red_send_sem, 13, edge_gathered.at[0], plane - 1)
    for out in outs:
        out.wait()


def write_out(pgrad, wgrad, bgrad, pgrad_out, wgrad_out, bgrad_out, pbuf, wbuf, bbuf, in_sems, out_sems):
    routes = [(pgrad, pbuf, pgrad_out), (bgrad, bbuf, bgrad_out)]
    for layer in range(2):
        for m, count in ((0, 2), (2, 2), (4, 3)):
            part = (layer, pl.ds(m, count))
            routes.append((wgrad.at[part], wbuf.at[part], wgrad_out.at[part]))
    reads = [pltpu.make_async_copy(a, b, in_sems.at[n]) for n, (a, b, _) in enumerate(routes)]
    writes = [pltpu.make_async_copy(b, c, out_sems.at[n]) for n, (_, b, c) in enumerate(routes)]
    for read in reads:
        read.start()
    for read, write in zip(reads, writes):
        read.wait()
        write.start()
    for write in writes:
        write.wait()


def solution(mesh):
    gx, gy = mesh.shape["gx"], mesh.shape["gy"]
    plane, depth = gx * Y_HI // 2, gy // Y_HI
    norm_scale = 1.0 / (gx * gy * 256) ** 0.5
    vmem = pltpu.VMEM

    def group_buffers(tiles):
        rows = tiles // (2 * plane) * 16
        return [
            vmem((2, plane, rows, 128), BF16),
            vmem((plane, rows, 128), BF16),
            vmem((plane, rows, 128), BF16),
            vmem((plane, rows, 128), BF16),
            vmem((depth, rows, 128), BF16),
            vmem((2, plane, rows, 128), BF16),
        ]

    def shards(particles, neighbours, edge_valid, dropout_keep, weights, biases, cotangent):
        scratch = [
            vmem((256, 128), F32),
            vmem((2, 7, 128, 128), F32),
            vmem((3, 2, 128), F32),
            vmem((16, 16, 16), jnp.int32),
            vmem((16, 16, 16), jnp.int32),
            vmem((4, 256, 128), jnp.int32),
            vmem((2, 7, 128, 128), BF16),
            vmem((3, 2, 128), F32),
            vmem((256, 128), F32),
            vmem((2, 6, 6, 16, 128), BF16),
            vmem((6, 6, 16, 128), BF16),
            vmem((16, 256, 256), BF16),
            vmem((16, 144, 256), BF16),
            vmem((16, 256, 128), BF16),
            vmem((16, 256), F32),
            vmem((256, 128), F32),
            vmem((2, 16, 256, 128), BF16),
            vmem((2, 16, 256, 128), BF16),
            vmem((2, 16, 128, 256), BF16),
            vmem((2, 256, 128), BF16),
            vmem((2, 256, 128), BF16),
            vmem((2, 256, 128), BF16),
            vmem((2, 256, 128), F32),
            vmem((2, 256, 128), BF16),
            vmem((256, 128), F32),
            vmem((2, 256, 128), BF16),
            vmem((2, 256, 128), BF16),
            vmem((256, 128), BF16),
            vmem((2, 256, 128), F32),
            vmem((2, 6, 6, 16, 128), F32),
            vmem((2, 6, 6, 16, 128), BF16),
            vmem((2, 8, 4, 16, 128), BF16),
            vmem((2, 128, 128), F32),
            vmem((2, 256, 256), BF16),
        ]
        for tiles in TILES[:2]:
            scratch += group_buffers(tiles)
        rows = TILES[2] // plane * 16
        scratch += [
            vmem((1, plane, rows, 128), BF16),
            vmem((plane, rows, 128), BF16),
            vmem((2, rows, 128), BF16),
            vmem((depth, rows, 128), BF16),
            vmem((1, plane, rows, 128), BF16),
        ]
        scratch += [
            pltpu.SemaphoreType.DMA((7,)),
            pltpu.SemaphoreType.DMA((7,)),
            pltpu.SemaphoreType.DMA((2, 8)),
            pltpu.SemaphoreType.DMA((2, 8)),
            pltpu.SemaphoreType.DMA((2, 8)),
            pltpu.SemaphoreType.DMA((2, 8)),
            pltpu.SemaphoreType.DMA((15,)),
            pltpu.SemaphoreType.DMA((15,)),
        ]
        far_off = pl.BlockSpec(memory_space=pl.ANY)
        shapes = (
            jax.ShapeDtypeStruct((256, 128), F32),
            jax.ShapeDtypeStruct((2, 7, 128, 128), F32),
            jax.ShapeDtypeStruct((3, 2, 128), F32),
        )
        results = pl.pallas_call(
            functools.partial(kernel, gx, gy, norm_scale),
            out_shape=shapes,
            in_specs=[far_off] * 7,
            out_specs=(far_off, far_off, far_off),
            scratch_shapes=scratch,
            compiler_params=pltpu.CompilerParams(
                collective_id=0, has_side_effects=True, vmem_limit_bytes=VMEM_BYTES
            ),
            name="evolver",
        )(
            particles,
            neighbours.reshape(16, 16, 16),
            edge_valid.reshape(16, 16, 16),
            dropout_keep.reshape(4, 256, 128),
            weights,
            biases.transpose(1, 0, 2),
            cotangent.reshape(256, 128),
        )
        pgrad, wgrad, bgrad = pl.pallas_call(
            write_out,
            out_shape=shapes,
            in_specs=[far_off] * 3,
            out_specs=(far_off, far_off, far_off),
            scratch_shapes=[vmem(s.shape, s.dtype) for s in shapes]
            + [pltpu.SemaphoreType.DMA((8,)), pltpu.SemaphoreType.DMA((8,))],
            compiler_params=pltpu.CompilerParams(vmem_limit_bytes=VMEM_BYTES),
            name="write_out",
        )(*results)
        return (pgrad.reshape(particles.shape), wgrad, bgrad.transpose(1, 0, 2))

    cells = P("gx", "gy", None, None)
    return jax.shard_map(
        shards,
        mesh=mesh,
        in_specs=(cells, cells, cells, P(None, None, "gx", "gy", None, None), P(), P(), cells),
        out_specs=(cells, P(), P()),
        check_vma=False,
    )
```

```python
import functools

import jax
import jax.experimental.pallas as pl
import jax.experimental.pallas.tpu as pltpu
import jax.numpy as jnp
from jax import lax
from jax.sharding import PartitionSpec as P

MESH = pl.DeviceIdType.MESH
BF16, F32 = jnp.bfloat16, jnp.float32
keep_scale = 10.0 / 9.0
VMEM_BYTES = 60 * 2**20

Y_HI = 2
NEAR, FAR, SELF, MSG, MID, POOL, OUT = range(7)
TOP = [(1, m) for m in range(7)]
NODE = [(0, OUT), (0, SELF), (0, MSG), (0, POOL)]
EDGE = [(0, NEAR), (0, FAR), (0, MID)]
GROUPS = [TOP, NODE, EDGE]
TILES = [64, 32, 32]
BIAS_TILE = 24
ROUTES = [(1, 0), (-1, 0), (0, 1), (0, -1), (1, 1), (1, -1), (-1, 1), (-1, -1)]
BY_X, BY_Y, BY_CORNER = [0, 1], [2, 3], [4, 5, 6, 7]
SIDE_X, SIDE_Y, CORNERS, INSIDE = [1, 2, 13, 14], [4, 8, 7, 11], [0, 3, 12, 15], [5, 6, 9, 10]
BORDER = SIDE_X + SIDE_Y + CORNERS


def dot(a, b):
    return jnp.dot(a, b, preferred_element_type=F32)


def side_dot(a, b):
    return lax.dot_general(a, b, (((1,), (1,)), ((), ())), preferred_element_type=F32)


def back_dot(a, b):
    return lax.dot_general(a, b, (((0,), (0,)), ((), ())), preferred_element_type=F32)


def silu_parts(v):
    sig = 0.5 * jnp.tanh(0.5 * v) + 0.5
    value = v * sig
    return value, sig + value * (1.0 - sig)


def ones_where(mask):
    return jnp.where(mask, 1.0, 0.0)


def rows_of(ref, cells):
    return jnp.concatenate([ref[c * 16 : (c + 1) * 16, :] for c in cells], axis=0)


def set_rows(ref, cells, value):
    for n, c in enumerate(cells):
        ref[c * 16 : (c + 1) * 16, :] = value[n * 16 : (n + 1) * 16]


def halves_side_by_side(a):
    return jnp.concatenate([a[:128], a[128:]], axis=1)


def halves_stacked(a):
    return jnp.concatenate([a[:, :128], a[:, 128:]], axis=0)


def kernel(
    gx,
    gy,
    norm_scale,
    part_hbm,
    code_hbm,
    valid_hbm,
    drop_hbm,
    w_hbm,
    b_hbm,
    cot_hbm,
    pgrad_hbm,
    wgrad_hbm,
    bgrad_hbm,
    pgrad_ref,
    wgrad_ref,
    bgrad_ref,
    code_ref,
    valid_ref,
    drop_ref,
    w_ref,
    b_ref,
    cot_ref,
    state_tab,
    far_tab,
    pick,
    place,
    valid_b,
    code_rows,
    near,
    g_one,
    g_two,
    first_t,
    pooled,
    message,
    hidden,
    g_node,
    up_b_ref,
    upstream,
    d_pre_ref,
    d_msg_ref,
    d_pool,
    d_near,
    far_acc,
    far_send,
    far_recv,
    mid_acc,
    mid_pair,
    *rest,
):
    groups = [rest[0:6], rest[6:12], rest[12:17]]
    (
        in_sem,
        out_sem,
        halo_send_sem,
        halo_recv_sem,
        back_send_sem,
        back_recv_sem,
        red_send_sem,
        red_recv_sem,
    ) = rest[17:]
    me_x = lax.axis_index("gx")
    me_y = lax.axis_index("gy")
    depth = gy // Y_HI
    plane = gx * Y_HI // 2
    me_z = lax.rem(me_y, depth)
    core = lax.rem(me_x, 2)
    me_p = (me_x // 4) * 4 + (me_y // depth) * 2 + lax.rem(me_x // 2, 2)

    def plane_device(p):
        return (
            (p // 4) * 4 + lax.rem(p, 2) * 2 + core,
            lax.rem(p // 2, 2) * depth + me_z,
        )

    def z_device(z):
        return (me_x, me_y - me_z + z)

    partner = (me_x + 1 - 2 * core, me_y)

    def neighbour(dx, dy):
        return (lax.rem(me_x + dx + gx, gx), lax.rem(me_y + dy + gy, gy))

    barrier = pltpu.get_barrier_semaphore()

    def greet(device):
        pl.semaphore_signal(barrier, inc=1, device_id=device, device_id_type=MESH)

    for dx, dy in ROUTES:
        greet(neighbour(dx, dy))

    def greet_plane(d, _):
        greet(plane_device(lax.rem(me_p + d, plane)))
        return 0

    def greet_z(d, _):
        greet(z_device(lax.rem(me_z + d, depth)))
        return 0

    lax.fori_loop(1, plane, greet_plane, 0)
    lax.fori_loop(1, depth, greet_z, 0)

    loads = [
        pltpu.make_async_copy(source, target, in_sem.at[n])
        for n, (source, target) in enumerate(
            [
                (part_hbm, state_tab.at[0, pl.ds(1, 4), pl.ds(1, 4)]),
                (code_hbm, code_ref),
                (valid_hbm, valid_ref),
                (w_hbm, w_ref),
                (b_hbm, b_ref),
                (drop_hbm, drop_ref),
                (cot_hbm, cot_ref),
            ]
        )
    ]
    for load in loads:
        load.start()

    def part(step, edge):
        return pl.ds(1, 4) if step == 0 else pl.ds(edge[0] if step > 0 else edge[1], 1)

    def halo_copies(layer):
        copies = []
        for n, (dx, dy) in enumerate(ROUTES):
            tab = state_tab.at[layer]
            copies.append(
                pltpu.make_async_remote_copy(
                    src_ref=tab.at[part(dx, (4, 1)), part(dy, (4, 1))],
                    dst_ref=tab.at[part(dx, (0, 5)), part(dy, (0, 5))],
                    send_sem=halo_send_sem.at[layer, n],
                    recv_sem=halo_recv_sem.at[layer, n],
                    device_id=neighbour(dx, dy),
                    device_id_type=MESH,
                )
            )
        return copies

    def back_copies(layer):
        copies = []
        for n, (dx, dy) in enumerate(ROUTES):
            x = pl.ds(1, 4) if dx == 0 else (5 if dx > 0 else 0)
            y = pl.ds(1, 4) if dy == 0 else (5 if dy > 0 else 0)
            target = far_recv.at[layer, n]
            copies.append(
                pltpu.make_async_remote_copy(
                    src_ref=far_send.at[layer, x, y],
                    dst_ref=target.at[0] if dx and dy else target,
                    send_sem=back_send_sem.at[layer, n],
                    recv_sem=back_recv_sem.at[layer, n],
                    device_id=neighbour(dx, dy),
                    device_id_type=MESH,
                )
            )
        return copies

    halos = [halo_copies(layer) for layer in range(2)]
    backs = [back_copies(layer) for layer in range(2)]

    loads[0].wait()
    pl.semaphore_wait(barrier, plane - 1 + depth - 1 + len(ROUTES))
    for copy in reversed(halos[0]):
        copy.start()

    spread = ones_where(
        lax.broadcasted_iota(jnp.int32, (16, 256), 1) // 16
        == lax.broadcasted_iota(jnp.int32, (16, 256), 0)
    ).astype(BF16)
    own = ones_where(
        lax.rem(lax.broadcasted_iota(jnp.int32, (256, 256), 0), 16)
        == lax.rem(lax.broadcasted_iota(jnp.int32, (256, 256), 1), 16)
    )
    gather_cell = ones_where(
        lax.broadcasted_iota(jnp.int32, (16, 256), 1) // 16
        == lax.broadcasted_iota(jnp.int32, (16, 256), 0)
    ).astype(BF16)
    loads[1].wait()
    loads[2].wait()
    codes = code_ref[...].reshape(256, 16).astype(F32).astype(BF16)
    code_rows[...] = dot(gather_cell, (dot(codes, spread) * own).astype(BF16))

    slot_rows = lax.broadcasted_iota(jnp.int32, (144, 256), 0).astype(F32)
    slot_lanes = lax.broadcasted_iota(jnp.int32, (16, 256), 1).astype(F32)

    def prepare(c, _):
        row = code_rows[pl.ds(c, 1), :]
        place[c] = ones_where(slot_rows == row).astype(BF16)
        code = code_ref[c].astype(F32)
        flag = valid_ref[c].astype(F32)
        for k in range(16):
            rows = slice(k * 16, (k + 1) * 16)
            column = jnp.broadcast_to(code[:, k : k + 1], (16, 256))
            pick[c, rows, :] = ones_where(column == slot_lanes).astype(BF16)
            valid_b[c, rows, :] = jnp.broadcast_to(flag[:, k : k + 1], (16, 128)).astype(BF16)
        return 0

    lax.fori_loop(0, 16, prepare, 0)
    for load in loads[3:]:
        load.wait()
    empty = jnp.zeros((128, 128), BF16)
    for layer in range(2):
        mid_w = w_ref[layer, MID]
        mid_pair[layer] = jnp.concatenate(
            [
                jnp.concatenate([mid_w, empty], axis=1),
                jnp.concatenate([empty, mid_w], axis=1),
            ],
            axis=0,
        )

    def matrix(layer, m):
        return w_ref[layer, m]

    def bias(layer, m):
        return b_ref[m, layer : layer + 1, :]

    def state_of(layer, cells):
        return jnp.concatenate(
            [state_tab[layer, c // 4 + 1, c % 4 + 1] for c in cells], axis=0
        )

    def inner_state(layer):
        return state_tab[layer, 1:5, 1:5].reshape(256, 128)

    def padded_state(layer):
        return state_tab[layer].reshape(576, 128)

    def kept(layer, which, cells, scale):
        return rows_of(drop_ref.at[2 * layer + which], cells).astype(F32) * scale

    def own_projections(layer):
        state = inner_state(layer)
        near[...] = dot(state, matrix(layer, NEAR)) + bias(layer, 0)
        far = dot(state, matrix(layer, FAR)).astype(BF16)
        far_tab[1:5, 1:5] = far.reshape(4, 4, 16, 128)

    def halo_projections(layer, routes):
        for n in routes:
            halos[layer][n].wait_recv()
        places = []
        for n in routes:
            dx, dy = ROUTES[n]
            places.append((part(dx, (0, 5)), part(dy, (0, 5)), 16 if dx and dy else 64))
        pieces = [state_tab[layer, x, y].reshape(rows, 128) for x, y, rows in places]
        far = dot(jnp.concatenate(pieces, axis=0), matrix(layer, FAR)).astype(BF16)
        done = 0
        for n, (x, y, rows) in zip(routes, places):
            dx, dy = ROUTES[n]
            shape = (1 if dx else 4, 1 if dy else 4, 16, 128)
            far_tab[x, y] = far[done : done + rows].reshape(shape)
            done += rows

    def edges_forward(layer, cells):
        fetched = []
        for c in cells:
            x, y = c // 4, c % 4
            block = far_tab[x : x + 3, y : y + 3].reshape(144, 128)
            block = jnp.concatenate([block, jnp.zeros((112, 128), BF16)], axis=0)
            fetched.append(dot(pick[c], block))
        firsts = []
        for n, c in enumerate(cells):
            base = near[c * 16 : (c + 1) * 16, :]
            pre_one = (fetched[n].reshape(16, 16, 128) + base[None]).reshape(256, 128)
            value, slope = silu_parts(pre_one)
            first = value.astype(BF16)
            g_one[layer, c] = slope.astype(BF16)
            first_t[layer, c] = first.T
            firsts.append(halves_side_by_side(first))
        seconds = [dot(first, mid_pair[layer]) for first in firsts]
        for n, c in enumerate(cells):
            value, slope = silu_parts(halves_stacked(seconds[n]) + bias(layer, 1))
            flags = valid_b[c].astype(F32)
            g_two[layer, c] = (slope * flags).astype(BF16)
            total = jnp.sum((value * flags).reshape(16, 16, 128), axis=0)
            pooled[layer, c * 16 : (c + 1) * 16, :] = total.astype(BF16)

    def nodes_forward(layer, cells):
        state = state_of(layer, cells)
        keep_msg = kept(layer, 0, cells, keep_scale / 16)
        keep_node = kept(layer, 1, cells, keep_scale)
        total = rows_of(pooled.at[layer], cells)
        msg = (dot(total, matrix(layer, POOL)) * keep_msg).astype(BF16)
        set_rows(message.at[layer], cells, msg)
        node_pre = dot(state, matrix(layer, SELF)) + dot(msg, matrix(layer, MSG)) + bias(layer, 2)
        value, slope = silu_parts(node_pre)
        node_hidden = (value * keep_node).astype(BF16)
        set_rows(hidden.at[layer], cells, node_hidden)
        set_rows(g_node.at[layer], cells, slope * keep_node)
        if layer == 0:
            after = (state.astype(F32) + dot(node_hidden, matrix(0, OUT))).astype(BF16)
            for n, c in enumerate(cells):
                state_tab[1, c // 4 + 1, c % 4 + 1] = after[n * 16 : (n + 1) * 16]

    def border_forward(layer):
        for routes, cells in (
            (BY_X, SIDE_X),
            (BY_Y, SIDE_Y),
            (BY_CORNER, CORNERS),
        ):
            halo_projections(layer, routes)
            edges_forward(layer, cells)
        nodes_forward(layer, BORDER)

    own_projections(0)
    border_forward(0)
    for copy in reversed(halos[1]):
        copy.start()
    edges_forward(0, INSIDE)
    nodes_forward(0, INSIDE)
    own_projections(1)
    edges_forward(1, INSIDE)
    nodes_forward(1, INSIDE)
    border_forward(1)

    def node_back(layer, cells):
        up_b = rows_of(upstream, cells).astype(BF16)
        set_rows(up_b_ref.at[layer], cells, up_b)
        d_pre = side_dot(up_b, matrix(layer, OUT)) * rows_of(g_node.at[layer], cells)
        d_pre_b = d_pre.astype(BF16)
        set_rows(d_pre_ref.at[layer], cells, d_pre_b)
        keep_msg = kept(layer, 0, cells, keep_scale / 16)
        d_msg = (side_dot(d_pre_b, matrix(layer, MSG)) * keep_msg).astype(BF16)
        set_rows(d_msg_ref.at[layer], cells, d_msg)
        set_rows(d_pool, cells, side_dot(d_msg, matrix(layer, POOL)).astype(BF16))
        return jnp.sum(d_pre, axis=0, keepdims=True)

    def edges_back(layer, cells, mid_b_sum):
        twos = []
        for c in cells:
            upper = d_pool[c * 16 : (c + 1) * 16, :].astype(F32)
            d_two = g_two[layer, c].astype(F32).reshape(16, 16, 128) * upper[None]
            mid_b_sum = mid_b_sum + jnp.sum(d_two, axis=0)
            twos.append(d_two.reshape(256, 128).astype(BF16))
        outs = [side_dot(halves_side_by_side(two), mid_pair[layer]) for two in twos]
        ones = []
        for n, c in enumerate(cells):
            d_one = halves_stacked(outs[n]) * g_one[layer, c].astype(F32)
            d_near[layer, c * 16 : (c + 1) * 16, :] = jnp.sum(d_one.reshape(16, 16, 128), axis=0)
            ones.append(d_one.astype(BF16))
        both = [
            dot(
                jnp.concatenate([first_t[layer, c], place[c]], axis=0),
                jnp.concatenate([twos[n], ones[n]], axis=1),
            )
            for n, c in enumerate(cells)
        ]
        mid_acc[layer] += sum(b[:128, :128] for b in both)
        for n, c in enumerate(cells):
            x, y = c // 4, c % 4
            far_acc[layer, x : x + 3, y : y + 3] += both[n][128:, 128:].reshape(3, 3, 16, 128)
        return mid_b_sum

    def send_far(layer, routes):
        for n in routes:
            dx, dy = ROUTES[n]
            x = pl.ds(1, 4) if dx == 0 else pl.ds(5 if dx > 0 else 0, 1)
            y = pl.ds(1, 4) if dy == 0 else pl.ds(5 if dy > 0 else 0, 1)
            far_send[layer, x, y] = far_acc[layer, x, y].astype(BF16)
            backs[layer][n].start()

    def add_arrivals(layer, routes):
        for n in routes:
            dx, dy = ROUTES[n]
            backs[layer][n].wait_recv()
            x = pl.ds(1, 4) if dx == 0 else pl.ds(1 if dx > 0 else 4, 1)
            y = pl.ds(1, 4) if dy == 0 else pl.ds(1 if dy > 0 else 4, 1)
            block = far_recv[layer, n].astype(F32)
            if dx and dy:
                far_acc[layer, x, y] += block[0:1][None]
            elif dx:
                far_acc[layer, x, y] += block[None]
            else:
                far_acc[layer, x, y] += block[:, None]

    def far_rows(layer, cells):
        return jnp.concatenate(
            [far_acc[layer, c // 4 + 1, c % 4 + 1] for c in cells], axis=0
        ).astype(BF16)

    def new_upstream(layer, cells):
        return (
            rows_of(upstream, cells)
            + side_dot(rows_of(d_pre_ref.at[layer], cells), matrix(layer, SELF))
            + side_dot(rows_of(d_near.at[layer], cells).astype(BF16), matrix(layer, NEAR))
            + side_dot(far_rows(layer, cells), matrix(layer, FAR))
        )

    def spans(n, index):
        rows = groups[n][0].shape[2]
        found = []
        done = 0
        while done < 128:
            chunk, offset = divmod(index * 128 + done, rows)
            count = min(rows - offset, 128 - done)
            found.append((done, count, chunk // plane, chunk % plane, offset))
            done += count
        return found

    def put(layer, m, value):
        value = value.astype(BF16)
        for n in range(3):
            if (layer, m) in GROUPS[n]:
                stage = groups[n][0]
                for done, count, half, p, offset in spans(n, GROUPS[n].index((layer, m))):
                    stage[half, p, offset : offset + count, :] = value[done : done + count]

    def take(n):
        gathered = groups[n][-1]
        for index, (layer, m) in enumerate(GROUPS[n]):
            for done, count, half, p, offset in spans(n, index):
                piece = gathered[half, p, offset : offset + count, :]
                wgrad_ref[layer, m, done : done + count, :] = piece.astype(F32) * norm_scale

    def clear_rest(n, used):
        stage = groups[n][0]
        rows = stage.shape[2]
        while used < TILES[n] * 16:
            chunk, offset = divmod(used, rows)
            stage[chunk // plane, chunk % plane, offset:rows, :] = jnp.zeros(
                (rows - offset, 128), BF16
            )
            used += rows - offset

    def edge_grads(layer):
        put(layer, MID, mid_acc[layer])
        near_b = d_near[layer].astype(BF16)
        put(layer, NEAR, back_dot(inner_state(layer), near_b))
        far_b = far_acc[layer].astype(BF16).reshape(576, 128)
        put(layer, FAR, back_dot(padded_state(layer), far_b))
        return jnp.sum(d_near[layer], axis=0, keepdims=True)

    def node_grads(layer):
        put(layer, OUT, back_dot(hidden[layer], up_b_ref[layer]))
        put(layer, SELF, back_dot(inner_state(layer), d_pre_ref[layer]))
        put(layer, MSG, back_dot(message[layer], d_pre_ref[layer]))
        put(layer, POOL, back_dot(pooled[layer], d_msg_ref[layer]))

    bias_rows = TILES[2] // plane * 16
    bias_p, bias_offset = divmod(BIAS_TILE * 16, bias_rows)
    bias_here = slice(bias_offset, bias_offset + 16)

    def split_again(tile):
        both = tile[0:8] + tile[8:16]
        high = both.astype(BF16).astype(F32)
        return jnp.concatenate([high, both - high], axis=0).astype(BF16)

    def remote(source, target, sem, device):
        return pltpu.make_async_remote_copy(
            src_ref=source,
            dst_ref=target,
            send_sem=red_send_sem.at[sem],
            recv_sem=red_recv_sem.at[sem],
            device_id=device,
            device_id_type=MESH,
        )

    def wait_all(sems, sem, buffer, count):
        view = buffer.at[pl.ds(0, count)]
        pltpu.make_async_copy(view, view, sems.at[sem]).wait()

    def fold(buffer, count):
        total = buffer[0].astype(F32)
        for n in range(1, count):
            total = total + buffer[n].astype(F32)
        return total

    def core_copy(n):
        return remote(groups[n][0].at[1 - core], groups[n][1], 5 * n, partner)

    def share_copy(n):
        return remote(groups[n][5].at[core], groups[n][5].at[core], 5 * n + 4, partner)

    def over_core(n):
        core_copy(n).start()

    def over_plane(n):
        stage, arrived, added, slots, across, gathered = groups[n]
        core_copy(n).wait_recv()
        total = stage[core].astype(F32) + arrived[...].astype(F32)
        added[...] = total.astype(BF16)

        def body(d, _):
            p = lax.rem(me_p + d, plane)
            remote(added.at[p], slots.at[me_p], 5 * n + 1, plane_device(p)).start()
            return 0

        lax.fori_loop(1, plane, body, 0)
        slots[me_p] = added[me_p]

    def rounded(total):
        plain = total.astype(BF16)
        pieces = [
            plain[:bias_offset],
            jnp.where(me_p == bias_p, split_again(total[bias_here]), plain[bias_here]),
            plain[bias_offset + 16 :],
        ]
        return jnp.concatenate([p for p in pieces if p.shape[0]], axis=0)

    def over_z(n):
        stage, arrived, added, slots, across, gathered = groups[n]
        wait_all(red_recv_sem, 5 * n + 1, slots, plane - 1)
        across[me_z] = fold(slots, plane).astype(BF16)

        def body(d, _):
            z = lax.rem(me_z + d, depth)
            remote(across.at[me_z], across.at[me_z], 5 * n + 2, z_device(z)).start()
            return 0

        lax.fori_loop(1, depth, body, 0)

    def back_over_plane(n):
        stage, arrived, added, slots, across, gathered = groups[n]
        wait_all(red_recv_sem, 5 * n + 2, across, depth - 1)
        gathered[core, me_p] = fold(across, depth).astype(BF16)

        def body(d, _):
            p = lax.rem(me_p + d, plane)
            here = gathered.at[core, me_p]
            remote(here, here, 5 * n + 3, plane_device(p)).start()
            return 0

        lax.fori_loop(1, plane, body, 0)

    def back_over_core(n):
        gathered = groups[n][5]
        wait_all(red_recv_sem, 5 * n + 3, gathered.at[core], plane - 1)
        share_copy(n).start()

    def arrived_whole(n):
        pltpu.make_async_copy(
            groups[n][5].at[1 - core], groups[n][5].at[1 - core], red_recv_sem.at[5 * n + 4]
        ).wait()

    edge_stage, edge_slots, edge_pair, edge_across, edge_gathered = groups[2]

    def edge_core_copy():
        return remote(edge_pair.at[core], edge_pair.at[core], 11, partner)

    def edge_plane():
        edge_slots[me_p] = edge_stage[0, me_p]

        def body(d, _):
            p = lax.rem(me_p + d, plane)
            remote(edge_stage.at[0, p], edge_slots.at[me_p], 10, plane_device(p)).start()
            return 0

        lax.fori_loop(1, plane, body, 0)

    def edge_core():
        wait_all(red_recv_sem, 10, edge_slots, plane - 1)
        edge_pair[core] = rounded(fold(edge_slots, plane))
        edge_core_copy().start()

    def edge_z():
        pltpu.make_async_copy(
            edge_pair.at[1 - core], edge_pair.at[1 - core], red_recv_sem.at[11]
        ).wait()
        edge_across[me_z] = rounded(fold(edge_pair, 2))

        def body(d, _):
            here = edge_across.at[me_z]
            remote(here, here, 12, z_device(lax.rem(me_z + d, depth))).start()
            return 0

        lax.fori_loop(1, depth, body, 0)

    def edge_gather():
        wait_all(red_recv_sem, 12, edge_across, depth - 1)
        edge_gathered[0, me_p] = rounded(fold(edge_across, depth))

        def body(d, _):
            here = edge_gathered.at[0, me_p]
            remote(here, here, 13, plane_device(lax.rem(me_p + d, plane))).start()
            return 0

        lax.fori_loop(1, plane, body, 0)

    runs = [(1, 0, 7), (0, SELF, 2), (0, POOL, 2), (0, NEAR, 2), (0, MID, 1)]
    outs = [
        pltpu.make_async_copy(
            wgrad_ref.at[layer, pl.ds(m, count)],
            wgrad_hbm.at[layer, pl.ds(m, count)],
            out_sem.at[n],
        )
        for n, (layer, m, count) in enumerate(runs)
    ]
    outs.append(pltpu.make_async_copy(pgrad_ref, pgrad_hbm, out_sem.at[5]))
    outs.append(pltpu.make_async_copy(bgrad_ref, bgrad_hbm, out_sem.at[6]))

    no_sum = jnp.zeros((16, 128), F32)

    upstream[...] = cot_ref[...]
    for layer in range(2):
        far_acc[layer] = jnp.zeros((6, 6, 16, 128), F32)
        mid_acc[layer] = jnp.zeros((128, 128), F32)
    node_b1 = node_back(1, BORDER + INSIDE)
    mid_b1 = edges_back(1, CORNERS, no_sum)
    send_far(1, BY_CORNER)
    mid_b1 = edges_back(1, SIDE_Y, mid_b1)
    send_far(1, BY_Y)
    mid_b1 = edges_back(1, SIDE_X, mid_b1)
    send_far(1, BY_X)
    mid_b1 = edges_back(1, INSIDE, mid_b1)
    edge_b1 = edge_grads(1)
    node_grads(1)
    clear_rest(0, len(TOP) * 128)
    over_core(0)

    def start_layer(cells):
        set_rows(upstream, cells, new_upstream(1, cells))
        return node_back(0, cells)

    node_b0 = start_layer(INSIDE)
    mid_b0 = edges_back(0, INSIDE, no_sum)
    over_plane(0)
    add_arrivals(1, BY_X)
    node_b0 = node_b0 + start_layer(SIDE_X)
    mid_b0 = edges_back(0, SIDE_X, mid_b0)
    add_arrivals(1, BY_Y + BY_CORNER)
    node_b0 = node_b0 + start_layer(SIDE_Y + CORNERS)
    node_grads(0)
    over_core(1)
    mid_b0 = edges_back(0, CORNERS, mid_b0)
    over_plane(1)
    mid_b0 = edges_back(0, SIDE_Y, mid_b0)
    edge_b0 = edge_grads(0)
    column = [jnp.sum(v, axis=0, keepdims=True) for v in (mid_b0, mid_b1)]
    sums = jnp.concatenate(
        [edge_b0, edge_b1, column[0], column[1], node_b0, node_b1, jnp.zeros((2, 128), F32)],
        axis=0,
    )
    high = sums.astype(BF16).astype(F32)
    edge_stage[0, bias_p, bias_here, :] = jnp.concatenate([high, sums - high], axis=0).astype(BF16)
    clear_rest(2, (BIAS_TILE + 1) * 16)
    edge_plane()
    over_z(0)
    send_far(0, BY_CORNER + BY_Y + BY_X)
    over_z(1)
    edge_core()
    back_over_plane(0)
    edge_z()
    add_arrivals(0, BY_X + BY_Y + BY_CORNER)
    pgrad_ref[...] = new_upstream(0, list(range(16)))
    outs[5].start()
    back_over_plane(1)
    edge_gather()
    back_over_core(0)
    arrived_whole(0)
    take(0)
    outs[0].start()
    back_over_core(1)
    arrived_whole(1)
    take(1)
    outs[1].start()
    outs[2].start()
    wait_all(red_recv_sem, 13, edge_gathered.at[0], plane - 1)
    take(2)
    outs[3].start()
    outs[4].start()
    pair = edge_gathered[0, bias_p, bias_here, :].astype(F32)
    bias_total = (pair[0:8] + pair[8:16]) * norm_scale
    for m in range(3):
        bgrad_ref[m] = bias_total[2 * m : 2 * m + 2]
    outs[6].start()

    for layer in range(2):
        for copy in halos[layer] + backs[layer]:
            copy.wait_send()
    for n in range(2):
        stage, arrived, added, slots, across, gathered = groups[n]
        core_copy(n).wait_send()
        wait_all(red_send_sem, 5 * n + 1, slots, plane - 1)
        wait_all(red_send_sem, 5 * n + 2, across, depth - 1)
        wait_all(red_send_sem, 5 * n + 3, gathered.at[core], plane - 1)
        share_copy(n).wait_send()
    wait_all(red_send_sem, 10, edge_slots, plane - 1)
    edge_core_copy().wait_send()
    wait_all(red_send_sem, 12, edge_across, depth - 1)
    wait_all(red_send_sem, 13, edge_gathered.at[0], plane - 1)
    for out in outs:
        out.wait()


def write_out(pgrad, wgrad, bgrad, pgrad_out, wgrad_out, bgrad_out, pbuf, wbuf, bbuf, in_sems, out_sems):
    routes = [(pgrad, pbuf, pgrad_out), (bgrad, bbuf, bgrad_out)]
    for layer in range(2):
        for m, count in ((0, 2), (2, 2), (4, 3)):
            part = (layer, pl.ds(m, count))
            routes.append((wgrad.at[part], wbuf.at[part], wgrad_out.at[part]))
    reads = [pltpu.make_async_copy(a, b, in_sems.at[n]) for n, (a, b, _) in enumerate(routes)]
    writes = [pltpu.make_async_copy(b, c, out_sems.at[n]) for n, (_, b, c) in enumerate(routes)]
    for read in reads:
        read.start()
    for read, write in zip(reads, writes):
        read.wait()
        write.start()
    for write in writes:
        write.wait()


def solution(mesh):
    gx, gy = mesh.shape["gx"], mesh.shape["gy"]
    plane, depth = gx * Y_HI // 2, gy // Y_HI
    norm_scale = 1.0 / (gx * gy * 256) ** 0.5
    vmem = pltpu.VMEM

    def group_buffers(tiles):
        rows = tiles // (2 * plane) * 16
        return [
            vmem((2, plane, rows, 128), BF16),
            vmem((plane, rows, 128), BF16),
            vmem((plane, rows, 128), BF16),
            vmem((plane, rows, 128), BF16),
            vmem((depth, rows, 128), BF16),
            vmem((2, plane, rows, 128), BF16),
        ]

    def shards(particles, neighbours, edge_valid, dropout_keep, weights, biases, cotangent):
        scratch = [
            vmem((256, 128), F32),
            vmem((2, 7, 128, 128), F32),
            vmem((3, 2, 128), F32),
            vmem((16, 16, 16), jnp.int32),
            vmem((16, 16, 16), jnp.int32),
            vmem((4, 256, 128), jnp.int32),
            vmem((2, 7, 128, 128), BF16),
            vmem((3, 2, 128), F32),
            vmem((256, 128), F32),
            vmem((2, 6, 6, 16, 128), BF16),
            vmem((6, 6, 16, 128), BF16),
            vmem((16, 256, 256), BF16),
            vmem((16, 144, 256), BF16),
            vmem((16, 256, 128), BF16),
            vmem((16, 256), F32),
            vmem((256, 128), F32),
            vmem((2, 16, 256, 128), BF16),
            vmem((2, 16, 256, 128), BF16),
            vmem((2, 16, 128, 256), BF16),
            vmem((2, 256, 128), BF16),
            vmem((2, 256, 128), BF16),
            vmem((2, 256, 128), BF16),
            vmem((2, 256, 128), F32),
            vmem((2, 256, 128), BF16),
            vmem((256, 128), F32),
            vmem((2, 256, 128), BF16),
            vmem((2, 256, 128), BF16),
            vmem((256, 128), BF16),
            vmem((2, 256, 128), F32),
            vmem((2, 6, 6, 16, 128), F32),
            vmem((2, 6, 6, 16, 128), BF16),
            vmem((2, 8, 4, 16, 128), BF16),
            vmem((2, 128, 128), F32),
            vmem((2, 256, 256), BF16),
        ]
        for tiles in TILES[:2]:
            scratch += group_buffers(tiles)
        rows = TILES[2] // plane * 16
        scratch += [
            vmem((1, plane, rows, 128), BF16),
            vmem((plane, rows, 128), BF16),
            vmem((2, rows, 128), BF16),
            vmem((depth, rows, 128), BF16),
            vmem((1, plane, rows, 128), BF16),
        ]
        scratch += [
            pltpu.SemaphoreType.DMA((7,)),
            pltpu.SemaphoreType.DMA((7,)),
            pltpu.SemaphoreType.DMA((2, 8)),
            pltpu.SemaphoreType.DMA((2, 8)),
            pltpu.SemaphoreType.DMA((2, 8)),
            pltpu.SemaphoreType.DMA((2, 8)),
            pltpu.SemaphoreType.DMA((15,)),
            pltpu.SemaphoreType.DMA((15,)),
        ]
        far_off = pl.BlockSpec(memory_space=pl.ANY)
        shapes = (
            jax.ShapeDtypeStruct((256, 128), F32),
            jax.ShapeDtypeStruct((2, 7, 128, 128), F32),
            jax.ShapeDtypeStruct((3, 2, 128), F32),
        )
        results = pl.pallas_call(
            functools.partial(kernel, gx, gy, norm_scale),
            out_shape=shapes,
            in_specs=[far_off] * 7,
            out_specs=(far_off, far_off, far_off),
            scratch_shapes=scratch,
            compiler_params=pltpu.CompilerParams(
                collective_id=0, has_side_effects=True, vmem_limit_bytes=VMEM_BYTES
            ),
            name="evolver",
        )(
            particles,
            neighbours.reshape(16, 16, 16),
            edge_valid.reshape(16, 16, 16),
            dropout_keep.reshape(4, 256, 128),
            weights,
            biases.transpose(1, 0, 2),
            cotangent.reshape(256, 128),
        )
        pgrad, wgrad, bgrad = pl.pallas_call(
            write_out,
            out_shape=shapes,
            in_specs=[far_off] * 3,
            out_specs=(far_off, far_off, far_off),
            scratch_shapes=[vmem(s.shape, s.dtype) for s in shapes]
            + [pltpu.SemaphoreType.DMA((8,)), pltpu.SemaphoreType.DMA((8,))],
            compiler_params=pltpu.CompilerParams(vmem_limit_bytes=VMEM_BYTES),
            name="write_out",
        )(*results)
        return (pgrad.reshape(particles.shape), wgrad, bgrad.transpose(1, 0, 2))

    cells = P("gx", "gy", None, None)
    return jax.shard_map(
        shards,
        mesh=mesh,
        in_specs=(cells, cells, cells, P(None, None, "gx", "gy", None, None), P(), P(), cells),
        out_specs=(cells, P(), P()),
        check_vma=False,
    )
```

```python
import functools

import jax
import jax.experimental.pallas as pl
import jax.experimental.pallas.tpu as pltpu
import jax.numpy as jnp
from jax import lax
from jax.sharding import PartitionSpec as P

MESH = pl.DeviceIdType.MESH
BF16, F32 = jnp.bfloat16, jnp.float32
keep_scale = 10.0 / 9.0
VMEM_BYTES = 60 * 2**20

Y_HI = 2
NEAR, FAR, SELF, MSG, MID, POOL, OUT = range(7)
TOP = [(1, m) for m in range(7)]
NODE = [(0, OUT), (0, SELF), (0, MSG), (0, POOL)]
EDGE = [(0, NEAR), (0, FAR), (0, MID)]
GROUPS = [TOP, NODE, EDGE]
TILES = [64, 32, 32]
BIAS_TILE = 24
ROUTES = [(1, 0), (-1, 0), (0, 1), (0, -1), (1, 1), (1, -1), (-1, 1), (-1, -1)]
BY_X, BY_Y, BY_CORNER = [0, 1], [2, 3], [4, 5, 6, 7]
SIDE_X, SIDE_Y, CORNERS, INSIDE = [1, 2, 13, 14], [4, 8, 7, 11], [0, 3, 12, 15], [5, 6, 9, 10]
BORDER = SIDE_X + SIDE_Y + CORNERS


def dot(a, b):
    return jnp.dot(a, b, preferred_element_type=F32)


def side_dot(a, b):
    return lax.dot_general(a, b, (((1,), (1,)), ((), ())), preferred_element_type=F32)


def back_dot(a, b):
    return lax.dot_general(a, b, (((0,), (0,)), ((), ())), preferred_element_type=F32)


def silu_parts(v):
    sig = 0.5 * jnp.tanh(0.5 * v) + 0.5
    value = v * sig
    return value, sig + value * (1.0 - sig)


def ones_where(mask):
    return jnp.where(mask, 1.0, 0.0)


def rows_of(ref, cells):
    return jnp.concatenate([ref[c * 16 : (c + 1) * 16, :] for c in cells], axis=0)


def set_rows(ref, cells, value):
    for n, c in enumerate(cells):
        ref[c * 16 : (c + 1) * 16, :] = value[n * 16 : (n + 1) * 16]


def halves_side_by_side(a):
    return jnp.concatenate([a[:128], a[128:]], axis=1)


def halves_stacked(a):
    return jnp.concatenate([a[:, :128], a[:, 128:]], axis=0)


def kernel(
    gx,
    gy,
    norm_scale,
    part_hbm,
    code_hbm,
    valid_hbm,
    drop_hbm,
    w_hbm,
    b_hbm,
    cot_hbm,
    pgrad_hbm,
    wgrad_hbm,
    bgrad_hbm,
    pgrad_ref,
    wgrad_ref,
    bgrad_ref,
    code_ref,
    valid_ref,
    drop_ref,
    w_ref,
    b_ref,
    cot_ref,
    state_tab,
    far_tab,
    pick,
    place,
    valid_b,
    code_rows,
    near,
    g_one,
    g_two,
    first_t,
    pooled,
    message,
    hidden,
    g_node,
    up_b_ref,
    upstream,
    d_pre_ref,
    d_msg_ref,
    d_pool,
    d_near,
    far_acc,
    far_send,
    far_recv,
    mid_acc,
    mid_pair,
    *rest,
):
    groups = [rest[0:6], rest[6:12], rest[12:17]]
    (
        in_sem,
        out_sem,
        halo_send_sem,
        halo_recv_sem,
        back_send_sem,
        back_recv_sem,
        red_send_sem,
        red_recv_sem,
    ) = rest[17:]
    me_x = lax.axis_index("gx")
    me_y = lax.axis_index("gy")
    depth = gy // Y_HI
    plane = gx * Y_HI // 2
    me_z = lax.rem(me_y, depth)
    core = lax.rem(me_x, 2)
    me_p = (me_x // 4) * 4 + (me_y // depth) * 2 + lax.rem(me_x // 2, 2)

    def plane_device(p):
        return (
            (p // 4) * 4 + lax.rem(p, 2) * 2 + core,
            lax.rem(p // 2, 2) * depth + me_z,
        )

    def z_device(z):
        return (me_x, me_y - me_z + z)

    partner = (me_x + 1 - 2 * core, me_y)

    def neighbour(dx, dy):
        return (lax.rem(me_x + dx + gx, gx), lax.rem(me_y + dy + gy, gy))

    barrier = pltpu.get_barrier_semaphore()

    def greet(device):
        pl.semaphore_signal(barrier, inc=1, device_id=device, device_id_type=MESH)

    for dx, dy in ROUTES:
        greet(neighbour(dx, dy))

    def greet_plane(d, _):
        greet(plane_device(lax.rem(me_p + d, plane)))
        return 0

    def greet_z(d, _):
        greet(z_device(lax.rem(me_z + d, depth)))
        return 0

    lax.fori_loop(1, plane, greet_plane, 0)
    lax.fori_loop(1, depth, greet_z, 0)

    loads = [
        pltpu.make_async_copy(source, target, in_sem.at[n])
        for n, (source, target) in enumerate(
            [
                (part_hbm, state_tab.at[0, pl.ds(1, 4), pl.ds(1, 4)]),
                (code_hbm, code_ref),
                (valid_hbm, valid_ref),
                (w_hbm, w_ref),
                (b_hbm, b_ref),
                (drop_hbm, drop_ref),
                (cot_hbm, cot_ref),
            ]
        )
    ]
    for load in loads:
        load.start()

    def part(step, edge):
        return pl.ds(1, 4) if step == 0 else pl.ds(edge[0] if step > 0 else edge[1], 1)

    def halo_copies(layer):
        copies = []
        for n, (dx, dy) in enumerate(ROUTES):
            tab = state_tab.at[layer]
            copies.append(
                pltpu.make_async_remote_copy(
                    src_ref=tab.at[part(dx, (4, 1)), part(dy, (4, 1))],
                    dst_ref=tab.at[part(dx, (0, 5)), part(dy, (0, 5))],
                    send_sem=halo_send_sem.at[layer, n],
                    recv_sem=halo_recv_sem.at[layer, n],
                    device_id=neighbour(dx, dy),
                    device_id_type=MESH,
                )
            )
        return copies

    def back_copies(layer):
        copies = []
        for n, (dx, dy) in enumerate(ROUTES):
            x = pl.ds(1, 4) if dx == 0 else (5 if dx > 0 else 0)
            y = pl.ds(1, 4) if dy == 0 else (5 if dy > 0 else 0)
            target = far_recv.at[layer, n]
            copies.append(
                pltpu.make_async_remote_copy(
                    src_ref=far_send.at[layer, x, y],
                    dst_ref=target.at[0] if dx and dy else target,
                    send_sem=back_send_sem.at[layer, n],
                    recv_sem=back_recv_sem.at[layer, n],
                    device_id=neighbour(dx, dy),
                    device_id_type=MESH,
                )
            )
        return copies

    halos = [halo_copies(layer) for layer in range(2)]
    backs = [back_copies(layer) for layer in range(2)]

    loads[0].wait()
    pl.semaphore_wait(barrier, plane - 1 + depth - 1 + len(ROUTES))
    for copy in reversed(halos[0]):
        copy.start()

    spread = ones_where(
        lax.broadcasted_iota(jnp.int32, (16, 256), 1) // 16
        == lax.broadcasted_iota(jnp.int32, (16, 256), 0)
    ).astype(BF16)
    own = ones_where(
        lax.rem(lax.broadcasted_iota(jnp.int32, (256, 256), 0), 16)
        == lax.rem(lax.broadcasted_iota(jnp.int32, (256, 256), 1), 16)
    )
    gather_cell = ones_where(
        lax.broadcasted_iota(jnp.int32, (16, 256), 1) // 16
        == lax.broadcasted_iota(jnp.int32, (16, 256), 0)
    ).astype(BF16)
    loads[1].wait()
    loads[2].wait()
    codes = code_ref[...].reshape(256, 16).astype(F32).astype(BF16)
    code_rows[...] = dot(gather_cell, (dot(codes, spread) * own).astype(BF16))

    slot_rows = lax.broadcasted_iota(jnp.int32, (144, 256), 0).astype(F32)
    slot_lanes = lax.broadcasted_iota(jnp.int32, (16, 256), 1).astype(F32)

    def prepare(c, _):
        row = code_rows[pl.ds(c, 1), :]
        place[c] = ones_where(slot_rows == row).astype(BF16)
        code = code_ref[c].astype(F32)
        flag = valid_ref[c].astype(F32)
        for k in range(16):
            rows = slice(k * 16, (k + 1) * 16)
            column = jnp.broadcast_to(code[:, k : k + 1], (16, 256))
            pick[c, rows, :] = ones_where(column == slot_lanes).astype(BF16)
            valid_b[c, rows, :] = jnp.broadcast_to(flag[:, k : k + 1], (16, 128)).astype(BF16)
        return 0

    lax.fori_loop(0, 16, prepare, 0)
    for load in loads[3:]:
        load.wait()
    empty = jnp.zeros((128, 128), BF16)
    for layer in range(2):
        mid_w = w_ref[layer, MID]
        mid_pair[layer] = jnp.concatenate(
            [
                jnp.concatenate([mid_w, empty], axis=1),
                jnp.concatenate([empty, mid_w], axis=1),
            ],
            axis=0,
        )

    def matrix(layer, m):
        return w_ref[layer, m]

    def bias(layer, m):
        return b_ref[m, layer : layer + 1, :]

    def state_of(layer, cells):
        return jnp.concatenate(
            [state_tab[layer, c // 4 + 1, c % 4 + 1] for c in cells], axis=0
        )

    def inner_state(layer):
        return state_tab[layer, 1:5, 1:5].reshape(256, 128)

    def padded_state(layer):
        return state_tab[layer].reshape(576, 128)

    def kept(layer, which, cells, scale):
        return rows_of(drop_ref.at[2 * layer + which], cells).astype(F32) * scale

    def own_projections(layer):
        state = inner_state(layer)
        near[...] = dot(state, matrix(layer, NEAR)) + bias(layer, 0)
        far = dot(state, matrix(layer, FAR)).astype(BF16)
        far_tab[1:5, 1:5] = far.reshape(4, 4, 16, 128)

    def halo_projections(layer, routes):
        for n in routes:
            halos[layer][n].wait_recv()
        places = []
        for n in routes:
            dx, dy = ROUTES[n]
            places.append((part(dx, (0, 5)), part(dy, (0, 5)), 16 if dx and dy else 64))
        pieces = [state_tab[layer, x, y].reshape(rows, 128) for x, y, rows in places]
        far = dot(jnp.concatenate(pieces, axis=0), matrix(layer, FAR)).astype(BF16)
        done = 0
        for n, (x, y, rows) in zip(routes, places):
            dx, dy = ROUTES[n]
            shape = (1 if dx else 4, 1 if dy else 4, 16, 128)
            far_tab[x, y] = far[done : done + rows].reshape(shape)
            done += rows

    def edges_forward(layer, cells):
        fetched = []
        for c in cells:
            x, y = c // 4, c % 4
            block = far_tab[x : x + 3, y : y + 3].reshape(144, 128)
            block = jnp.concatenate([block, jnp.zeros((112, 128), BF16)], axis=0)
            fetched.append(dot(pick[c], block))
        firsts = []
        for n, c in enumerate(cells):
            base = near[c * 16 : (c + 1) * 16, :]
            pre_one = (fetched[n].reshape(16, 16, 128) + base[None]).reshape(256, 128)
            value, slope = silu_parts(pre_one)
            first = value.astype(BF16)
            g_one[layer, c] = slope.astype(BF16)
            first_t[layer, c] = first.T
            firsts.append(halves_side_by_side(first))
        seconds = [dot(first, mid_pair[layer]) for first in firsts]
        for n, c in enumerate(cells):
            value, slope = silu_parts(halves_stacked(seconds[n]) + bias(layer, 1))
            flags = valid_b[c].astype(F32)
            g_two[layer, c] = (slope * flags).astype(BF16)
            total = jnp.sum((value * flags).reshape(16, 16, 128), axis=0)
            pooled[layer, c * 16 : (c + 1) * 16, :] = total.astype(BF16)

    def nodes_forward(layer, cells):
        state = state_of(layer, cells)
        keep_msg = kept(layer, 0, cells, keep_scale / 16)
        keep_node = kept(layer, 1, cells, keep_scale)
        total = rows_of(pooled.at[layer], cells)
        msg = (dot(total, matrix(layer, POOL)) * keep_msg).astype(BF16)
        set_rows(message.at[layer], cells, msg)
        node_pre = dot(state, matrix(layer, SELF)) + dot(msg, matrix(layer, MSG)) + bias(layer, 2)
        value, slope = silu_parts(node_pre)
        node_hidden = (value * keep_node).astype(BF16)
        set_rows(hidden.at[layer], cells, node_hidden)
        set_rows(g_node.at[layer], cells, slope * keep_node)
        if layer == 0:
            after = (state.astype(F32) + dot(node_hidden, matrix(0, OUT))).astype(BF16)
            for n, c in enumerate(cells):
                state_tab[1, c // 4 + 1, c % 4 + 1] = after[n * 16 : (n + 1) * 16]

    def border_forward(layer):
        for routes, cells in (
            (BY_X, SIDE_X),
            (BY_Y, SIDE_Y),
            (BY_CORNER, CORNERS),
        ):
            halo_projections(layer, routes)
            edges_forward(layer, cells)
        nodes_forward(layer, BORDER)

    own_projections(0)
    upstream[...] = cot_ref[...]
    for layer in range(2):
        far_acc[layer] = jnp.zeros((6, 6, 16, 128), F32)
        mid_acc[layer] = jnp.zeros((128, 128), F32)
    border_forward(0)
    for copy in reversed(halos[1]):
        copy.start()
    edges_forward(0, INSIDE)
    nodes_forward(0, INSIDE)
    own_projections(1)
    edges_forward(1, INSIDE)
    nodes_forward(1, INSIDE)
    border_forward(1)

    def node_back(layer, cells):
        up_b = rows_of(upstream, cells).astype(BF16)
        set_rows(up_b_ref.at[layer], cells, up_b)
        d_pre = side_dot(up_b, matrix(layer, OUT)) * rows_of(g_node.at[layer], cells)
        d_pre_b = d_pre.astype(BF16)
        set_rows(d_pre_ref.at[layer], cells, d_pre_b)
        keep_msg = kept(layer, 0, cells, keep_scale / 16)
        d_msg = (side_dot(d_pre_b, matrix(layer, MSG)) * keep_msg).astype(BF16)
        set_rows(d_msg_ref.at[layer], cells, d_msg)
        set_rows(d_pool, cells, side_dot(d_msg, matrix(layer, POOL)).astype(BF16))
        return jnp.sum(d_pre, axis=0, keepdims=True)

    def edges_back(layer, cells, mid_b_sum):
        twos = []
        for c in cells:
            upper = d_pool[c * 16 : (c + 1) * 16, :].astype(F32)
            d_two = g_two[layer, c].astype(F32).reshape(16, 16, 128) * upper[None]
            mid_b_sum = mid_b_sum + jnp.sum(d_two, axis=0)
            twos.append(d_two.reshape(256, 128).astype(BF16))
        outs = [side_dot(halves_side_by_side(two), mid_pair[layer]) for two in twos]
        ones = []
        for n, c in enumerate(cells):
            d_one = halves_stacked(outs[n]) * g_one[layer, c].astype(F32)
            d_near[layer, c * 16 : (c + 1) * 16, :] = jnp.sum(d_one.reshape(16, 16, 128), axis=0)
            ones.append(d_one.astype(BF16))
        both = [
            dot(
                jnp.concatenate([first_t[layer, c], place[c]], axis=0),
                jnp.concatenate([twos[n], ones[n]], axis=1),
            )
            for n, c in enumerate(cells)
        ]
        mid_acc[layer] += sum(b[:128, :128] for b in both)
        for n, c in enumerate(cells):
            x, y = c // 4, c % 4
            far_acc[layer, x : x + 3, y : y + 3] += both[n][128:, 128:].reshape(3, 3, 16, 128)
        return mid_b_sum

    def send_far(layer, routes):
        for n in routes:
            dx, dy = ROUTES[n]
            x = pl.ds(1, 4) if dx == 0 else pl.ds(5 if dx > 0 else 0, 1)
            y = pl.ds(1, 4) if dy == 0 else pl.ds(5 if dy > 0 else 0, 1)
            far_send[layer, x, y] = far_acc[layer, x, y].astype(BF16)
            backs[layer][n].start()

    def add_arrivals(layer, routes):
        for n in routes:
            dx, dy = ROUTES[n]
            backs[layer][n].wait_recv()
            x = pl.ds(1, 4) if dx == 0 else pl.ds(1 if dx > 0 else 4, 1)
            y = pl.ds(1, 4) if dy == 0 else pl.ds(1 if dy > 0 else 4, 1)
            block = far_recv[layer, n].astype(F32)
            if dx and dy:
                far_acc[layer, x, y] += block[0:1][None]
            elif dx:
                far_acc[layer, x, y] += block[None]
            else:
                far_acc[layer, x, y] += block[:, None]

    def far_rows(layer, cells):
        return jnp.concatenate(
            [far_acc[layer, c // 4 + 1, c % 4 + 1] for c in cells], axis=0
        ).astype(BF16)

    def new_upstream(layer, cells):
        return (
            rows_of(upstream, cells)
            + side_dot(rows_of(d_pre_ref.at[layer], cells), matrix(layer, SELF))
            + side_dot(rows_of(d_near.at[layer], cells).astype(BF16), matrix(layer, NEAR))
            + side_dot(far_rows(layer, cells), matrix(layer, FAR))
        )

    def spans(n, index):
        rows = groups[n][0].shape[2]
        found = []
        done = 0
        while done < 128:
            chunk, offset = divmod(index * 128 + done, rows)
            count = min(rows - offset, 128 - done)
            found.append((done, count, chunk // plane, chunk % plane, offset))
            done += count
        return found

    def put(layer, m, value):
        value = value.astype(BF16)
        for n in range(3):
            if (layer, m) in GROUPS[n]:
                stage = groups[n][0]
                for done, count, half, p, offset in spans(n, GROUPS[n].index((layer, m))):
                    stage[half, p, offset : offset + count, :] = value[done : done + count]

    def take(n):
        gathered = groups[n][-1]
        for index, (layer, m) in enumerate(GROUPS[n]):
            for done, count, half, p, offset in spans(n, index):
                piece = gathered[half, p, offset : offset + count, :]
                wgrad_ref[layer, m, done : done + count, :] = piece

    def clear_rest(n, used):
        stage = groups[n][0]
        rows = stage.shape[2]
        while used < TILES[n] * 16:
            chunk, offset = divmod(used, rows)
            stage[chunk // plane, chunk % plane, offset:rows, :] = jnp.zeros(
                (rows - offset, 128), BF16
            )
            used += rows - offset

    def edge_grads(layer):
        put(layer, MID, mid_acc[layer])
        near_b = d_near[layer].astype(BF16)
        put(layer, NEAR, back_dot(inner_state(layer), near_b))
        far_b = far_acc[layer].astype(BF16).reshape(576, 128)
        put(layer, FAR, back_dot(padded_state(layer), far_b))
        return jnp.sum(d_near[layer], axis=0, keepdims=True)

    def node_grads(layer):
        put(layer, OUT, back_dot(hidden[layer], up_b_ref[layer]))
        put(layer, SELF, back_dot(inner_state(layer), d_pre_ref[layer]))
        put(layer, MSG, back_dot(message[layer], d_pre_ref[layer]))
        put(layer, POOL, back_dot(pooled[layer], d_msg_ref[layer]))

    bias_rows = TILES[2] // plane * 16
    bias_p, bias_offset = divmod(BIAS_TILE * 16, bias_rows)
    bias_here = slice(bias_offset, bias_offset + 16)

    def split_again(tile):
        both = tile[0:8] + tile[8:16]
        high = both.astype(BF16).astype(F32)
        return jnp.concatenate([high, both - high], axis=0).astype(BF16)

    def remote(source, target, sem, device):
        return pltpu.make_async_remote_copy(
            src_ref=source,
            dst_ref=target,
            send_sem=red_send_sem.at[sem],
            recv_sem=red_recv_sem.at[sem],
            device_id=device,
            device_id_type=MESH,
        )

    def wait_all(sems, sem, buffer, count):
        view = buffer.at[pl.ds(0, count)]
        pltpu.make_async_copy(view, view, sems.at[sem]).wait()

    def fold(buffer, count):
        total = buffer[0].astype(F32)
        for n in range(1, count):
            total = total + buffer[n].astype(F32)
        return total

    def core_copy(n):
        return remote(groups[n][0].at[1 - core], groups[n][1], 5 * n, partner)

    def share_copy(n):
        return remote(groups[n][5].at[core], groups[n][5].at[core], 5 * n + 4, partner)

    def over_core(n):
        core_copy(n).start()

    def over_plane(n):
        stage, arrived, added, slots, across, gathered = groups[n]
        core_copy(n).wait_recv()
        total = stage[core].astype(F32) + arrived[...].astype(F32)
        added[...] = total.astype(BF16)

        def body(d, _):
            p = lax.rem(me_p + d, plane)
            remote(added.at[p], slots.at[me_p], 5 * n + 1, plane_device(p)).start()
            return 0

        lax.fori_loop(1, plane, body, 0)
        slots[me_p] = added[me_p]

    def rounded(total):
        plain = total.astype(BF16)
        pieces = [
            plain[:bias_offset],
            jnp.where(me_p == bias_p, split_again(total[bias_here]), plain[bias_here]),
            plain[bias_offset + 16 :],
        ]
        return jnp.concatenate([p for p in pieces if p.shape[0]], axis=0)

    def over_z(n):
        stage, arrived, added, slots, across, gathered = groups[n]
        wait_all(red_recv_sem, 5 * n + 1, slots, plane - 1)
        across[me_z] = fold(slots, plane).astype(BF16)

        def body(d, _):
            z = lax.rem(me_z + d, depth)
            remote(across.at[me_z], across.at[me_z], 5 * n + 2, z_device(z)).start()
            return 0

        lax.fori_loop(1, depth, body, 0)

    def back_over_plane(n):
        stage, arrived, added, slots, across, gathered = groups[n]
        wait_all(red_recv_sem, 5 * n + 2, across, depth - 1)
        gathered[core, me_p] = fold(across, depth).astype(BF16)

        def body(d, _):
            p = lax.rem(me_p + d, plane)
            here = gathered.at[core, me_p]
            remote(here, here, 5 * n + 3, plane_device(p)).start()
            return 0

        lax.fori_loop(1, plane, body, 0)

    def back_over_core(n):
        gathered = groups[n][5]
        wait_all(red_recv_sem, 5 * n + 3, gathered.at[core], plane - 1)
        share_copy(n).start()

    def arrived_whole(n):
        pltpu.make_async_copy(
            groups[n][5].at[1 - core], groups[n][5].at[1 - core], red_recv_sem.at[5 * n + 4]
        ).wait()

    edge_stage, edge_slots, edge_pair, edge_across, edge_gathered = groups[2]

    def edge_core_copy():
        return remote(edge_pair.at[core], edge_pair.at[core], 11, partner)

    def edge_plane():
        edge_slots[me_p] = edge_stage[0, me_p]

        def body(d, _):
            p = lax.rem(me_p + d, plane)
            remote(edge_stage.at[0, p], edge_slots.at[me_p], 10, plane_device(p)).start()
            return 0

        lax.fori_loop(1, plane, body, 0)

    def edge_core():
        wait_all(red_recv_sem, 10, edge_slots, plane - 1)
        edge_pair[core] = rounded(fold(edge_slots, plane))
        edge_core_copy().start()

    def edge_z():
        pltpu.make_async_copy(
            edge_pair.at[1 - core], edge_pair.at[1 - core], red_recv_sem.at[11]
        ).wait()
        edge_across[me_z] = rounded(fold(edge_pair, 2))

        def body(d, _):
            here = edge_across.at[me_z]
            remote(here, here, 12, z_device(lax.rem(me_z + d, depth))).start()
            return 0

        lax.fori_loop(1, depth, body, 0)

    def edge_gather():
        wait_all(red_recv_sem, 12, edge_across, depth - 1)
        edge_gathered[0, me_p] = rounded(fold(edge_across, depth))

        def body(d, _):
            here = edge_gathered.at[0, me_p]
            remote(here, here, 13, plane_device(lax.rem(me_p + d, plane))).start()
            return 0

        lax.fori_loop(1, plane, body, 0)

    runs = [(1, 0, 7), (0, SELF, 2), (0, POOL, 2), (0, NEAR, 2), (0, MID, 1)]
    outs = [
        pltpu.make_async_copy(
            wgrad_ref.at[layer, pl.ds(m, count)],
            wgrad_hbm.at[layer, pl.ds(m, count)],
            out_sem.at[n],
        )
        for n, (layer, m, count) in enumerate(runs)
    ]
    outs.append(pltpu.make_async_copy(pgrad_ref, pgrad_hbm, out_sem.at[5]))
    outs.append(pltpu.make_async_copy(bgrad_ref, bgrad_hbm, out_sem.at[6]))

    no_sum = jnp.zeros((16, 128), F32)

    node_b1 = node_back(1, BORDER + INSIDE)
    mid_b1 = edges_back(1, CORNERS, no_sum)
    send_far(1, BY_CORNER)
    mid_b1 = edges_back(1, SIDE_Y, mid_b1)
    send_far(1, BY_Y)
    mid_b1 = edges_back(1, SIDE_X, mid_b1)
    send_far(1, BY_X)
    mid_b1 = edges_back(1, INSIDE, mid_b1)
    edge_b1 = edge_grads(1)
    node_grads(1)
    clear_rest(0, len(TOP) * 128)
    over_core(0)

    def start_layer(cells):
        set_rows(upstream, cells, new_upstream(1, cells))
        return node_back(0, cells)

    node_b0 = start_layer(INSIDE)
    mid_b0 = edges_back(0, INSIDE, no_sum)
    over_plane(0)
    add_arrivals(1, BY_X)
    node_b0 = node_b0 + start_layer(SIDE_X)
    mid_b0 = edges_back(0, SIDE_X, mid_b0)
    add_arrivals(1, BY_Y + BY_CORNER)
    node_b0 = node_b0 + start_layer(SIDE_Y + CORNERS)
    node_grads(0)
    over_core(1)
    mid_b0 = edges_back(0, CORNERS, mid_b0)
    mid_b0 = edges_back(0, SIDE_Y, mid_b0)
    over_plane(1)
    edge_b0 = edge_grads(0)
    column = [jnp.sum(v, axis=0, keepdims=True) for v in (mid_b0, mid_b1)]
    sums = jnp.concatenate(
        [edge_b0, edge_b1, column[0], column[1], node_b0, node_b1, jnp.zeros((2, 128), F32)],
        axis=0,
    )
    high = sums.astype(BF16).astype(F32)
    edge_stage[0, bias_p, bias_here, :] = jnp.concatenate([high, sums - high], axis=0).astype(BF16)
    clear_rest(2, (BIAS_TILE + 1) * 16)
    edge_plane()
    over_z(0)
    send_far(0, BY_CORNER + BY_Y + BY_X)
    over_z(1)
    edge_core()
    back_over_plane(0)
    edge_z()
    add_arrivals(0, BY_X + BY_Y + BY_CORNER)
    pgrad_ref[...] = new_upstream(0, list(range(16)))
    outs[5].start()
    back_over_plane(1)
    edge_gather()
    back_over_core(0)
    arrived_whole(0)
    take(0)
    outs[0].start()
    back_over_core(1)
    arrived_whole(1)
    take(1)
    outs[1].start()
    outs[2].start()
    wait_all(red_recv_sem, 13, edge_gathered.at[0], plane - 1)
    take(2)
    outs[3].start()
    outs[4].start()
    pair = edge_gathered[0, bias_p, bias_here, :].astype(F32)
    bias_total = (pair[0:8] + pair[8:16]) * norm_scale
    for m in range(3):
        bgrad_ref[m] = bias_total[2 * m : 2 * m + 2]
    outs[6].start()

    for layer in range(2):
        for copy in halos[layer] + backs[layer]:
            copy.wait_send()
    for n in range(2):
        stage, arrived, added, slots, across, gathered = groups[n]
        core_copy(n).wait_send()
        wait_all(red_send_sem, 5 * n + 1, slots, plane - 1)
        wait_all(red_send_sem, 5 * n + 2, across, depth - 1)
        wait_all(red_send_sem, 5 * n + 3, gathered.at[core], plane - 1)
        share_copy(n).wait_send()
    wait_all(red_send_sem, 10, edge_slots, plane - 1)
    edge_core_copy().wait_send()
    wait_all(red_send_sem, 12, edge_across, depth - 1)
    wait_all(red_send_sem, 13, edge_gathered.at[0], plane - 1)
    for out in outs:
        out.wait()


def write_out(
    norm_scale,
    pgrad,
    wgrad,
    bgrad,
    pgrad_out,
    wgrad_out,
    bgrad_out,
    pbuf,
    wbuf,
    bbuf,
    narrow,
    in_sems,
    out_sems,
):
    parts = [(layer, pl.ds(m, count)) for layer in range(2) for m, count in ((0, 2), (2, 2), (4, 3))]
    reads = [
        pltpu.make_async_copy(wgrad.at[part], narrow.at[part], in_sems.at[n])
        for n, part in enumerate(parts)
    ]
    reads.append(pltpu.make_async_copy(pgrad, pbuf, in_sems.at[6]))
    reads.append(pltpu.make_async_copy(bgrad, bbuf, in_sems.at[7]))
    writes = [
        pltpu.make_async_copy(wbuf.at[part], wgrad_out.at[part], out_sems.at[n])
        for n, part in enumerate(parts)
    ]
    writes.append(pltpu.make_async_copy(pbuf, pgrad_out, out_sems.at[6]))
    writes.append(pltpu.make_async_copy(bbuf, bgrad_out, out_sems.at[7]))
    for read in reads:
        read.start()
    for n, part in enumerate(parts):
        reads[n].wait()
        wbuf[part] = narrow[part].astype(F32) * norm_scale
        writes[n].start()
    for n in (6, 7):
        reads[n].wait()
        writes[n].start()
    for write in writes:
        write.wait()


def solution(mesh):
    gx, gy = mesh.shape["gx"], mesh.shape["gy"]
    plane, depth = gx * Y_HI // 2, gy // Y_HI
    norm_scale = 1.0 / (gx * gy * 256) ** 0.5
    vmem = pltpu.VMEM

    def group_buffers(tiles):
        rows = tiles // (2 * plane) * 16
        return [
            vmem((2, plane, rows, 128), BF16),
            vmem((plane, rows, 128), BF16),
            vmem((plane, rows, 128), BF16),
            vmem((plane, rows, 128), BF16),
            vmem((depth, rows, 128), BF16),
            vmem((2, plane, rows, 128), BF16),
        ]

    def shards(particles, neighbours, edge_valid, dropout_keep, weights, biases, cotangent):
        scratch = [
            vmem((256, 128), F32),
            vmem((2, 7, 128, 128), BF16),
            vmem((3, 2, 128), F32),
            vmem((16, 16, 16), jnp.int32),
            vmem((16, 16, 16), jnp.int32),
            vmem((4, 256, 128), jnp.int32),
            vmem((2, 7, 128, 128), BF16),
            vmem((3, 2, 128), F32),
            vmem((256, 128), F32),
            vmem((2, 6, 6, 16, 128), BF16),
            vmem((6, 6, 16, 128), BF16),
            vmem((16, 256, 256), BF16),
            vmem((16, 144, 256), BF16),
            vmem((16, 256, 128), BF16),
            vmem((16, 256), F32),
            vmem((256, 128), F32),
            vmem((2, 16, 256, 128), BF16),
            vmem((2, 16, 256, 128), BF16),
            vmem((2, 16, 128, 256), BF16),
            vmem((2, 256, 128), BF16),
            vmem((2, 256, 128), BF16),
            vmem((2, 256, 128), BF16),
            vmem((2, 256, 128), F32),
            vmem((2, 256, 128), BF16),
            vmem((256, 128), F32),
            vmem((2, 256, 128), BF16),
            vmem((2, 256, 128), BF16),
            vmem((256, 128), BF16),
            vmem((2, 256, 128), F32),
            vmem((2, 6, 6, 16, 128), F32),
            vmem((2, 6, 6, 16, 128), BF16),
            vmem((2, 8, 4, 16, 128), BF16),
            vmem((2, 128, 128), F32),
            vmem((2, 256, 256), BF16),
        ]
        for tiles in TILES[:2]:
            scratch += group_buffers(tiles)
        rows = TILES[2] // plane * 16
        scratch += [
            vmem((1, plane, rows, 128), BF16),
            vmem((plane, rows, 128), BF16),
            vmem((2, rows, 128), BF16),
            vmem((depth, rows, 128), BF16),
            vmem((1, plane, rows, 128), BF16),
        ]
        scratch += [
            pltpu.SemaphoreType.DMA((7,)),
            pltpu.SemaphoreType.DMA((7,)),
            pltpu.SemaphoreType.DMA((2, 8)),
            pltpu.SemaphoreType.DMA((2, 8)),
            pltpu.SemaphoreType.DMA((2, 8)),
            pltpu.SemaphoreType.DMA((2, 8)),
            pltpu.SemaphoreType.DMA((15,)),
            pltpu.SemaphoreType.DMA((15,)),
        ]
        far_off = pl.BlockSpec(memory_space=pl.ANY)
        shapes = (
            jax.ShapeDtypeStruct((256, 128), F32),
            jax.ShapeDtypeStruct((2, 7, 128, 128), F32),
            jax.ShapeDtypeStruct((3, 2, 128), F32),
        )
        results = pl.pallas_call(
            functools.partial(kernel, gx, gy, norm_scale),
            out_shape=(shapes[0], jax.ShapeDtypeStruct((2, 7, 128, 128), BF16), shapes[2]),
            in_specs=[far_off] * 7,
            out_specs=(far_off, far_off, far_off),
            scratch_shapes=scratch,
            compiler_params=pltpu.CompilerParams(
                collective_id=0, has_side_effects=True, vmem_limit_bytes=VMEM_BYTES
            ),
            name="evolver",
        )(
            particles,
            neighbours.reshape(16, 16, 16),
            edge_valid.reshape(16, 16, 16),
            dropout_keep.reshape(4, 256, 128),
            weights,
            biases.transpose(1, 0, 2),
            cotangent.reshape(256, 128),
        )
        pgrad, wgrad, bgrad = pl.pallas_call(
            functools.partial(write_out, norm_scale),
            out_shape=shapes,
            in_specs=[far_off] * 3,
            out_specs=(far_off, far_off, far_off),
            scratch_shapes=[vmem(s.shape, s.dtype) for s in shapes]
            + [vmem((2, 7, 128, 128), BF16)]
            + [pltpu.SemaphoreType.DMA((8,)), pltpu.SemaphoreType.DMA((8,))],
            compiler_params=pltpu.CompilerParams(vmem_limit_bytes=VMEM_BYTES),
            name="write_out",
        )(*results)
        return (pgrad.reshape(particles.shape), wgrad, bgrad.transpose(1, 0, 2))

    cells = P("gx", "gy", None, None)
    return jax.shard_map(
        shards,
        mesh=mesh,
        in_specs=(cells, cells, cells, P(None, None, "gx", "gy", None, None), P(), P(), cells),
        out_specs=(cells, P(), P()),
        check_vma=False,
    )
```

```python
import functools

import jax
import jax.experimental.pallas as pl
import jax.experimental.pallas.tpu as pltpu
import jax.numpy as jnp
from jax import lax
from jax.sharding import PartitionSpec as P

MESH = pl.DeviceIdType.MESH
BF16, F32 = jnp.bfloat16, jnp.float32
keep_scale = 10.0 / 9.0
VMEM_BYTES = 60 * 2**20

Y_HI = 2
NEAR, FAR, SELF, MSG, MID, POOL, OUT = range(7)
TOP = [(1, m) for m in range(7)]
NODE = [(0, OUT), (0, SELF), (0, MSG), (0, POOL)]
EDGE = [(0, NEAR), (0, FAR), (0, MID)]
GROUPS = [TOP, NODE, EDGE]
TILES = [64, 32, 32]
BIAS_TILE = 24
ROUTES = [(1, 0), (-1, 0), (0, 1), (0, -1), (1, 1), (1, -1), (-1, 1), (-1, -1)]
BY_X, BY_Y, BY_CORNER = [0, 1], [2, 3], [4, 5, 6, 7]
SIDE_X, SIDE_Y, CORNERS, INSIDE = [1, 2, 13, 14], [4, 8, 7, 11], [0, 3, 12, 15], [5, 6, 9, 10]
BORDER = SIDE_X + SIDE_Y + CORNERS


def dot(a, b):
    return jnp.dot(a, b, preferred_element_type=F32)


def side_dot(a, b):
    return lax.dot_general(a, b, (((1,), (1,)), ((), ())), preferred_element_type=F32)


def back_dot(a, b):
    return lax.dot_general(a, b, (((0,), (0,)), ((), ())), preferred_element_type=F32)


def silu_parts(v):
    sig = 0.5 * jnp.tanh(0.5 * v) + 0.5
    value = v * sig
    return value, sig + value * (1.0 - sig)


def ones_where(mask):
    return jnp.where(mask, 1.0, 0.0)


def rows_of(ref, cells):
    return jnp.concatenate([ref[c * 16 : (c + 1) * 16, :] for c in cells], axis=0)


def set_rows(ref, cells, value):
    for n, c in enumerate(cells):
        ref[c * 16 : (c + 1) * 16, :] = value[n * 16 : (n + 1) * 16]


def halves_side_by_side(a):
    return jnp.concatenate([a[:128], a[128:]], axis=1)


def halves_stacked(a):
    return jnp.concatenate([a[:, :128], a[:, 128:]], axis=0)


def kernel(
    gx,
    gy,
    norm_scale,
    part_hbm,
    code_hbm,
    valid_hbm,
    drop_hbm,
    w_hbm,
    b_hbm,
    cot_hbm,
    pgrad_hbm,
    wgrad_hbm,
    bgrad_hbm,
    pgrad_ref,
    wgrad_ref,
    bgrad_ref,
    code_ref,
    valid_ref,
    drop_ref,
    w_ref,
    b_ref,
    cot_ref,
    state_tab,
    far_tab,
    pick,
    place,
    valid_b,
    code_rows,
    near,
    g_one,
    g_two,
    first_t,
    pooled,
    message,
    hidden,
    g_node,
    up_b_ref,
    upstream,
    d_pre_ref,
    d_msg_ref,
    d_pool,
    d_near,
    far_acc,
    far_send,
    far_recv,
    mid_acc,
    mid_pair,
    *rest,
):
    groups = [rest[0:6], rest[6:12], rest[12:17]]
    (
        in_sem,
        out_sem,
        halo_send_sem,
        halo_recv_sem,
        back_send_sem,
        back_recv_sem,
        red_send_sem,
        red_recv_sem,
    ) = rest[17:]
    me_x = lax.axis_index("gx")
    me_y = lax.axis_index("gy")
    depth = gy // Y_HI
    plane = gx * Y_HI // 2
    me_z = lax.rem(me_y, depth)
    core = lax.rem(me_x, 2)
    me_p = (me_x // 4) * 4 + (me_y // depth) * 2 + lax.rem(me_x // 2, 2)

    def plane_device(p):
        return (
            (p // 4) * 4 + lax.rem(p, 2) * 2 + core,
            lax.rem(p // 2, 2) * depth + me_z,
        )

    def z_device(z):
        return (me_x, me_y - me_z + z)

    partner = (me_x + 1 - 2 * core, me_y)

    def neighbour(dx, dy):
        return (lax.rem(me_x + dx + gx, gx), lax.rem(me_y + dy + gy, gy))

    barrier = pltpu.get_barrier_semaphore()

    def greet(device):
        pl.semaphore_signal(barrier, inc=1, device_id=device, device_id_type=MESH)

    for dx, dy in ROUTES:
        greet(neighbour(dx, dy))

    def greet_plane(d, _):
        greet(plane_device(lax.rem(me_p + d, plane)))
        return 0

    def greet_z(d, _):
        greet(z_device(lax.rem(me_z + d, depth)))
        return 0

    lax.fori_loop(1, plane, greet_plane, 0)
    lax.fori_loop(1, depth, greet_z, 0)

    loads = [
        pltpu.make_async_copy(source, target, in_sem.at[n])
        for n, (source, target) in enumerate(
            [
                (part_hbm, state_tab.at[0, pl.ds(1, 4), pl.ds(1, 4)]),
                (code_hbm, code_ref),
                (valid_hbm, valid_ref),
                (w_hbm, w_ref),
                (b_hbm, b_ref),
                (drop_hbm, drop_ref),
                (cot_hbm, cot_ref),
            ]
        )
    ]
    for load in loads:
        load.start()

    def part(step, edge):
        return pl.ds(1, 4) if step == 0 else pl.ds(edge[0] if step > 0 else edge[1], 1)

    def halo_copies(layer):
        copies = []
        for n, (dx, dy) in enumerate(ROUTES):
            tab = state_tab.at[layer]
            copies.append(
                pltpu.make_async_remote_copy(
                    src_ref=tab.at[part(dx, (4, 1)), part(dy, (4, 1))],
                    dst_ref=tab.at[part(dx, (0, 5)), part(dy, (0, 5))],
                    send_sem=halo_send_sem.at[layer, n],
                    recv_sem=halo_recv_sem.at[layer, n],
                    device_id=neighbour(dx, dy),
                    device_id_type=MESH,
                )
            )
        return copies

    def back_copies(layer):
        copies = []
        for n, (dx, dy) in enumerate(ROUTES):
            x = pl.ds(1, 4) if dx == 0 else (5 if dx > 0 else 0)
            y = pl.ds(1, 4) if dy == 0 else (5 if dy > 0 else 0)
            target = far_recv.at[layer, n]
            copies.append(
                pltpu.make_async_remote_copy(
                    src_ref=far_send.at[layer, x, y],
                    dst_ref=target.at[0] if dx and dy else target,
                    send_sem=back_send_sem.at[layer, n],
                    recv_sem=back_recv_sem.at[layer, n],
                    device_id=neighbour(dx, dy),
                    device_id_type=MESH,
                )
            )
        return copies

    halos = [halo_copies(layer) for layer in range(2)]
    backs = [back_copies(layer) for layer in range(2)]

    loads[0].wait()
    pl.semaphore_wait(barrier, plane - 1 + depth - 1 + len(ROUTES))
    for copy in reversed(halos[0]):
        copy.start()

    spread = ones_where(
        lax.broadcasted_iota(jnp.int32, (16, 256), 1) // 16
        == lax.broadcasted_iota(jnp.int32, (16, 256), 0)
    ).astype(BF16)
    own = ones_where(
        lax.rem(lax.broadcasted_iota(jnp.int32, (256, 256), 0), 16)
        == lax.rem(lax.broadcasted_iota(jnp.int32, (256, 256), 1), 16)
    )
    gather_cell = ones_where(
        lax.broadcasted_iota(jnp.int32, (16, 256), 1) // 16
        == lax.broadcasted_iota(jnp.int32, (16, 256), 0)
    ).astype(BF16)
    loads[1].wait()
    loads[2].wait()
    codes = code_ref[...].reshape(256, 16).astype(F32).astype(BF16)
    code_rows[...] = dot(gather_cell, (dot(codes, spread) * own).astype(BF16))

    slot_rows = lax.broadcasted_iota(jnp.int32, (144, 256), 0).astype(F32)
    slot_lanes = lax.broadcasted_iota(jnp.int32, (16, 256), 1).astype(F32)

    def prepare(c, _):
        row = code_rows[pl.ds(c, 1), :]
        place[c] = ones_where(slot_rows == row).astype(BF16)
        code = code_ref[c].astype(F32)
        flag = valid_ref[c].astype(F32)
        for k in range(16):
            rows = slice(k * 16, (k + 1) * 16)
            column = jnp.broadcast_to(code[:, k : k + 1], (16, 256))
            pick[c, rows, :] = ones_where(column == slot_lanes).astype(BF16)
            valid_b[c, rows, :] = jnp.broadcast_to(flag[:, k : k + 1], (16, 128)).astype(BF16)
        return 0

    lax.fori_loop(0, 16, prepare, 0)
    for load in loads[3:]:
        load.wait()
    empty = jnp.zeros((128, 128), BF16)
    for layer in range(2):
        mid_w = w_ref[layer, MID]
        mid_pair[layer] = jnp.concatenate(
            [
                jnp.concatenate([mid_w, empty], axis=1),
                jnp.concatenate([empty, mid_w], axis=1),
            ],
            axis=0,
        )

    def matrix(layer, m):
        return w_ref[layer, m]

    def bias(layer, m):
        return b_ref[m, layer : layer + 1, :]

    def state_of(layer, cells):
        return jnp.concatenate(
            [state_tab[layer, c // 4 + 1, c % 4 + 1] for c in cells], axis=0
        )

    def inner_state(layer):
        return state_tab[layer, 1:5, 1:5].reshape(256, 128)

    def padded_state(layer):
        return state_tab[layer].reshape(576, 128)

    def kept(layer, which, cells, scale):
        return rows_of(drop_ref.at[2 * layer + which], cells).astype(F32) * scale

    def own_projections(layer):
        state = inner_state(layer)
        near[...] = dot(state, matrix(layer, NEAR)) + bias(layer, 0)
        far = dot(state, matrix(layer, FAR)).astype(BF16)
        far_tab[1:5, 1:5] = far.reshape(4, 4, 16, 128)

    def halo_projections(layer, routes):
        for n in routes:
            halos[layer][n].wait_recv()
        places = []
        for n in routes:
            dx, dy = ROUTES[n]
            places.append((part(dx, (0, 5)), part(dy, (0, 5)), 16 if dx and dy else 64))
        pieces = [state_tab[layer, x, y].reshape(rows, 128) for x, y, rows in places]
        far = dot(jnp.concatenate(pieces, axis=0), matrix(layer, FAR)).astype(BF16)
        done = 0
        for n, (x, y, rows) in zip(routes, places):
            dx, dy = ROUTES[n]
            shape = (1 if dx else 4, 1 if dy else 4, 16, 128)
            far_tab[x, y] = far[done : done + rows].reshape(shape)
            done += rows

    def edges_forward(layer, cells):
        fetched = []
        for c in cells:
            x, y = c // 4, c % 4
            block = far_tab[x : x + 3, y : y + 3].reshape(144, 128)
            block = jnp.concatenate([block, jnp.zeros((112, 128), BF16)], axis=0)
            fetched.append(dot(pick[c], block))
        firsts = []
        for n, c in enumerate(cells):
            base = near[c * 16 : (c + 1) * 16, :]
            pre_one = (fetched[n].reshape(16, 16, 128) + base[None]).reshape(256, 128)
            value, slope = silu_parts(pre_one)
            first = value.astype(BF16)
            g_one[layer, c] = slope.astype(BF16)
            first_t[layer, c] = first.T
            firsts.append(halves_side_by_side(first))
        seconds = [dot(first, mid_pair[layer]) for first in firsts]
        for n, c in enumerate(cells):
            value, slope = silu_parts(halves_stacked(seconds[n]) + bias(layer, 1))
            flags = valid_b[c].astype(F32)
            g_two[layer, c] = (slope * flags).astype(BF16)
            total = jnp.sum((value * flags).reshape(16, 16, 128), axis=0)
            pooled[layer, c * 16 : (c + 1) * 16, :] = total.astype(BF16)

    def nodes_forward(layer, cells):
        state = state_of(layer, cells)
        keep_msg = kept(layer, 0, cells, keep_scale / 16)
        keep_node = kept(layer, 1, cells, keep_scale)
        total = rows_of(pooled.at[layer], cells)
        msg = (dot(total, matrix(layer, POOL)) * keep_msg).astype(BF16)
        set_rows(message.at[layer], cells, msg)
        node_pre = dot(state, matrix(layer, SELF)) + dot(msg, matrix(layer, MSG)) + bias(layer, 2)
        value, slope = silu_parts(node_pre)
        node_hidden = (value * keep_node).astype(BF16)
        set_rows(hidden.at[layer], cells, node_hidden)
        set_rows(g_node.at[layer], cells, slope * keep_node)
        if layer == 0:
            after = (state.astype(F32) + dot(node_hidden, matrix(0, OUT))).astype(BF16)
            for n, c in enumerate(cells):
                state_tab[1, c // 4 + 1, c % 4 + 1] = after[n * 16 : (n + 1) * 16]

    def border_forward(layer):
        for routes, cells in (
            (BY_X, SIDE_X),
            (BY_Y, SIDE_Y),
            (BY_CORNER, CORNERS),
        ):
            halo_projections(layer, routes)
            edges_forward(layer, cells)
        nodes_forward(layer, BORDER)

    own_projections(0)
    upstream[...] = cot_ref[...]
    for layer in range(2):
        far_acc[layer] = jnp.zeros((6, 6, 16, 128), F32)
        mid_acc[layer] = jnp.zeros((128, 128), F32)
    border_forward(0)
    for copy in reversed(halos[1]):
        copy.start()
    edges_forward(0, INSIDE)
    nodes_forward(0, INSIDE)
    own_projections(1)
    edges_forward(1, INSIDE)
    nodes_forward(1, INSIDE)
    border_forward(1)

    def node_back(layer, cells):
        up_b = rows_of(upstream, cells).astype(BF16)
        set_rows(up_b_ref.at[layer], cells, up_b)
        d_pre = side_dot(up_b, matrix(layer, OUT)) * rows_of(g_node.at[layer], cells)
        d_pre_b = d_pre.astype(BF16)
        set_rows(d_pre_ref.at[layer], cells, d_pre_b)
        keep_msg = kept(layer, 0, cells, keep_scale / 16)
        d_msg = (side_dot(d_pre_b, matrix(layer, MSG)) * keep_msg).astype(BF16)
        set_rows(d_msg_ref.at[layer], cells, d_msg)
        set_rows(d_pool, cells, side_dot(d_msg, matrix(layer, POOL)).astype(BF16))
        return jnp.sum(d_pre, axis=0, keepdims=True)

    def edges_back(layer, cells, mid_b_sum):
        twos = []
        for c in cells:
            upper = d_pool[c * 16 : (c + 1) * 16, :].astype(F32)
            d_two = g_two[layer, c].astype(F32).reshape(16, 16, 128) * upper[None]
            mid_b_sum = mid_b_sum + jnp.sum(d_two, axis=0)
            twos.append(d_two.reshape(256, 128).astype(BF16))
        outs = [side_dot(halves_side_by_side(two), mid_pair[layer]) for two in twos]
        ones = []
        for n, c in enumerate(cells):
            d_one = halves_stacked(outs[n]) * g_one[layer, c].astype(F32)
            d_near[layer, c * 16 : (c + 1) * 16, :] = jnp.sum(d_one.reshape(16, 16, 128), axis=0)
            ones.append(d_one.astype(BF16))
        both = [
            dot(
                jnp.concatenate([first_t[layer, c], place[c]], axis=0),
                jnp.concatenate([twos[n], ones[n]], axis=1),
            )
            for n, c in enumerate(cells)
        ]
        mid_acc[layer] += sum(b[:128, :128] for b in both)
        for n, c in enumerate(cells):
            x, y = c // 4, c % 4
            far_acc[layer, x : x + 3, y : y + 3] += both[n][128:, 128:].reshape(3, 3, 16, 128)
        return mid_b_sum

    def send_far(layer, routes):
        for n in routes:
            dx, dy = ROUTES[n]
            x = pl.ds(1, 4) if dx == 0 else pl.ds(5 if dx > 0 else 0, 1)
            y = pl.ds(1, 4) if dy == 0 else pl.ds(5 if dy > 0 else 0, 1)
            far_send[layer, x, y] = far_acc[layer, x, y].astype(BF16)
            backs[layer][n].start()

    def add_arrivals(layer, routes):
        for n in routes:
            dx, dy = ROUTES[n]
            backs[layer][n].wait_recv()
            x = pl.ds(1, 4) if dx == 0 else pl.ds(1 if dx > 0 else 4, 1)
            y = pl.ds(1, 4) if dy == 0 else pl.ds(1 if dy > 0 else 4, 1)
            block = far_recv[layer, n].astype(F32)
            if dx and dy:
                far_acc[layer, x, y] += block[0:1][None]
            elif dx:
                far_acc[layer, x, y] += block[None]
            else:
                far_acc[layer, x, y] += block[:, None]

    def far_rows(layer, cells):
        return jnp.concatenate(
            [far_acc[layer, c // 4 + 1, c % 4 + 1] for c in cells], axis=0
        ).astype(BF16)

    def new_upstream(layer, cells):
        return (
            rows_of(upstream, cells)
            + side_dot(rows_of(d_pre_ref.at[layer], cells), matrix(layer, SELF))
            + side_dot(rows_of(d_near.at[layer], cells).astype(BF16), matrix(layer, NEAR))
            + side_dot(far_rows(layer, cells), matrix(layer, FAR))
        )

    def spans(n, index):
        rows = groups[n][0].shape[2]
        found = []
        done = 0
        while done < 128:
            chunk, offset = divmod(index * 128 + done, rows)
            count = min(rows - offset, 128 - done)
            found.append((done, count, chunk // plane, chunk % plane, offset))
            done += count
        return found

    def put(layer, m, value):
        value = value.astype(BF16)
        for n in range(3):
            if (layer, m) in GROUPS[n]:
                stage = groups[n][0]
                for done, count, half, p, offset in spans(n, GROUPS[n].index((layer, m))):
                    stage[half, p, offset : offset + count, :] = value[done : done + count]

    def take(n):
        gathered = groups[n][-1]
        for index, (layer, m) in enumerate(GROUPS[n]):
            for done, count, half, p, offset in spans(n, index):
                piece = gathered[half, p, offset : offset + count, :]
                wgrad_ref[layer, m, done : done + count, :] = piece

    def clear_rest(n, used):
        stage = groups[n][0]
        rows = stage.shape[2]
        while used < TILES[n] * 16:
            chunk, offset = divmod(used, rows)
            stage[chunk // plane, chunk % plane, offset:rows, :] = jnp.zeros(
                (rows - offset, 128), BF16
            )
            used += rows - offset

    def edge_grads(layer):
        put(layer, MID, mid_acc[layer])
        near_b = d_near[layer].astype(BF16)
        put(layer, NEAR, back_dot(inner_state(layer), near_b))
        far_b = far_acc[layer].astype(BF16).reshape(576, 128)
        put(layer, FAR, back_dot(padded_state(layer), far_b))
        return jnp.sum(d_near[layer], axis=0, keepdims=True)

    def node_grads(layer):
        put(layer, OUT, back_dot(hidden[layer], up_b_ref[layer]))
        put(layer, SELF, back_dot(inner_state(layer), d_pre_ref[layer]))
        put(layer, MSG, back_dot(message[layer], d_pre_ref[layer]))
        put(layer, POOL, back_dot(pooled[layer], d_msg_ref[layer]))

    bias_rows = TILES[2] // plane * 16
    bias_p, bias_offset = divmod(BIAS_TILE * 16, bias_rows)
    bias_here = slice(bias_offset, bias_offset + 16)

    def split_again(tile):
        both = tile[0:8] + tile[8:16]
        high = both.astype(BF16).astype(F32)
        return jnp.concatenate([high, both - high], axis=0).astype(BF16)

    def remote(source, target, sem, device):
        return pltpu.make_async_remote_copy(
            src_ref=source,
            dst_ref=target,
            send_sem=red_send_sem.at[sem],
            recv_sem=red_recv_sem.at[sem],
            device_id=device,
            device_id_type=MESH,
        )

    def wait_all(sems, sem, buffer, count):
        view = buffer.at[pl.ds(0, count)]
        pltpu.make_async_copy(view, view, sems.at[sem]).wait()

    def fold(buffer, count):
        total = buffer[0].astype(F32)
        for n in range(1, count):
            total = total + buffer[n].astype(F32)
        return total

    def core_copy(n):
        return remote(groups[n][0].at[1 - core], groups[n][1], 5 * n, partner)

    def share_copy(n):
        return remote(groups[n][5].at[core], groups[n][5].at[core], 5 * n + 4, partner)

    def over_core(n):
        core_copy(n).start()

    def over_plane(n):
        stage, arrived, added, slots, across, gathered = groups[n]
        core_copy(n).wait_recv()
        total = stage[core].astype(F32) + arrived[...].astype(F32)
        added[...] = total.astype(BF16)

        def body(d, _):
            p = lax.rem(me_p + d, plane)
            remote(added.at[p], slots.at[me_p], 5 * n + 1, plane_device(p)).start()
            return 0

        lax.fori_loop(1, plane, body, 0)
        slots[me_p] = added[me_p]

    def rounded(total):
        plain = total.astype(BF16)
        pieces = [
            plain[:bias_offset],
            jnp.where(me_p == bias_p, split_again(total[bias_here]), plain[bias_here]),
            plain[bias_offset + 16 :],
        ]
        return jnp.concatenate([p for p in pieces if p.shape[0]], axis=0)

    def over_z(n):
        stage, arrived, added, slots, across, gathered = groups[n]
        wait_all(red_recv_sem, 5 * n + 1, slots, plane - 1)
        across[me_z] = fold(slots, plane).astype(BF16)

        def body(d, _):
            z = lax.rem(me_z + d, depth)
            remote(across.at[me_z], across.at[me_z], 5 * n + 2, z_device(z)).start()
            return 0

        lax.fori_loop(1, depth, body, 0)

    def back_over_plane(n):
        stage, arrived, added, slots, across, gathered = groups[n]
        wait_all(red_recv_sem, 5 * n + 2, across, depth - 1)
        gathered[core, me_p] = fold(across, depth).astype(BF16)

        def body(d, _):
            p = lax.rem(me_p + d, plane)
            here = gathered.at[core, me_p]
            remote(here, here, 5 * n + 3, plane_device(p)).start()
            return 0

        lax.fori_loop(1, plane, body, 0)

    def back_over_core(n):
        gathered = groups[n][5]
        wait_all(red_recv_sem, 5 * n + 3, gathered.at[core], plane - 1)
        share_copy(n).start()

    def arrived_whole(n):
        pltpu.make_async_copy(
            groups[n][5].at[1 - core], groups[n][5].at[1 - core], red_recv_sem.at[5 * n + 4]
        ).wait()

    edge_stage, edge_slots, edge_pair, edge_across, edge_gathered = groups[2]

    def edge_core_copy():
        return remote(edge_pair.at[core], edge_pair.at[core], 11, partner)

    def edge_plane():
        edge_slots[me_p] = edge_stage[0, me_p]

        def body(d, _):
            p = lax.rem(me_p + d, plane)
            remote(edge_stage.at[0, p], edge_slots.at[me_p], 10, plane_device(p)).start()
            return 0

        lax.fori_loop(1, plane, body, 0)

    def edge_core():
        wait_all(red_recv_sem, 10, edge_slots, plane - 1)
        edge_pair[core] = rounded(fold(edge_slots, plane))
        edge_core_copy().start()

    def edge_z():
        pltpu.make_async_copy(
            edge_pair.at[1 - core], edge_pair.at[1 - core], red_recv_sem.at[11]
        ).wait()
        edge_across[me_z] = rounded(fold(edge_pair, 2))

        def body(d, _):
            here = edge_across.at[me_z]
            remote(here, here, 12, z_device(lax.rem(me_z + d, depth))).start()
            return 0

        lax.fori_loop(1, depth, body, 0)

    def edge_gather():
        wait_all(red_recv_sem, 12, edge_across, depth - 1)
        edge_gathered[0, me_p] = rounded(fold(edge_across, depth))

        def body(d, _):
            here = edge_gathered.at[0, me_p]
            remote(here, here, 13, plane_device(lax.rem(me_p + d, plane))).start()
            return 0

        lax.fori_loop(1, plane, body, 0)

    runs = [(1, 0, 7), (0, SELF, 2), (0, POOL, 2), (0, NEAR, 2), (0, MID, 1)]
    outs = [
        pltpu.make_async_copy(
            wgrad_ref.at[layer, pl.ds(m, count)],
            wgrad_hbm.at[layer, pl.ds(m, count)],
            out_sem.at[n],
        )
        for n, (layer, m, count) in enumerate(runs)
    ]
    outs.append(pltpu.make_async_copy(pgrad_ref, pgrad_hbm, out_sem.at[5]))
    outs.append(pltpu.make_async_copy(bgrad_ref, bgrad_hbm, out_sem.at[6]))

    no_sum = jnp.zeros((16, 128), F32)

    node_b1 = node_back(1, BORDER + INSIDE)
    mid_b1 = edges_back(1, CORNERS, no_sum)
    send_far(1, BY_CORNER)
    mid_b1 = edges_back(1, SIDE_Y, mid_b1)
    send_far(1, BY_Y)
    mid_b1 = edges_back(1, SIDE_X, mid_b1)
    send_far(1, BY_X)
    mid_b1 = edges_back(1, INSIDE, mid_b1)
    edge_b1 = edge_grads(1)
    node_grads(1)
    clear_rest(0, len(TOP) * 128)
    over_core(0)

    def start_layer(cells):
        set_rows(upstream, cells, new_upstream(1, cells))
        return node_back(0, cells)

    node_b0 = start_layer(INSIDE)
    mid_b0 = edges_back(0, INSIDE, no_sum)
    over_plane(0)
    add_arrivals(1, BY_X)
    node_b0 = node_b0 + start_layer(SIDE_X)
    mid_b0 = edges_back(0, SIDE_X, mid_b0)
    add_arrivals(1, BY_Y + BY_CORNER)
    node_b0 = node_b0 + start_layer(SIDE_Y + CORNERS)
    node_grads(0)
    over_core(1)
    mid_b0 = edges_back(0, CORNERS, mid_b0)
    mid_b0 = edges_back(0, SIDE_Y, mid_b0)
    over_plane(1)
    edge_b0 = edge_grads(0)
    column = [jnp.sum(v, axis=0, keepdims=True) for v in (mid_b0, mid_b1)]
    sums = jnp.concatenate(
        [edge_b0, edge_b1, column[0], column[1], node_b0, node_b1, jnp.zeros((2, 128), F32)],
        axis=0,
    )
    high = sums.astype(BF16).astype(F32)
    edge_stage[0, bias_p, bias_here, :] = jnp.concatenate([high, sums - high], axis=0).astype(BF16)
    clear_rest(2, (BIAS_TILE + 1) * 16)
    edge_plane()
    over_z(0)
    send_far(0, BY_CORNER + BY_Y + BY_X)
    over_z(1)
    edge_core()
    back_over_plane(0)
    edge_z()
    back_over_plane(1)
    add_arrivals(0, BY_X + BY_Y + BY_CORNER)
    pgrad_ref[...] = new_upstream(0, list(range(16)))
    outs[5].start()
    edge_gather()
    back_over_core(0)
    arrived_whole(0)
    take(0)
    outs[0].start()
    back_over_core(1)
    arrived_whole(1)
    take(1)
    outs[1].start()
    outs[2].start()
    wait_all(red_recv_sem, 13, edge_gathered.at[0], plane - 1)
    take(2)
    outs[3].start()
    outs[4].start()
    pair = edge_gathered[0, bias_p, bias_here, :].astype(F32)
    bias_total = (pair[0:8] + pair[8:16]) * norm_scale
    for m in range(3):
        bgrad_ref[m] = bias_total[2 * m : 2 * m + 2]
    outs[6].start()

    for layer in range(2):
        for copy in halos[layer] + backs[layer]:
            copy.wait_send()
    for n in range(2):
        stage, arrived, added, slots, across, gathered = groups[n]
        core_copy(n).wait_send()
        wait_all(red_send_sem, 5 * n + 1, slots, plane - 1)
        wait_all(red_send_sem, 5 * n + 2, across, depth - 1)
        wait_all(red_send_sem, 5 * n + 3, gathered.at[core], plane - 1)
        share_copy(n).wait_send()
    wait_all(red_send_sem, 10, edge_slots, plane - 1)
    edge_core_copy().wait_send()
    wait_all(red_send_sem, 12, edge_across, depth - 1)
    wait_all(red_send_sem, 13, edge_gathered.at[0], plane - 1)
    for out in outs:
        out.wait()


def write_out(
    norm_scale,
    pgrad,
    wgrad,
    bgrad,
    pgrad_out,
    wgrad_out,
    bgrad_out,
    pbuf,
    wbuf,
    bbuf,
    narrow,
    in_sems,
    out_sems,
):
    parts = [(layer, pl.ds(m, count)) for layer in range(2) for m, count in ((0, 2), (2, 2), (4, 3))]
    reads = [
        pltpu.make_async_copy(wgrad.at[part], narrow.at[part], in_sems.at[n])
        for n, part in enumerate(parts)
    ]
    reads.append(pltpu.make_async_copy(pgrad, pbuf, in_sems.at[6]))
    reads.append(pltpu.make_async_copy(bgrad, bbuf, in_sems.at[7]))
    writes = [
        pltpu.make_async_copy(wbuf.at[part], wgrad_out.at[part], out_sems.at[n])
        for n, part in enumerate(parts)
    ]
    writes.append(pltpu.make_async_copy(pbuf, pgrad_out, out_sems.at[6]))
    writes.append(pltpu.make_async_copy(bbuf, bgrad_out, out_sems.at[7]))
    for read in reads:
        read.start()
    for n, part in enumerate(parts):
        reads[n].wait()
        wbuf[part] = narrow[part].astype(F32) * norm_scale
        writes[n].start()
    for n in (6, 7):
        reads[n].wait()
        writes[n].start()
    for write in writes:
        write.wait()


def solution(mesh):
    gx, gy = mesh.shape["gx"], mesh.shape["gy"]
    plane, depth = gx * Y_HI // 2, gy // Y_HI
    norm_scale = 1.0 / (gx * gy * 256) ** 0.5
    vmem = pltpu.VMEM

    def group_buffers(tiles):
        rows = tiles // (2 * plane) * 16
        return [
            vmem((2, plane, rows, 128), BF16),
            vmem((plane, rows, 128), BF16),
            vmem((plane, rows, 128), BF16),
            vmem((plane, rows, 128), BF16),
            vmem((depth, rows, 128), BF16),
            vmem((2, plane, rows, 128), BF16),
        ]

    def shards(particles, neighbours, edge_valid, dropout_keep, weights, biases, cotangent):
        scratch = [
            vmem((256, 128), F32),
            vmem((2, 7, 128, 128), BF16),
            vmem((3, 2, 128), F32),
            vmem((16, 16, 16), jnp.int32),
            vmem((16, 16, 16), jnp.int32),
            vmem((4, 256, 128), jnp.int32),
            vmem((2, 7, 128, 128), BF16),
            vmem((3, 2, 128), F32),
            vmem((256, 128), F32),
            vmem((2, 6, 6, 16, 128), BF16),
            vmem((6, 6, 16, 128), BF16),
            vmem((16, 256, 256), BF16),
            vmem((16, 144, 256), BF16),
            vmem((16, 256, 128), BF16),
            vmem((16, 256), F32),
            vmem((256, 128), F32),
            vmem((2, 16, 256, 128), BF16),
            vmem((2, 16, 256, 128), BF16),
            vmem((2, 16, 128, 256), BF16),
            vmem((2, 256, 128), BF16),
            vmem((2, 256, 128), BF16),
            vmem((2, 256, 128), BF16),
            vmem((2, 256, 128), F32),
            vmem((2, 256, 128), BF16),
            vmem((256, 128), F32),
            vmem((2, 256, 128), BF16),
            vmem((2, 256, 128), BF16),
            vmem((256, 128), BF16),
            vmem((2, 256, 128), F32),
            vmem((2, 6, 6, 16, 128), F32),
            vmem((2, 6, 6, 16, 128), BF16),
            vmem((2, 8, 4, 16, 128), BF16),
            vmem((2, 128, 128), F32),
            vmem((2, 256, 256), BF16),
        ]
        for tiles in TILES[:2]:
            scratch += group_buffers(tiles)
        rows = TILES[2] // plane * 16
        scratch += [
            vmem((1, plane, rows, 128), BF16),
            vmem((plane, rows, 128), BF16),
            vmem((2, rows, 128), BF16),
            vmem((depth, rows, 128), BF16),
            vmem((1, plane, rows, 128), BF16),
        ]
        scratch += [
            pltpu.SemaphoreType.DMA((7,)),
            pltpu.SemaphoreType.DMA((7,)),
            pltpu.SemaphoreType.DMA((2, 8)),
            pltpu.SemaphoreType.DMA((2, 8)),
            pltpu.SemaphoreType.DMA((2, 8)),
            pltpu.SemaphoreType.DMA((2, 8)),
            pltpu.SemaphoreType.DMA((15,)),
            pltpu.SemaphoreType.DMA((15,)),
        ]
        far_off = pl.BlockSpec(memory_space=pl.ANY)
        shapes = (
            jax.ShapeDtypeStruct((256, 128), F32),
            jax.ShapeDtypeStruct((2, 7, 128, 128), F32),
            jax.ShapeDtypeStruct((3, 2, 128), F32),
        )
        results = pl.pallas_call(
            functools.partial(kernel, gx, gy, norm_scale),
            out_shape=(shapes[0], jax.ShapeDtypeStruct((2, 7, 128, 128), BF16), shapes[2]),
            in_specs=[far_off] * 7,
            out_specs=(far_off, far_off, far_off),
            scratch_shapes=scratch,
            compiler_params=pltpu.CompilerParams(
                collective_id=0, has_side_effects=True, vmem_limit_bytes=VMEM_BYTES
            ),
            name="evolver",
        )(
            particles,
            neighbours.reshape(16, 16, 16),
            edge_valid.reshape(16, 16, 16),
            dropout_keep.reshape(4, 256, 128),
            weights,
            biases.transpose(1, 0, 2),
            cotangent.reshape(256, 128),
        )
        pgrad, wgrad, bgrad = pl.pallas_call(
            functools.partial(write_out, norm_scale),
            out_shape=shapes,
            in_specs=[far_off] * 3,
            out_specs=(far_off, far_off, far_off),
            scratch_shapes=[vmem(s.shape, s.dtype) for s in shapes]
            + [vmem((2, 7, 128, 128), BF16)]
            + [pltpu.SemaphoreType.DMA((8,)), pltpu.SemaphoreType.DMA((8,))],
            compiler_params=pltpu.CompilerParams(vmem_limit_bytes=VMEM_BYTES),
            name="write_out",
        )(*results)
        return (pgrad.reshape(particles.shape), wgrad, bgrad.transpose(1, 0, 2))

    cells = P("gx", "gy", None, None)
    return jax.shard_map(
        shards,
        mesh=mesh,
        in_specs=(cells, cells, cells, P(None, None, "gx", "gy", None, None), P(), P(), cells),
        out_specs=(cells, P(), P()),
        check_vma=False,
    )
```
